32 devices in a mesh: dp: 8 (over y, x, core), expert: 4 (over z).
Axes of the slice: x: 2, y: 2, z: 4, core: 2. Of those that a mesh axis runs over, the one named last changes fastest.
Arguments:
- layer_in: bfloat16 [4, 8192, 768], P(None, ('dp', 'expert')), may hold values from -6 to 6
- out_grad: bfloat16 [4, 8192, 768], P(None, ('dp', 'expert')), may hold values from -6 to 6
- routes: int32 [4, 8192, 2], P(None, ('dp', 'expert')), may hold values from 0 to 3, all different within a row; in each aligned block of 256 rows (0 to 255, 256 to 511, ..., all dimensions but the last counted through in order) at most 192 rows name the same one
- segments: int32 [4, 8192], P(None, 'dp'), may hold values from 0 to 3, as said below
- buckets: int32 [1024], replicated, may hold values from 0 to 31, as said below
- gain_attn: bfloat16 [768], P('dp'), may hold values from 0.25 to 1.75
- w_query: bfloat16 [768, 768], P('dp'), may hold values from -0.21875 to 0.21875
- w_key: bfloat16 [768, 768], P('dp'), may hold values from -0.21875 to 0.21875
- w_value: bfloat16 [768, 768], P('dp'), may hold values from -0.21875 to 0.21875
- w_output: bfloat16 [768, 768], P('dp'), may hold values from -1.25 to 1.25
- gain_moe: bfloat16 [768], P('dp'), may hold values from 0.25 to 1.75
- router: bfloat16 [768, 4], P('dp'), may hold values from -0.15625 to 0.15625
- rel_bias: bfloat16 [32, 12], P('dp'), may hold values from -4 to 4
- w_expert_in: bfloat16 [4, 768, 3072], P('expert'), may hold values from -0.21875 to 0.21875
- w_expert_out: bfloat16 [4, 3072, 768], P('expert'), may hold values from -0.109375 to 0.109375
Outputs:
- layer_out: bfloat16 [4, 8192, 768], P(None, ('dp', 'expert'))
- grad_in: float32 [4, 8192, 768], P(None, ('dp', 'expert'))
- grad_gain_attn: float32 [768], P('dp')
- grad_query: float32 [768, 768], P('dp')
- grad_key: float32 [768, 768], P('dp')
- grad_value: float32 [768, 768], P('dp')
- grad_output: float32 [768, 768], P('dp')
- grad_gain_moe: float32 [768], P('dp')
- grad_router: float32 [768, 4], P('dp')
- grad_rel_bias: float32 [32, 12], P('dp')
- grad_expert_in: float32 [4, 768, 3072], P('expert')
- grad_expert_out: float32 [4, 3072, 768], P('expert')
The draws below stay inside these ranges and needn't reach their ends.
Inputs may be any that keep to these rules, and one draw needn't show every extreme that they name: `routes`: within the 256 rows of one device in one micro-batch (aligned blocks of rows), no expert is named more than 192 times; a row names two different experts. `segments`: each sequence of 1024 rows holds exactly four documents, numbered 0 to 3 in order; document 2 begins before row 256 of its sequence and includes row 768. Entry r is the bucket of a key r rows before its query; buckets never fall as r grows, and r = 0 has bucket 0.
All inputs are finite; a program needn't handle non-finite values.
Results may differ from the reference program's by a relative error of at most 0.015.
Values may be sent and summed in bfloat16 or wider, within the bound.
A program may use at most 512 MiB of HBM per device.

```python
import math
import jax
import jax.numpy as jnp
import numpy as np
from jax import lax

D = 768
HEADS = 12
HEAD_DIM = 64
FF = 3072
NB = 32
SEQ = 1024
MICRO = 4
EXPERTS = 4
TOK_DEV = 256
TOKENS = 8192
CAP = 192


def draw_segments(key, part):
    key = jax.random.fold_in(key, 3)
    key_first, key_start, key_end = jax.random.split(key, 3)
    count = TOKENS // SEQ
    start = jax.random.randint(key_start, (MICRO, count, 1), 2, TOK_DEV)
    first = 1 + jax.random.randint(key_first, (MICRO, count, 1), 0, TOK_DEV) % (start - 1)
    finish = jax.random.randint(key_end, (MICRO, count, 1), SEQ - TOK_DEV + 1, SEQ)
    places = jnp.arange(SEQ, dtype=jnp.int32)[None, None, :]
    labels = (places >= first).astype(jnp.int32) + (places >= start).astype(jnp.int32) + (places >= finish).astype(jnp.int32)
    return labels.reshape(MICRO, TOKENS).astype(jnp.int32)


def draw_buckets(key, part):
    key = jax.random.fold_in(key, 7)
    widths = jax.random.randint(key, (NB,), 1, 2 + jnp.arange(NB, dtype=jnp.int32))
    bounds = jnp.cumsum(widths)
    offsets = jnp.arange(SEQ, dtype=jnp.int32)
    labels = jnp.sum((offsets[:, None] >= bounds[None, :NB - 1]).astype(jnp.int32), axis=1)
    return labels.astype(jnp.int32)


def block_levels(own_key, dims, shards, smallest, top_value):
    factor_of, own = 1.0, jax.random.fold_in(own_key, 6)
    for position, parts in shards:
        heights = jnp.exp(jax.random.uniform(jax.random.fold_in(own, position), (parts,), jnp.float32, smallest / len(shards), top_value / len(shards)))
        factor_of = factor_of * jnp.repeat(heights, dims[position] // parts).reshape([-1 if axis == position else 1 for axis in range(len(dims))])
    return factor_of


def routed_block(key, own, number, rows, count, top, limit, slope):
    order = jax.random.permutation(key, count)
    heavy_load, ordinary = shares(count, rows * top, limit, slope, True), shares(count, rows * top, limit, slope, False)
    places = jnp.arange(count)

    def named(tallies, turn):
        used = int((tallies > 0).sum())
        fixed = max(1, used // 4)
        passed = fixed + (places - fixed + turn * (used - fixed)) % max(1, count - fixed)
        return jnp.zeros((count,), jnp.int32).at[order[jnp.where(places < fixed, places, passed)]].set(jnp.asarray(tallies, jnp.int32))

    tallies = jnp.where(number % 4 == 0, named(heavy_load, number // 4), named(ordinary, number - number // 4 - 1))
    mixed = jax.random.permutation(jax.random.fold_in(own, 3), count)
    donor, receiver = mixed[0:count // 2 * 2:2], mixed[1:count // 2 * 2:2]
    margin = jnp.minimum(tallies[donor] - 1, limit - tallies[receiver]) // 2
    margin = jnp.where((donor == order[0]) | (receiver == order[0]) | (tallies[receiver] == 0), 0, jnp.maximum(margin, 0))
    passed = jax.random.randint(jax.random.fold_in(own, 4), (count // 2,), 0, 1 << 20) % (margin + 1)
    tallies = tallies.at[donor].add(-passed).at[receiver].add(passed)
    items = jnp.searchsorted(jnp.cumsum(tallies), jnp.arange(rows * top), side="right").astype(jnp.int32)
    listing = items.reshape(top, rows).T
    listing = listing[jax.random.permutation(jax.random.fold_in(own, 1), rows)]
    turn = jax.random.randint(jax.random.fold_in(own, 2), (rows, 1), 0, top)
    return jnp.take_along_axis(listing, (jnp.arange(top)[None, :] + turn) % top, axis=1)


def shares(count, total, most, lean, full):
    portions = [(1 << 20) // math.isqrt(standing ** lean) + 1 for standing in range(1, count + 1)]
    largest = most if full else min(most, max(-(-total // count), total * portions[0] // sum(portions)))
    least = 1 if total - largest >= count - 1 else 0
    holding, rest = [largest] + [least] * (count - 1), total - largest - least * (count - 1)
    while rest > 0:
        free = [i for i in range(1, count) if holding[i] < largest] or [i for i in range(1, count) if holding[i] < most]
        whole, remaining = sum([portions[i] for i in free]), rest
        for i in free:
            addition = min(most - holding[i], max(1, remaining * portions[i] // whole), rest)
            holding[i] = holding[i] + addition
            rest = rest - addition
    return np.array(holding)


def centred(stream_key, shape, scale, bound, cuts=(), held_as=jnp.bfloat16):
    factor_of = block_levels(stream_key, shape, cuts, -0.22, 0.18) if cuts else 1.0
    entries = jax.random.normal(stream_key, shape, jnp.float32) * scale * factor_of
    return jnp.minimum(jnp.maximum(entries, -bound), bound).astype(held_as)


def setup_inputs(seed: int = 0) -> dict:
    splits = jax.random.split(jax.random.key(seed), 16)
    layer_in = centred(splits[0], (MICRO, TOKENS, D), 1.0, 6.0, ((1, 32),))
    out_grad = centred(splits[1], (MICRO, TOKENS, D), 1.0, 6.0, ((1, 32),))
    routes_keys = jax.random.split(jax.random.fold_in(splits[2], 1), MICRO * TOKENS // TOK_DEV)
    routes_turns = jax.random.permutation(jax.random.fold_in(splits[2], 3), MICRO * TOKENS // TOK_DEV)
    routes = jax.vmap(lambda own, number: routed_block(jax.random.fold_in(splits[2], 2), own, number, TOK_DEV, EXPERTS, 2, CAP, 2))(routes_keys, routes_turns).reshape((MICRO, TOKENS, 2))
    segments = draw_segments(jax.random.fold_in(splits[15], 71), 0)
    buckets = draw_buckets(jax.random.fold_in(splits[15], 71), 0)
    gain_attn = jnp.clip(1.0 + 0.15 * jax.random.normal(splits[5], (D,), jnp.float32), 0.25, 1.75).astype(jnp.bfloat16)
    w_query = centred(splits[6], (D, D), D ** -0.5, 0.21875, ((0, 8),))
    w_key = centred(splits[7], (D, D), D ** -0.5, 0.21875, ((0, 8),))
    w_value = centred(splits[8], (D, D), D ** -0.5, 0.21875, ((0, 8),))
    w_output = centred(splits[9], (D, D), (D // 32) ** -0.5, 1.25, ((0, 8),))
    gain_moe = jnp.clip(1.0 + 0.15 * jax.random.normal(splits[10], (D,), jnp.float32), 0.25, 1.75).astype(jnp.bfloat16)
    router = centred(splits[11], (D, EXPERTS), (2 * D) ** -0.5, 0.15625, ((0, 8),))
    rel_bias = centred(splits[12], (NB, HEADS), 1.0, 4.0, ((0, 8),))
    w_expert_in = centred(splits[13], (EXPERTS, D, FF), D ** -0.5, 0.21875, ((0, 4),))
    w_expert_out = centred(splits[14], (EXPERTS, FF, D), FF ** -0.5, 0.109375, ((0, 4),))
    return {"layer_in": layer_in, "out_grad": out_grad, "routes": routes, "segments": segments, "buckets": buckets, "gain_attn": gain_attn, "w_query": w_query, "w_key": w_key, "w_value": w_value, "w_output": w_output, "gain_moe": gain_moe, "router": router, "rel_bias": rel_bias, "w_expert_in": w_expert_in, "w_expert_out": w_expert_out}


EPSILON = 1e-06
MASKED = -1e+30
TOP_PRECISION = lax.Precision.HIGHEST

@jax.custom_vjp
def low(v):
    return lax.optimization_barrier(v.astype(jnp.bfloat16)).astype(jnp.float32)

@jax.custom_vjp
def low_back(v):
    return v

def low_keep(v):
    return (low(v), None)

def low_pass(kept, grad):
    return (grad,)

def back_keep(v):
    return (v, None)

def back_low(kept, grad):
    return (low(grad),)
low.defvjp(low_keep, low_pass)
low_back.defvjp(back_keep, back_low)

def rms_scale(values, gain):
    inverse = lax.rsqrt(lax.optimization_barrier(jnp.mean(values * values, axis=-1, keepdims=True)) + EPSILON)
    return values * inverse * gain

def attend_sequence(queries, keys, values, seg_ids, bias_table, bucket_ids):
    q_heads = queries.reshape(SEQ, HEADS, HEAD_DIM).transpose(1, 0, 2)
    k_heads = keys.reshape(SEQ, HEADS, HEAD_DIM).transpose(1, 0, 2)
    v_heads = values.reshape(SEQ, HEADS, HEAD_DIM).transpose(1, 0, 2)
    raw = low_back(jnp.einsum('hqd,hkd->hqk', q_heads, k_heads, precision=TOP_PRECISION))
    places = jnp.arange(SEQ, dtype=jnp.int32)
    offsets = jnp.maximum(places[:, None] - places[None, :], 0)
    bias = jnp.take(bias_table.T, jnp.take(bucket_ids, offsets), axis=1)
    scores = raw * (1.0 / math.sqrt(HEAD_DIM)) + bias
    allowed = (places[:, None] >= places[None, :]) & (seg_ids[:, None] == seg_ids[None, :])
    scores = jnp.where(allowed[None], scores, MASKED)
    probs = low(jax.nn.softmax(scores, axis=-1))
    mixed = jnp.einsum('hqk,hkd->hqd', probs, v_heads, precision=TOP_PRECISION)
    return low(low_back(mixed.transpose(1, 0, 2).reshape(SEQ, D)))

def expert_block(rows, w_in, w_out):
    pre_act = low_back(jnp.dot(rows, w_in, precision=TOP_PRECISION))
    post_act = low(jax.nn.gelu(pre_act))
    return low(low_back(jnp.dot(post_act, w_out, precision=TOP_PRECISION)))

def route_experts(normed, routes_now, w_in, w_out):
    blocks = TOKENS // TOK_DEV
    flat = routes_now.reshape(blocks, 2 * TOK_DEV)
    onehot = (flat[:, :, None] == jnp.arange(EXPERTS, dtype=jnp.int32)).astype(jnp.int32)
    places = lax.optimization_barrier(jnp.sum((jnp.cumsum(onehot, axis=1) - 1) * onehot, axis=-1))
    slots = (jnp.arange(blocks, dtype=jnp.int32)[:, None] * CAP + places).reshape(TOKENS, 2).astype(jnp.int32)
    copies = jnp.broadcast_to(normed[:, None, :], (TOKENS, 2, D))
    buffer = jnp.zeros((EXPERTS, blocks * CAP, D), jnp.float32).at[routes_now, slots].add(copies)
    buffer = low_back(buffer)
    checked = jax.checkpoint(expert_block)
    results = lax.map(lambda items: checked(items[0], items[1], items[2]), (buffer, w_in, w_out))
    return results[routes_now, slots]

def layer(inputs, seg_now, routes_now, bucket_ids, params):
    gain_a, w_q, w_k, w_v, w_o, gain_m, w_router, table, w_in, w_out = params
    normed = low(rms_scale(inputs, gain_a))
    queries = low(low_back(jnp.dot(normed, w_q, precision=TOP_PRECISION)))
    keys = low(low_back(jnp.dot(normed, w_k, precision=TOP_PRECISION)))
    values = low(low_back(jnp.dot(normed, w_v, precision=TOP_PRECISION)))
    count = TOKENS // SEQ
    checked = jax.checkpoint(attend_sequence)
    attended = lax.map(lambda items: checked(items[0], items[1], items[2], items[3], table, bucket_ids), (queries.reshape(count, SEQ, D), keys.reshape(count, SEQ, D), values.reshape(count, SEQ, D), seg_now.reshape(count, SEQ)))
    attended = attended.reshape(TOKENS, D)
    resid = inputs + low_back(jnp.dot(attended, w_o, precision=TOP_PRECISION))
    normed_moe = low(rms_scale(resid, gain_m))
    probs = jax.nn.softmax(jnp.dot(normed_moe, w_router, precision=TOP_PRECISION), axis=-1)
    picked = jnp.take_along_axis(probs, routes_now, axis=1)
    gates = picked / lax.optimization_barrier(jnp.sum(picked, axis=-1, keepdims=True))
    outputs = route_experts(normed_moe, routes_now, w_in, w_out)
    return resid + lax.optimization_barrier(jnp.sum(gates[:, :, None] * outputs, axis=1))

def reference(layer_in, out_grad, routes, segments, buckets, gain_attn, w_query, w_key, w_value, w_output, gain_moe, router, rel_bias, w_expert_in, w_expert_out):
    params = tuple((item.astype(jnp.float32) for item in (gain_attn, w_query, w_key, w_value, w_output, gain_moe, router, rel_bias, w_expert_in, w_expert_out)))

    def one_micro(totals, items):
        inputs, grad_top, routes_now, seg_now = items
        result, pull = jax.vjp(lambda xs, ps: layer(xs, seg_now, routes_now, buckets, ps), inputs.astype(jnp.float32), params)
        grad_inputs, grad_params = pull(grad_top.astype(jnp.float32))
        totals = jax.tree.map(lambda left, right: left + right, totals, grad_params)
        return (totals, (result.astype(jnp.bfloat16), grad_inputs))
    zeros = jax.tree.map(jnp.zeros_like, params)
    totals, stacked = lax.scan(one_micro, zeros, (layer_in, out_grad, routes, segments))
    return (stacked[0], stacked[1], totals[0], totals[1], totals[2], totals[3], totals[4], totals[5], totals[6], totals[7], totals[8], totals[9])
```

```python
import functools
import math

import jax
import jax.numpy as jnp
from jax import lax
from jax.experimental import pallas as pl
from jax.experimental.pallas import tpu as pltpu
from jax.sharding import PartitionSpec as P

D = 768
NB = 32
MICRO = 4


EPSILON = 1e-06
MASKED = -1e30
TOP_PRECISION = lax.Precision.HIGHEST
GELU_A = math.sqrt(2.0 / math.pi)
GELU_B = 0.044715


def norm_forward(values, gain):
    inverse = lax.rsqrt(jnp.mean(values * values, axis=-1, keepdims=True) + EPSILON)
    scaled = values * inverse
    return (scaled, inverse, scaled * gain)


def norm_backward(grad_top, scaled, inverse, gain):
    grad_scaled = grad_top * gain
    grad_values = inverse * (
        grad_scaled - scaled * jnp.mean(grad_scaled * scaled, axis=-1, keepdims=True)
    )
    return (grad_values, jnp.sum(grad_top * scaled, axis=0))


def split_heads(values, heads):
    return values.reshape(values.shape[0], heads, -1).transpose(1, 0, 2)


def merge_heads(values):
    return values.transpose(1, 0, 2).reshape(values.shape[1], -1)


def score_block(q_heads, k_heads, bias, allowed, scale):
    raw = jnp.einsum("hqd,hkd->hqk", q_heads, k_heads, preferred_element_type=jnp.float32)
    return jnp.where(allowed[None], raw * scale + bias, MASKED)


def bucket_table(distances, bucket_starts):
    lower = bucket_starts[:-1]
    upper = bucket_starts[1:]
    return (
        (distances[:, :, None] >= lower[None, None, :])
        & (distances[:, :, None] < upper[None, None, :])
    ).astype(jnp.bfloat16)


def on_device(
    layer_in,
    out_grad,
    routes,
    segments,
    buckets,
    gain_attn,
    w_query,
    w_key,
    w_value,
    w_output,
    gain_moe,
    router,
    rel_bias,
    w_expert_in,
    w_expert_out,
):
    tok_rows = layer_in.shape[1]
    seq_len = segments.shape[1]
    heads = rel_bias.shape[1]
    group_size = lax.axis_size("expert")
    rank_here = lax.axis_index("expert")
    expert_count = router.shape[1]
    local_experts = w_expert_in.shape[0]
    capacity = 3 * tok_rows // group_size
    scale = 1.0 / math.sqrt(D // heads)
    bucket_starts = jnp.sum(
        (buckets[None, :] < jnp.arange(NB + 1, dtype=jnp.int32)[:, None]).astype(jnp.int32), axis=1
    )
    query_pos = rank_here * tok_rows + jnp.arange(tok_rows, dtype=jnp.int32)
    key_pos = jnp.arange(seq_len, dtype=jnp.int32)
    offsets = jnp.maximum(query_pos[:, None] - key_pos[None, :], 0)
    bucket_onehot = bucket_table(offsets, bucket_starts)
    causal = query_pos[:, None] >= key_pos[None, :]
    slot_ids = jnp.arange(expert_count * capacity, dtype=jnp.int32)
    expert_ids = jnp.arange(expert_count, dtype=jnp.int32)
    pair_ids = jnp.arange(2 * tok_rows, dtype=jnp.int32)
    earlier = (pair_ids[None, :] < pair_ids[:, None]).astype(jnp.bfloat16)
    dense_sums = [
        jnp.zeros((D,), jnp.float32),
        jnp.zeros((D, D), jnp.float32),
        jnp.zeros((D, D), jnp.float32),
        jnp.zeros((D, D), jnp.float32),
        jnp.zeros((D, D), jnp.float32),
        jnp.zeros((D,), jnp.float32),
        jnp.zeros((D, expert_count), jnp.float32),
        jnp.zeros((NB, heads), jnp.float32),
    ]
    in_sum = jnp.zeros(w_expert_in.shape, jnp.float32)
    out_sum = jnp.zeros(w_expert_out.shape, jnp.float32)
    outputs_list = []
    grads_list = []
    for step_index in range(MICRO):
        weights_now = (
            lax.all_gather(gain_attn, "dp", axis=0, tiled=True),
            lax.all_gather(w_query, "dp", axis=0, tiled=True),
            lax.all_gather(w_key, "dp", axis=0, tiled=True),
            lax.all_gather(w_value, "dp", axis=0, tiled=True),
            lax.all_gather(w_output, "dp", axis=0, tiled=True),
            lax.all_gather(gain_moe, "dp", axis=0, tiled=True),
            lax.all_gather(router, "dp", axis=0, tiled=True),
            lax.all_gather(rel_bias, "dp", axis=0, tiled=True),
        )
        gain_a, query_w, key_w, value_w, output_w, gain_m, router_w, bias_table = weights_now
        gain_af = gain_a.astype(jnp.float32)
        gain_mf = gain_m.astype(jnp.float32)
        inputs = layer_in[step_index].astype(jnp.float32)
        scaled_a, inverse_a, normed_a = norm_forward(inputs, gain_af)
        normed_ab = normed_a.astype(jnp.bfloat16)
        queries = jnp.dot(normed_ab, query_w, preferred_element_type=jnp.float32).astype(
            jnp.bfloat16
        )
        keys_loc = jnp.dot(normed_ab, key_w, preferred_element_type=jnp.float32).astype(
            jnp.bfloat16
        )
        values_loc = jnp.dot(normed_ab, value_w, preferred_element_type=jnp.float32).astype(
            jnp.bfloat16
        )
        keys_all, values_all = (
            lax.all_gather(keys_loc, "expert", axis=0, tiled=True),
            lax.all_gather(values_loc, "expert", axis=0, tiled=True),
        )
        q_heads = split_heads(queries, heads)
        k_heads = split_heads(keys_all, heads)
        v_heads = split_heads(values_all, heads)
        bias = jnp.einsum(
            "qkb,bh->hqk", bucket_onehot, bias_table, preferred_element_type=jnp.float32
        )
        seg_all = segments[step_index]
        seg_here = lax.dynamic_slice_in_dim(seg_all, rank_here * tok_rows, tok_rows)
        allowed = causal & (seg_here[:, None] == seg_all[None, :])
        scores = score_block(q_heads, k_heads, bias, allowed, scale)
        top_score = jnp.max(scores, axis=-1, keepdims=True)
        lifted = jnp.exp(scores - top_score)
        total = jnp.sum(lifted, axis=-1, keepdims=True)
        log_total = top_score + jnp.log(total)
        probs_b = (lifted / total).astype(jnp.bfloat16)
        attended = merge_heads(
            jnp.einsum("hqk,hkd->hqd", probs_b, v_heads, preferred_element_type=jnp.float32)
        ).astype(jnp.bfloat16)
        resid = inputs + jnp.dot(attended, output_w, preferred_element_type=jnp.float32)
        scaled_m, inverse_m, normed_m = norm_forward(resid, gain_mf)
        normed_mb = normed_m.astype(jnp.bfloat16)
        logits = jnp.dot(normed_mb, router_w, preferred_element_type=jnp.float32)
        router_probs = jax.nn.softmax(logits, axis=-1)
        routes_now = routes[step_index]
        pick_first = (routes_now[:, 0:1] == expert_ids[None, :]).astype(jnp.float32)
        pick_second = (routes_now[:, 1:2] == expert_ids[None, :]).astype(jnp.float32)
        prob_first = jnp.sum(router_probs * pick_first, axis=-1)
        prob_second = jnp.sum(router_probs * pick_second, axis=-1)
        denom = prob_first + prob_second
        gate_first = prob_first / denom
        gate_second = prob_second / denom
        flat = routes_now.reshape(-1)
        flat_hot = (flat[:, None] == expert_ids[None, :]).astype(jnp.bfloat16)
        before = jnp.dot(earlier, flat_hot, preferred_element_type=jnp.float32)
        places = jnp.sum(before * flat_hot.astype(jnp.float32), axis=1).astype(jnp.int32)
        slot_pairs = (flat * capacity + places).reshape(tok_rows, 2)
        place_first = (slot_ids[:, None] == slot_pairs[None, :, 0]).astype(jnp.bfloat16)
        place_second = (slot_ids[:, None] == slot_pairs[None, :, 1]).astype(jnp.bfloat16)
        place_both = place_first + place_second
        outgoing = jnp.dot(place_both, normed_mb, preferred_element_type=jnp.float32).astype(
            jnp.bfloat16
        )
        outgoing = outgoing.reshape(group_size, local_experts, capacity, D)
        arrived_rows = lax.all_to_all(outgoing, "expert", split_axis=0, concat_axis=0, tiled=True)
        pre_act = jnp.einsum(
            "sjcd,jdf->sjcf", arrived_rows, w_expert_in, preferred_element_type=jnp.float32
        )
        post_act = jax.nn.gelu(pre_act).astype(jnp.bfloat16)
        produced = jnp.einsum(
            "sjcf,jfd->sjcd", post_act, w_expert_out, preferred_element_type=jnp.float32
        ).astype(jnp.bfloat16)
        produced, pre_act, post_act, arrived = (produced, pre_act, post_act, arrived_rows)
        returned = lax.all_to_all(
            produced, "expert", split_axis=0, concat_axis=0, tiled=True
        ).reshape(expert_count * capacity, D)
        got_first = jnp.einsum(
            "st,sd->td", place_first, returned, preferred_element_type=jnp.float32
        )
        got_second = jnp.einsum(
            "st,sd->td", place_second, returned, preferred_element_type=jnp.float32
        )
        result = resid + (gate_first[:, None] * got_first + gate_second[:, None] * got_second)
        outputs_list.append(result.astype(jnp.bfloat16))
        grad_top = out_grad[step_index].astype(jnp.float32)
        dgate_first = jnp.sum(grad_top * got_first, axis=-1)
        dgate_second = jnp.sum(grad_top * got_second, axis=-1)
        sent_first = (gate_first[:, None] * grad_top).astype(jnp.bfloat16)
        sent_second = (gate_second[:, None] * grad_top).astype(jnp.bfloat16)
        grad_slots = (
            jnp.dot(place_first, sent_first, preferred_element_type=jnp.float32)
            + jnp.dot(place_second, sent_second, preferred_element_type=jnp.float32)
        ).astype(jnp.bfloat16)
        grad_slots = grad_slots.reshape(group_size, local_experts, capacity, D)
        grad_arrived = lax.all_to_all(grad_slots, "expert", split_axis=0, concat_axis=0, tiled=True)
        grad_post = jnp.einsum(
            "sjcd,jfd->sjcf", grad_arrived, w_expert_out, preferred_element_type=jnp.float32
        )
        out_sum = out_sum + jnp.einsum(
            "sjcf,sjcd->jfd", post_act, grad_arrived, preferred_element_type=jnp.float32
        )
        grad_pre = jax.vjp(jax.nn.gelu, pre_act)[1](grad_post)[0].astype(jnp.bfloat16)
        in_sum = in_sum + jnp.einsum(
            "sjcd,sjcf->jdf", arrived, grad_pre, preferred_element_type=jnp.float32
        )
        grad_rows = jnp.einsum(
            "sjcf,jdf->sjcd", grad_pre, w_expert_in, preferred_element_type=jnp.float32
        ).astype(jnp.bfloat16)
        grad_back = lax.all_to_all(
            grad_rows, "expert", split_axis=0, concat_axis=0, tiled=True
        ).reshape(expert_count * capacity, D)
        grad_moe = jnp.einsum(
            "st,sd->td", place_both, grad_back, preferred_element_type=jnp.float32
        )
        weighted = dgate_first * gate_first + dgate_second * gate_second
        grad_pick = ((dgate_first - weighted) / denom)[:, None] * pick_first + (
            (dgate_second - weighted) / denom
        )[:, None] * pick_second
        grad_logits = router_probs * (
            grad_pick - jnp.sum(router_probs * grad_pick, axis=-1, keepdims=True)
        )
        normed_mf = normed_mb.astype(jnp.float32)
        grad_router_w = jnp.dot(normed_mf.T, grad_logits, precision=TOP_PRECISION)
        grad_moe = grad_moe + jnp.dot(
            grad_logits, router_w.astype(jnp.float32).T, precision=TOP_PRECISION
        )
        grad_resid_norm, grad_gain_m = norm_backward(grad_moe, scaled_m, inverse_m, gain_mf)
        grad_resid = grad_top + grad_resid_norm
        grad_branch = grad_resid.astype(jnp.bfloat16)
        grad_output_w = jnp.einsum(
            "td,te->de", attended, grad_branch, preferred_element_type=jnp.float32
        )
        grad_attended = jnp.einsum(
            "te,de->td", grad_branch, output_w, preferred_element_type=jnp.float32
        ).astype(jnp.bfloat16)
        grad_heads = split_heads(grad_attended, heads)
        scores_again = score_block(q_heads, k_heads, bias, allowed, scale)
        probs_again = jnp.exp(scores_again - log_total)
        probs_again_b = probs_again.astype(jnp.bfloat16)
        grad_probs = jnp.einsum(
            "hqd,hkd->hqk", grad_heads, v_heads, preferred_element_type=jnp.float32
        )
        row_delta = jnp.sum(probs_again * grad_probs, axis=-1, keepdims=True)
        grad_scores = probs_again * (grad_probs - row_delta)
        grad_table = jnp.einsum(
            "hqk,qkb->bh", grad_scores, bucket_onehot.astype(jnp.float32), precision=TOP_PRECISION
        )
        grad_scores_b = (grad_scores * scale).astype(jnp.bfloat16)
        grad_q_heads = jnp.einsum(
            "hqk,hkd->hqd", grad_scores_b, k_heads, preferred_element_type=jnp.float32
        )
        grad_v_heads = jnp.einsum(
            "hqk,hqd->hkd", probs_again_b, grad_heads, preferred_element_type=jnp.float32
        )
        grad_k_heads = jnp.einsum(
            "hqk,hqd->hkd", grad_scores_b, q_heads, preferred_element_type=jnp.float32
        )
        grad_keys, grad_values = (
            lax.psum_scatter(merge_heads(grad_k_heads), "expert", scatter_dimension=0, tiled=True),
            lax.psum_scatter(merge_heads(grad_v_heads), "expert", scatter_dimension=0, tiled=True),
        )
        grad_queries_b = merge_heads(grad_q_heads).astype(jnp.bfloat16)
        grad_keys_b = grad_keys.astype(jnp.bfloat16)
        grad_values_b = grad_values.astype(jnp.bfloat16)
        grad_query_w = jnp.einsum(
            "td,te->de", normed_ab, grad_queries_b, preferred_element_type=jnp.float32
        )
        grad_key_w = jnp.einsum(
            "td,te->de", normed_ab, grad_keys_b, preferred_element_type=jnp.float32
        )
        grad_value_w = jnp.einsum(
            "td,te->de", normed_ab, grad_values_b, preferred_element_type=jnp.float32
        )
        grad_normed = (
            jnp.einsum("te,de->td", grad_queries_b, query_w, preferred_element_type=jnp.float32)
            + jnp.einsum("te,de->td", grad_keys_b, key_w, preferred_element_type=jnp.float32)
            + jnp.einsum("te,de->td", grad_values_b, value_w, preferred_element_type=jnp.float32)
        )
        grad_in_norm, grad_gain_a = norm_backward(grad_normed, scaled_a, inverse_a, gain_af)
        grads_list.append(grad_resid + grad_in_norm)
        parts_now = (
            grad_gain_a,
            grad_query_w,
            grad_key_w,
            grad_value_w,
            grad_output_w,
            grad_gain_m,
            grad_router_w,
            grad_table,
        )
        dense_sums = [running + addend for running, addend in zip(dense_sums, parts_now)]
    sum_gain_a, sum_query, sum_key, sum_value, sum_output, sum_gain_m, sum_router, sum_table = (
        dense_sums
    )
    summed = lax.psum(
        (sum_gain_a, sum_query, sum_key, sum_value, sum_output, sum_gain_m, sum_router, sum_table),
        "expert",
    )
    (
        full_gain_a,
        full_query,
        full_key,
        full_value,
        full_output,
        full_gain_m,
        full_router,
        full_table,
    ) = summed
    shares = (
        lax.psum_scatter(full_gain_a, "dp", scatter_dimension=0, tiled=True),
        lax.psum_scatter(full_query, "dp", scatter_dimension=0, tiled=True),
        lax.psum_scatter(full_key, "dp", scatter_dimension=0, tiled=True),
        lax.psum_scatter(full_value, "dp", scatter_dimension=0, tiled=True),
        lax.psum_scatter(full_output, "dp", scatter_dimension=0, tiled=True),
        lax.psum_scatter(full_gain_m, "dp", scatter_dimension=0, tiled=True),
        lax.psum_scatter(full_router, "dp", scatter_dimension=0, tiled=True),
        lax.psum_scatter(full_table, "dp", scatter_dimension=0, tiled=True),
    )
    expert_in_grad, expert_out_grad = (
        lax.psum(in_sum.astype(jnp.bfloat16), "dp").astype(jnp.float32),
        lax.psum(out_sum.astype(jnp.bfloat16), "dp").astype(jnp.float32),
    )
    layer_out = jnp.stack(outputs_list)
    grad_in = jnp.stack(grads_list)
    return (
        layer_out,
        grad_in,
        shares[0],
        shares[1],
        shares[2],
        shares[3],
        shares[4],
        shares[5],
        shares[6],
        shares[7],
        expert_in_grad,
        expert_out_grad,
    )


F32 = jnp.float32
BF16 = jnp.bfloat16
TILE = 256
VMEM_LIMIT = 60 * 2**20


def nn(left, right):
    return lax.dot_general(left, right, (((1,), (0,)), ((), ())), preferred_element_type=F32)


def nt(left, right):
    return lax.dot_general(left, right, (((1,), (1,)), ((), ())), preferred_element_type=F32)


def tn(left, right):
    return lax.dot_general(left, right, (((0,), (0,)), ((), ())), preferred_element_type=F32)


def call(body, name, grid, ins, outs, out_shapes, scratch=(), flops=0, nbytes=0):
    return pl.pallas_call(
        body,
        grid=grid,
        in_specs=ins,
        out_specs=outs,
        out_shape=out_shapes,
        scratch_shapes=list(scratch),
        compiler_params=pltpu.CompilerParams(
            dimension_semantics=("arbitrary",) * len(grid), vmem_limit_bytes=VMEM_LIMIT
        ),
        cost_estimate=pl.CostEstimate(flops=flops, bytes_accessed=nbytes, transcendentals=0),
        name=name,
    )


def whole(shape):
    zeros = (0,) * len(shape)
    return pl.BlockSpec(shape, lambda *_: zeros)


def rows(width, tile=TILE):
    return pl.BlockSpec((tile, width), lambda i: (i, 0))


def sds(shape, dtype):
    return jax.ShapeDtypeStruct(shape, dtype)


def weight(wall_ref, index, share):
    return wall_ref[:, index * share : (index + 1) * share, :].reshape(-1, D)


def bias_kernel(bias_ref, table_ref):
    row = bias_ref[0]
    for delta in range(table_ref.shape[1]):
        ahead = row[:, delta * TILE : (delta + 1) * TILE]
        back = row[:, (delta - 1) * TILE : delta * TILE] if delta else jnp.zeros_like(ahead)
        line = jnp.concatenate([ahead, back], axis=1)
        grid = jnp.broadcast_to(line, (TILE, 2 * TILE))
        grid = pltpu.roll(grid, 0, 1, stride=1, stride_axis=0)
        table_ref[0, delta] = grid[:, :TILE].astype(BF16)


def project_kernel(x_ref, gain_ref, wall_ref, a_ref, q_ref, k_ref, v_ref, *, share, scale):
    x = x_ref[...].astype(F32)
    inverse = lax.rsqrt(jnp.mean(x * x, axis=-1, keepdims=True) + EPSILON)
    normed = (x * inverse * gain_ref[...]).astype(BF16)
    a_ref[...] = normed
    q = nn(normed, weight(wall_ref, 0, share)).astype(BF16)
    q_ref[...] = (q.astype(F32) * scale).astype(BF16)
    k_ref[...] = nn(normed, weight(wall_ref, 1, share)).astype(BF16)
    v_ref[...] = nn(normed, weight(wall_ref, 2, share)).astype(BF16)


def masked_scores(k, q, table_ref, head, i, j, seg_col, seg_row):
    scores = nt(k, q) + table_ref[head, i - j].astype(F32)
    allowed = seg_col == seg_row
    if i == j:
        key_at = lax.broadcasted_iota(jnp.int32, (TILE, TILE), 0)
        query_at = lax.broadcasted_iota(jnp.int32, (TILE, TILE), 1)
        allowed = allowed & (key_at <= query_at)
    return jnp.where(allowed, scores, MASKED)


def attend_kernel(q_ref, k_ref, v_ref, table_ref, col_ref, row_ref, o_ref, lse_ref, *, width):
    blocks = q_ref.shape[0] // TILE
    heads = q_ref.shape[1] // width
    turned = [v_ref[:, h * width : (h + 1) * width].T for h in range(heads)]
    for i in range(blocks):
        here = slice(i * TILE, (i + 1) * TILE)
        outs = []
        for h in range(heads):
            lanes = slice(h * width, (h + 1) * width)
            q = q_ref[here, lanes]
            pieces = []
            for j in range(i + 1):
                there = slice(j * TILE, (j + 1) * TILE)
                pieces.append(
                    masked_scores(
                        k_ref[there, lanes], q, table_ref, h, i, j, col_ref[there, :], row_ref[:, here]
                    )
                )
            top = pieces[0].max(axis=0, keepdims=True)
            for piece in pieces[1:]:
                top = jnp.maximum(top, piece.max(axis=0, keepdims=True))
            total = jnp.zeros_like(top)
            acc = jnp.zeros((width, TILE), F32)
            for j, piece in enumerate(pieces):
                lifted = jnp.exp(piece - top)
                total = total + lifted.sum(axis=0, keepdims=True)
                acc = acc + nn(turned[h][:, j * TILE : (j + 1) * TILE], lifted.astype(BF16))
            outs.append(acc / total)
            lse_ref[0, h : h + 1, here] = top + jnp.log(total)
        o_ref[here, :] = jnp.concatenate(outs, axis=0).T.astype(BF16)


def attend_back_kernel(
    q_ref, k_ref, v_ref, do_ref, table_ref, col_ref, row_ref, lse_ref,
    dq_ref, dk_ref, dv_ref, dist_ref, sum_ref, dk_sum, dv_sum, *, width, scale
):
    blocks = q_ref.shape[0] // TILE
    heads = q_ref.shape[1] // width
    turned = [k_ref[:, h * width : (h + 1) * width].T for h in range(heads)]
    dist_ref[...] = jnp.zeros_like(dist_ref)
    for h in range(heads):
        lanes = slice(h * width, (h + 1) * width)
        for i in range(blocks):
            here = slice(i * TILE, (i + 1) * TILE)
            q = q_ref[here, lanes]
            do = do_ref[here, lanes]
            lse = lse_ref[0, h : h + 1, here]
            probs, dprobs = [], []
            delta = jnp.zeros((1, TILE), F32)
            for j in range(i + 1):
                there = slice(j * TILE, (j + 1) * TILE)
                scores = masked_scores(
                    k_ref[there, lanes], q, table_ref, h, i, j, col_ref[there, :], row_ref[:, here]
                )
                p = jnp.exp(scores - lse)
                dp = nt(v_ref[there, lanes], do)
                delta = delta + (p * dp).sum(axis=0, keepdims=True)
                probs.append(p)
                dprobs.append(dp)
            turned_dq = jnp.zeros((width, TILE), F32)
            for j in range(i + 1):
                there = slice(j * TILE, (j + 1) * TILE)
                ds = probs[j] * (dprobs[j] - delta)
                low = ds.astype(BF16)
                dv = nn(probs[j].astype(BF16), do)
                dk = nn(low, q)
                if i == j:
                    dv_sum[there, lanes] = dv
                    dk_sum[there, lanes] = dk
                else:
                    dv_sum[there, lanes] += dv
                    dk_sum[there, lanes] += dk
                turned_dq = turned_dq + nn(turned[h][:, there], low)
                if j == 0:
                    sum_ref[i - j] = ds
                else:
                    sum_ref[i - j] += ds
            dq_ref[here, lanes] = (turned_dq * scale).T.astype(BF16)
        for gap in range(blocks):
            part = sum_ref[gap]
            part = jnp.concatenate([part, jnp.zeros_like(part)], axis=1)
            half = TILE // 2
            while half:
                part = part[:half] + pltpu.roll(part[half : 2 * half], 2 * TILE - half, 1)
                half //= 2
            dist_ref[0, h : h + 1, gap * TILE : (gap + 1) * TILE] += part[:, :TILE]
            if gap:
                dist_ref[0, h : h + 1, (gap - 1) * TILE : gap * TILE] += part[:, TILE:]
    dk_ref[...] = dk_sum[...].astype(BF16)
    dv_ref[...] = dv_sum[...].astype(BF16)


def route_kernel(
    x_ref, o_ref, wall_ref, gain_ref, router_ref, routes_ref, h_ref, a_ref, gate_ref, pr_ref,
    *, share, experts
):
    h1 = x_ref[...].astype(F32) + nn(o_ref[...], weight(wall_ref, 3, share))
    h_ref[...] = h1
    inverse = lax.rsqrt(jnp.mean(h1 * h1, axis=-1, keepdims=True) + EPSILON)
    normed = (h1 * inverse * gain_ref[...]).astype(BF16)
    a_ref[...] = normed
    logits = nn(normed, router_ref[...])
    lane = lax.broadcasted_iota(jnp.int32, logits.shape, 1)
    logits = jnp.where(lane < experts, logits, MASKED)
    lifted = jnp.exp(logits - logits.max(axis=-1, keepdims=True))
    pr = lifted / lifted.sum(axis=-1, keepdims=True)
    named = (routes_ref[:, 0:1] == lane) | (routes_ref[:, 1:2] == lane)
    picked = jnp.where(named, pr, 0.0)
    pr_ref[...] = pr
    gate_ref[...] = picked / picked.sum(axis=-1, keepdims=True)


def expert_kernel(
    a_ref, g_ref, gate_ref, pos_ref, w_ref, eo_ref, da_ref, dw_ref, rows_a, rows_d, eo_sum, da_sum,
    *, index, capacity
):
    step = pl.program_id(0)

    @pl.when(step == 0)
    def _():
        tokens = a_ref.shape[0]
        slot = lax.broadcasted_iota(jnp.int32, (capacity, tokens), 0)
        pick = (pos_ref[index : index + 1, :] == slot).astype(BF16)
        rows_a[...] = nn(pick, a_ref[...]).astype(BF16)
        scaled = (gate_ref[:, index : index + 1] * g_ref[...].astype(F32)).astype(BF16)
        rows_d[...] = nn(pick, scaled).astype(BF16)
        eo_sum[...] = jnp.zeros_like(eo_sum)
        da_sum[...] = jnp.zeros_like(da_sum)

    a = rows_a[...]
    d = rows_d[...]
    w_in = w_ref[0, 0]
    w_out = w_ref[0, 1]
    u = nt(a, w_in)
    cube = u * u
    t = jnp.tanh(GELU_A * u * (1.0 + GELU_B * cube))
    half = 0.5 * (1.0 + t)
    z = (u * half).astype(BF16)
    eo_sum[...] += nn(z, w_out)
    dw_ref[0, 1] = tn(z, d).astype(BF16)
    slope = half + (0.5 * GELU_A) * u * (1.0 - t * t) * (1.0 + 3.0 * GELU_B * cube)
    du = (nt(d, w_out) * slope).astype(BF16)
    da_sum[...] += nn(du, w_in)
    dw_ref[0, 0] = tn(du, a).astype(BF16)

    @pl.when(step == pl.num_programs(0) - 1)
    def _():
        eo_ref[...] = eo_sum[...].astype(BF16)
        da_ref[...] = da_sum[...].astype(BF16)


def combine_kernel(
    h_ref, a_ref, g_ref, o_ref, gate_ref, pr_ref, routes_ref, pos_ref, eo0, eo1, eo2, eo3,
    da0, da1, da2, da3, wall_ref, gain_ref, router_ref,
    out_ref, dh_ref, do_ref, dw_ref, dgain_ref, drouter_ref, *, share, experts, capacity
):
    step = pl.program_id(0)

    @pl.when(step == 0)
    def _():
        dw_ref[...] = jnp.zeros_like(dw_ref)
        dgain_ref[...] = jnp.zeros_like(dgain_ref)
        drouter_ref[...] = jnp.zeros_like(drouter_ref)

    tile = h_ref.shape[0]
    h1 = h_ref[...]
    g = g_ref[...].astype(F32)
    gates = gate_ref[...]
    pr = pr_ref[...]
    lane = lax.broadcasted_iota(jnp.int32, pr.shape, 1)
    slot = lax.broadcasted_iota(jnp.int32, (tile, capacity), 1)
    result = h1
    dgate = jnp.zeros_like(pr)
    da = jnp.zeros_like(h1)
    for k, (eo, back) in enumerate(((eo0, da0), (eo1, da1), (eo2, da2), (eo3, da3))):
        place = (pos_ref[:, k : k + 1] == slot).astype(BF16)
        got = nn(place, eo[...])
        result = result + gates[:, k : k + 1] * got
        dgate = jnp.where(lane == k, jnp.sum(g * got, axis=-1, keepdims=True), dgate)
        da = da + nn(place, back[...])
    out_ref[...] = result.astype(BF16)
    named = (routes_ref[:, 0:1] == lane) | (routes_ref[:, 1:2] == lane)
    denom = jnp.sum(jnp.where(named, pr, 0.0), axis=-1, keepdims=True)
    weighted = jnp.sum(dgate * gates, axis=-1, keepdims=True)
    dpr = jnp.where(named, (dgate - weighted) / denom, 0.0)
    dlog = pr * (dpr - jnp.sum(pr * dpr, axis=-1, keepdims=True))
    high = dlog.astype(BF16)
    lost = (dlog - high.astype(F32)).astype(BF16)
    a = a_ref[...]
    drouter_ref[...] += tn(a, high) + tn(a, lost)
    for k in range(experts):
        da = da + dlog[:, k : k + 1] * router_ref[k : k + 1, :]
    inverse = lax.rsqrt(jnp.mean(h1 * h1, axis=-1, keepdims=True) + EPSILON)
    n2 = h1 * inverse
    dgain_ref[...] += jnp.sum(da * n2, axis=0, keepdims=True)
    dn = da * gain_ref[...]
    dh = g + inverse * (dn - n2 * jnp.mean(dn * n2, axis=-1, keepdims=True))
    dh_ref[...] = dh
    dy = dh.astype(BF16)
    do_ref[...] = nt(dy, weight(wall_ref, 3, share)).astype(BF16)
    dw_ref[...] += tn(o_ref[...], dy)


def finish_kernel(
    x_ref, a_ref, dq_ref, dk_ref, dv_ref, dh_ref, wall_ref, gain_ref, dwo_ref,
    din_ref, pack_ref, dgain_ref, sum_ref, *, share
):
    step = pl.program_id(0)

    @pl.when(step == 0)
    def _():
        sum_ref[...] = jnp.zeros_like(sum_ref)
        dgain_ref[...] = jnp.zeros_like(dgain_ref)

    a = a_ref[...]
    da = jnp.zeros(dh_ref.shape, F32)
    for index, grad_ref in enumerate((dq_ref, dk_ref, dv_ref)):
        grad = grad_ref[...]
        sum_ref[index] += tn(a, grad)
        da = da + nt(grad, weight(wall_ref, index, share))
    x = x_ref[...].astype(F32)
    inverse = lax.rsqrt(jnp.mean(x * x, axis=-1, keepdims=True) + EPSILON)
    n1 = x * inverse
    dgain_ref[...] += jnp.sum(da * n1, axis=0, keepdims=True)
    dn = da * gain_ref[...]
    din = dh_ref[...] + inverse * (dn - n1 * jnp.mean(dn * n1, axis=-1, keepdims=True))
    din_ref[...] = din.astype(BF16)

    @pl.when(step == pl.num_programs(0) - 1)
    def _():
        for index in range(3):
            pack_ref[:, index * share : (index + 1) * share, :] = (
                sum_ref[index].astype(BF16).reshape(-1, share, D)
            )
        pack_ref[:, 3 * share :, :] = dwo_ref[...].astype(BF16).reshape(-1, share, D)


def unpack_kernel(w_ref, in_ref, out_ref):
    in_ref[0] = w_ref[0, 0].astype(F32).T
    out_ref[0] = w_ref[0, 1].astype(F32)


def on_device_whole(
    layer_in, out_grad, routes, segments, buckets, gain_attn, w_query, w_key, w_value, w_output,
    gain_moe, router, rel_bias, w_expert_in, w_expert_out,
):
    group = lax.axis_size("expert")
    rank = lax.axis_index("expert")
    shards = lax.axis_size("dp")
    shard = lax.axis_index("dp")
    experts = router.shape[1]
    seq = segments.shape[1]
    heads = rel_bias.shape[1]
    width = D // heads
    scale = 1.0 / math.sqrt(width)
    share = D // shards
    ff = w_expert_in.shape[2]
    chunk = ff // shards
    blocks = seq // TILE
    capacity = 3 * seq // group
    pairs = 128 // width

    def across(values):
        return lax.all_to_all(values, "expert", split_axis=0, concat_axis=1, tiled=True)[0]

    x = across(layer_in)
    routes_here = jnp.remainder(across(routes) - rank, experts)
    g = across(out_grad)
    row = lambda v: jnp.pad(v.reshape(1, -1), ((0, 0), (0, D - v.size)))
    pack = jnp.concatenate(
        [w_query, w_key, w_value, w_output, row(gain_attn), row(gain_moe), row(router), row(rel_bias),
         jnp.zeros((4, D), BF16)], axis=0)
    wall = lax.all_gather(pack, "dp", axis=0)
    base = 4 * share
    gain_a = wall[:, base, :share].reshape(1, D).astype(F32)
    gain_m = wall[:, base + 1, :share].reshape(1, D).astype(F32)
    router_all = wall[:, base + 2, : router.size].reshape(D, experts)
    bias_all = wall[:, base + 3, : rel_bias.size].reshape(NB, heads)
    turn = (jnp.arange(experts, dtype=jnp.int32)[:, None] == jnp.remainder(
        jnp.arange(experts, dtype=jnp.int32)[None, :] + rank, experts)).astype(BF16)
    router_rel = jnp.dot(router_all, turn, preferred_element_type=F32)
    router_pad = jnp.pad(router_rel, ((0, 0), (0, 128 - experts))).astype(BF16)
    router_turned = jnp.pad(router_rel.T, ((0, 8 - experts), (0, 0)))
    own = jnp.stack([
        lax.dynamic_slice_in_dim(w_expert_in[0], shard * chunk, chunk, axis=1).T,
        lax.dynamic_slice_in_dim(w_expert_out[0], shard * chunk, chunk, axis=0),
    ])
    local = jnp.stack(
        [w_expert_in[0].T.reshape(shards, chunk, D), w_expert_out[0].reshape(shards, chunk, D)], axis=1
    )
    weights = [local]
    for k in range(1, experts):
        moved = lax.ppermute(own, "expert", [((s + k) % group, s) for s in range(group)])
        weights.append(lax.all_gather(moved, "dp", axis=0))
    hot_buckets = (buckets[None, :] == jnp.arange(NB, dtype=jnp.int32)[:, None]).astype(BF16)
    bias_line = lax.dot_general(
        bias_all, hot_buckets, (((0,), (0,)), ((), ())), preferred_element_type=F32
    ).reshape(heads, 1, seq)
    table = call(
        bias_kernel, "bias", (heads,),
        [pl.BlockSpec((1, 1, seq), lambda i: (i, 0, 0))],
        pl.BlockSpec((1, blocks, TILE, TILE), lambda i: (i, 0, 0, 0)),
        sds((heads, blocks, TILE, TILE), BF16),
    )(bias_line)
    seg = lax.dynamic_slice_in_dim(segments, rank, 1, axis=0)
    seg_row = seg.reshape(1, seq)
    seg_col = seg.reshape(seq, 1)
    expert_ids = jnp.arange(experts, dtype=jnp.int32)
    named = (routes_here[:, 0:1] == expert_ids) | (routes_here[:, 1:2] == expert_ids)
    at = jnp.arange(seq, dtype=jnp.int32)
    before = jnp.dot(
        (at[None, :] < at[:, None]).astype(BF16), named.astype(BF16), preferred_element_type=F32
    ).astype(jnp.int32)
    pos = jnp.where(named, before, -1)
    pos_turned = jnp.pad(pos.T, ((0, 8 - experts), (0, 0)), constant_values=-1)

    tokens = (seq, D)
    normed, q, k, v = call(
        functools.partial(project_kernel, share=share, scale=scale), "project", (blocks,),
        [rows(D), whole((1, D)), whole(wall.shape)],
        [rows(D)] * 4, [sds(tokens, BF16)] * 4, flops=6 * seq * D * D, nbytes=12 * 2**20,
    )(x, gain_a, wall)
    cols = pl.BlockSpec((seq, 128), lambda i: (0, i))
    table_spec = pl.BlockSpec((pairs, blocks, TILE, TILE), lambda i: (i, 0, 0, 0))
    line_spec = pl.BlockSpec((1, pairs, seq), lambda i: (i, 0, 0))
    o, lse = call(
        functools.partial(attend_kernel, width=width), "attend", (heads // pairs,),
        [cols, cols, cols, table_spec, whole((seq, 1)), whole((1, seq))],
        [cols, line_spec],
        [sds(tokens, BF16), sds((heads // pairs, pairs, seq), F32)],
        flops=8 * seq * seq * D, nbytes=16 * 2**20,
    )(q, k, v, table, seg_col, seg_row)
    h1, normed_m, gates, pr = call(
        functools.partial(route_kernel, share=share, experts=experts), "route", (blocks,),
        [rows(D), rows(D), whole(wall.shape), whole((1, D)), whole((D, 128)), rows(2)],
        [rows(D), rows(D), rows(128), rows(128)],
        [sds(tokens, F32), sds(tokens, BF16), sds((seq, 128), F32), sds((seq, 128), F32)],
        flops=2 * seq * D * D, nbytes=12 * 2**20,
    )(x, o, wall, gain_m, router_pad, routes_here)
    produced, returned, partial_sums = [], [], []
    slots = (capacity, D)
    for index in range(experts):
        eo, da, dw = call(
            functools.partial(expert_kernel, index=index, capacity=capacity), f"expert{index}", (shards,),
            [whole(tokens), whole(tokens), whole((seq, 128)), whole((8, seq)),
             pl.BlockSpec((1, 2, chunk, D), lambda i: (i, 0, 0, 0))],
            [whole(slots), whole(slots), pl.BlockSpec((1, 2, chunk, D), lambda i: (i, 0, 0, 0))],
            [sds(slots, BF16), sds(slots, BF16), sds((shards, 2, chunk, D), BF16)],
            [pltpu.VMEM(slots, BF16), pltpu.VMEM(slots, BF16), pltpu.VMEM(slots, F32), pltpu.VMEM(slots, F32)],
            flops=12 * capacity * D * ff, nbytes=24 * 2**20,
        )(normed_m, g, gates, pos_turned, weights[index])
        produced.append(eo)
        returned.append(da)
        partial_sums.append(lax.psum_scatter(dw, "dp", scatter_dimension=0, tiled=True)[0])
    result, dh, do, grad_output, grad_gain_m, grad_router = call(
        functools.partial(combine_kernel, share=share, experts=experts, capacity=capacity), "combine",
        (blocks,),
        [rows(D)] * 4 + [rows(128), rows(128), rows(2), rows(experts)] + [whole(slots)] * 8
        + [whole(wall.shape), whole((1, D)), whole((8, D))],
        [rows(D), rows(D), rows(D), whole((D, D)), whole((1, D)), whole((D, 128))],
        [sds(tokens, BF16), sds(tokens, F32), sds(tokens, BF16), sds((D, D), F32), sds((1, D), F32),
         sds((D, 128), F32)],
        flops=24 * seq * D * D, nbytes=32 * 2**20,
    )(h1, normed_m, g, o, gates, pr, routes_here, pos, *produced, *returned, wall, gain_m, router_turned)
    dq, dk, dv, dist = call(
        functools.partial(attend_back_kernel, width=width, scale=scale), "attend_back", (heads // pairs,),
        [cols, cols, cols, cols, table_spec, whole((seq, 1)), whole((1, seq)), line_spec],
        [cols, cols, cols, line_spec],
        [sds(tokens, BF16)] * 3 + [sds((heads // pairs, pairs, seq), F32)],
        [pltpu.VMEM((blocks, TILE, TILE), F32), pltpu.VMEM((seq, 128), F32), pltpu.VMEM((seq, 128), F32)],
        flops=20 * seq * seq * D, nbytes=24 * 2**20,
    )(q, k, v, do, table, seg_col, seg_row, lse)
    din, dense, grad_gain_a = call(
        functools.partial(finish_kernel, share=share), "finish", (blocks,),
        [rows(D)] * 6 + [whole(wall.shape), whole((1, D)), whole((D, D))],
        [rows(D), whole((shards, 4 * share, D)), whole((1, D))],
        [sds(tokens, BF16), sds((shards, 4 * share, D), BF16), sds((1, D), F32)],
        [pltpu.VMEM((3, D, D), F32)],
        flops=12 * seq * D * D, nbytes=24 * 2**20,
    )(x, normed, dq, dk, dv, dh, wall, gain_a, grad_output)

    def back(values):
        return lax.all_to_all(
            values.reshape(group, seq // group, D), "expert", split_axis=0, concat_axis=0, tiled=True
        )

    layer_out = back(result)
    grad_in = back(din).astype(F32)
    total = partial_sums[0].astype(F32)
    for k in range(1, experts):
        moved = lax.ppermute(partial_sums[k], "expert", [(s, (s + k) % group) for s in range(group)])
        total = total + moved.astype(F32)
    gathered = lax.all_gather(total.astype(BF16), "dp", axis=0)
    expert_in, expert_out = call(
        unpack_kernel, "unpack", (shards,),
        [pl.BlockSpec((1, 2, chunk, D), lambda i: (i, 0, 0, 0))],
        [pl.BlockSpec((1, D, chunk), lambda i: (0, 0, i)), pl.BlockSpec((1, chunk, D), lambda i: (0, i, 0))],
        [sds(w_expert_in.shape, F32), sds(w_expert_out.shape, F32)], nbytes=28 * 2**20,
    )(gathered)
    dense = lax.psum(lax.psum_scatter(dense, "dp", scatter_dimension=0, tiled=True)[0], "expert").astype(F32)
    grad_table = jnp.einsum(
        "bx,hx->bh", hot_buckets.astype(F32), dist.reshape(heads, seq), precision=TOP_PRECISION
    )
    grad_router = jnp.dot(grad_router[:, :experts], turn.astype(F32).T, precision=TOP_PRECISION)
    small = lax.psum(
        jnp.concatenate([
            grad_gain_a.reshape(shards, -1), grad_gain_m.reshape(shards, -1),
            grad_router.reshape(shards, -1), grad_table.reshape(shards, -1)], axis=1),
        ("dp", "expert"),
    )
    small = lax.dynamic_slice_in_dim(small, shard, 1, axis=0)[0]
    return (
        layer_out,
        grad_in,
        small[:share],
        dense[:share],
        dense[share : 2 * share],
        dense[2 * share : 3 * share],
        dense[3 * share :],
        small[share : 2 * share],
        small[2 * share : 2 * share + router.size].reshape(router.shape),
        small[2 * share + router.size :].reshape(rel_bias.shape),
        expert_in,
        expert_out,
    )


def solution(mesh):
    in_specs = (
        P(None, ("dp", "expert"), None),
        P(None, ("dp", "expert"), None),
        P(None, ("dp", "expert"), None),
        P(None, "dp"),
        P(),
        P("dp"),
        P("dp", None),
        P("dp", None),
        P("dp", None),
        P("dp", None),
        P("dp"),
        P("dp", None),
        P("dp", None),
        P("expert", None, None),
        P("expert", None, None),
    )
    out_specs = (
        P(None, ("dp", "expert"), None),
        P(None, ("dp", "expert"), None),
        P("dp"),
        P("dp", None),
        P("dp", None),
        P("dp", None),
        P("dp", None),
        P("dp"),
        P("dp", None),
        P("dp", None),
        P("expert", None, None),
        P("expert", None, None),
    )
    body = on_device_whole if mesh.shape["expert"] == MICRO else on_device
    return jax.shard_map(
        body, mesh=mesh, in_specs=in_specs, out_specs=out_specs, check_vma=False
    )
```

```python
import functools
import math

import jax
import jax.numpy as jnp
from jax import lax
from jax.experimental import pallas as pl
from jax.experimental.pallas import tpu as pltpu
from jax.sharding import PartitionSpec as P

D = 768
NB = 32
MICRO = 4


EPSILON = 1e-06
MASKED = -1e30
TOP_PRECISION = lax.Precision.HIGHEST
GELU_A = math.sqrt(2.0 / math.pi)
GELU_B = 0.044715


def norm_forward(values, gain):
    inverse = lax.rsqrt(jnp.mean(values * values, axis=-1, keepdims=True) + EPSILON)
    scaled = values * inverse
    return (scaled, inverse, scaled * gain)


def norm_backward(grad_top, scaled, inverse, gain):
    grad_scaled = grad_top * gain
    grad_values = inverse * (
        grad_scaled - scaled * jnp.mean(grad_scaled * scaled, axis=-1, keepdims=True)
    )
    return (grad_values, jnp.sum(grad_top * scaled, axis=0))


def split_heads(values, heads):
    return values.reshape(values.shape[0], heads, -1).transpose(1, 0, 2)


def merge_heads(values):
    return values.transpose(1, 0, 2).reshape(values.shape[1], -1)


def score_block(q_heads, k_heads, bias, allowed, scale):
    raw = jnp.einsum("hqd,hkd->hqk", q_heads, k_heads, preferred_element_type=jnp.float32)
    return jnp.where(allowed[None], raw * scale + bias, MASKED)


def bucket_table(distances, bucket_starts):
    lower = bucket_starts[:-1]
    upper = bucket_starts[1:]
    return (
        (distances[:, :, None] >= lower[None, None, :])
        & (distances[:, :, None] < upper[None, None, :])
    ).astype(jnp.bfloat16)


def on_device(
    layer_in,
    out_grad,
    routes,
    segments,
    buckets,
    gain_attn,
    w_query,
    w_key,
    w_value,
    w_output,
    gain_moe,
    router,
    rel_bias,
    w_expert_in,
    w_expert_out,
):
    tok_rows = layer_in.shape[1]
    seq_len = segments.shape[1]
    heads = rel_bias.shape[1]
    group_size = lax.axis_size("expert")
    rank_here = lax.axis_index("expert")
    expert_count = router.shape[1]
    local_experts = w_expert_in.shape[0]
    capacity = 3 * tok_rows // group_size
    scale = 1.0 / math.sqrt(D // heads)
    bucket_starts = jnp.sum(
        (buckets[None, :] < jnp.arange(NB + 1, dtype=jnp.int32)[:, None]).astype(jnp.int32), axis=1
    )
    query_pos = rank_here * tok_rows + jnp.arange(tok_rows, dtype=jnp.int32)
    key_pos = jnp.arange(seq_len, dtype=jnp.int32)
    offsets = jnp.maximum(query_pos[:, None] - key_pos[None, :], 0)
    bucket_onehot = bucket_table(offsets, bucket_starts)
    causal = query_pos[:, None] >= key_pos[None, :]
    slot_ids = jnp.arange(expert_count * capacity, dtype=jnp.int32)
    expert_ids = jnp.arange(expert_count, dtype=jnp.int32)
    pair_ids = jnp.arange(2 * tok_rows, dtype=jnp.int32)
    earlier = (pair_ids[None, :] < pair_ids[:, None]).astype(jnp.bfloat16)
    dense_sums = [
        jnp.zeros((D,), jnp.float32),
        jnp.zeros((D, D), jnp.float32),
        jnp.zeros((D, D), jnp.float32),
        jnp.zeros((D, D), jnp.float32),
        jnp.zeros((D, D), jnp.float32),
        jnp.zeros((D,), jnp.float32),
        jnp.zeros((D, expert_count), jnp.float32),
        jnp.zeros((NB, heads), jnp.float32),
    ]
    in_sum = jnp.zeros(w_expert_in.shape, jnp.float32)
    out_sum = jnp.zeros(w_expert_out.shape, jnp.float32)
    outputs_list = []
    grads_list = []
    for step_index in range(MICRO):
        weights_now = (
            lax.all_gather(gain_attn, "dp", axis=0, tiled=True),
            lax.all_gather(w_query, "dp", axis=0, tiled=True),
            lax.all_gather(w_key, "dp", axis=0, tiled=True),
            lax.all_gather(w_value, "dp", axis=0, tiled=True),
            lax.all_gather(w_output, "dp", axis=0, tiled=True),
            lax.all_gather(gain_moe, "dp", axis=0, tiled=True),
            lax.all_gather(router, "dp", axis=0, tiled=True),
            lax.all_gather(rel_bias, "dp", axis=0, tiled=True),
        )
        gain_a, query_w, key_w, value_w, output_w, gain_m, router_w, bias_table = weights_now
        gain_af = gain_a.astype(jnp.float32)
        gain_mf = gain_m.astype(jnp.float32)
        inputs = layer_in[step_index].astype(jnp.float32)
        scaled_a, inverse_a, normed_a = norm_forward(inputs, gain_af)
        normed_ab = normed_a.astype(jnp.bfloat16)
        queries = jnp.dot(normed_ab, query_w, preferred_element_type=jnp.float32).astype(
            jnp.bfloat16
        )
        keys_loc = jnp.dot(normed_ab, key_w, preferred_element_type=jnp.float32).astype(
            jnp.bfloat16
        )
        values_loc = jnp.dot(normed_ab, value_w, preferred_element_type=jnp.float32).astype(
            jnp.bfloat16
        )
        keys_all, values_all = (
            lax.all_gather(keys_loc, "expert", axis=0, tiled=True),
            lax.all_gather(values_loc, "expert", axis=0, tiled=True),
        )
        q_heads = split_heads(queries, heads)
        k_heads = split_heads(keys_all, heads)
        v_heads = split_heads(values_all, heads)
        bias = jnp.einsum(
            "qkb,bh->hqk", bucket_onehot, bias_table, preferred_element_type=jnp.float32
        )
        seg_all = segments[step_index]
        seg_here = lax.dynamic_slice_in_dim(seg_all, rank_here * tok_rows, tok_rows)
        allowed = causal & (seg_here[:, None] == seg_all[None, :])
        scores = score_block(q_heads, k_heads, bias, allowed, scale)
        top_score = jnp.max(scores, axis=-1, keepdims=True)
        lifted = jnp.exp(scores - top_score)
        total = jnp.sum(lifted, axis=-1, keepdims=True)
        log_total = top_score + jnp.log(total)
        probs_b = (lifted / total).astype(jnp.bfloat16)
        attended = merge_heads(
            jnp.einsum("hqk,hkd->hqd", probs_b, v_heads, preferred_element_type=jnp.float32)
        ).astype(jnp.bfloat16)
        resid = inputs + jnp.dot(attended, output_w, preferred_element_type=jnp.float32)
        scaled_m, inverse_m, normed_m = norm_forward(resid, gain_mf)
        normed_mb = normed_m.astype(jnp.bfloat16)
        logits = jnp.dot(normed_mb, router_w, preferred_element_type=jnp.float32)
        router_probs = jax.nn.softmax(logits, axis=-1)
        routes_now = routes[step_index]
        pick_first = (routes_now[:, 0:1] == expert_ids[None, :]).astype(jnp.float32)
        pick_second = (routes_now[:, 1:2] == expert_ids[None, :]).astype(jnp.float32)
        prob_first = jnp.sum(router_probs * pick_first, axis=-1)
        prob_second = jnp.sum(router_probs * pick_second, axis=-1)
        denom = prob_first + prob_second
        gate_first = prob_first / denom
        gate_second = prob_second / denom
        flat = routes_now.reshape(-1)
        flat_hot = (flat[:, None] == expert_ids[None, :]).astype(jnp.bfloat16)
        before = jnp.dot(earlier, flat_hot, preferred_element_type=jnp.float32)
        places = jnp.sum(before * flat_hot.astype(jnp.float32), axis=1).astype(jnp.int32)
        slot_pairs = (flat * capacity + places).reshape(tok_rows, 2)
        place_first = (slot_ids[:, None] == slot_pairs[None, :, 0]).astype(jnp.bfloat16)
        place_second = (slot_ids[:, None] == slot_pairs[None, :, 1]).astype(jnp.bfloat16)
        place_both = place_first + place_second
        outgoing = jnp.dot(place_both, normed_mb, preferred_element_type=jnp.float32).astype(
            jnp.bfloat16
        )
        outgoing = outgoing.reshape(group_size, local_experts, capacity, D)
        arrived_rows = lax.all_to_all(outgoing, "expert", split_axis=0, concat_axis=0, tiled=True)
        pre_act = jnp.einsum(
            "sjcd,jdf->sjcf", arrived_rows, w_expert_in, preferred_element_type=jnp.float32
        )
        post_act = jax.nn.gelu(pre_act).astype(jnp.bfloat16)
        produced = jnp.einsum(
            "sjcf,jfd->sjcd", post_act, w_expert_out, preferred_element_type=jnp.float32
        ).astype(jnp.bfloat16)
        produced, pre_act, post_act, arrived = (produced, pre_act, post_act, arrived_rows)
        returned = lax.all_to_all(
            produced, "expert", split_axis=0, concat_axis=0, tiled=True
        ).reshape(expert_count * capacity, D)
        got_first = jnp.einsum(
            "st,sd->td", place_first, returned, preferred_element_type=jnp.float32
        )
        got_second = jnp.einsum(
            "st,sd->td", place_second, returned, preferred_element_type=jnp.float32
        )
        result = resid + (gate_first[:, None] * got_first + gate_second[:, None] * got_second)
        outputs_list.append(result.astype(jnp.bfloat16))
        grad_top = out_grad[step_index].astype(jnp.float32)
        dgate_first = jnp.sum(grad_top * got_first, axis=-1)
        dgate_second = jnp.sum(grad_top * got_second, axis=-1)
        sent_first = (gate_first[:, None] * grad_top).astype(jnp.bfloat16)
        sent_second = (gate_second[:, None] * grad_top).astype(jnp.bfloat16)
        grad_slots = (
            jnp.dot(place_first, sent_first, preferred_element_type=jnp.float32)
            + jnp.dot(place_second, sent_second, preferred_element_type=jnp.float32)
        ).astype(jnp.bfloat16)
        grad_slots = grad_slots.reshape(group_size, local_experts, capacity, D)
        grad_arrived = lax.all_to_all(grad_slots, "expert", split_axis=0, concat_axis=0, tiled=True)
        grad_post = jnp.einsum(
            "sjcd,jfd->sjcf", grad_arrived, w_expert_out, preferred_element_type=jnp.float32
        )
        out_sum = out_sum + jnp.einsum(
            "sjcf,sjcd->jfd", post_act, grad_arrived, preferred_element_type=jnp.float32
        )
        grad_pre = jax.vjp(jax.nn.gelu, pre_act)[1](grad_post)[0].astype(jnp.bfloat16)
        in_sum = in_sum + jnp.einsum(
            "sjcd,sjcf->jdf", arrived, grad_pre, preferred_element_type=jnp.float32
        )
        grad_rows = jnp.einsum(
            "sjcf,jdf->sjcd", grad_pre, w_expert_in, preferred_element_type=jnp.float32
        ).astype(jnp.bfloat16)
        grad_back = lax.all_to_all(
            grad_rows, "expert", split_axis=0, concat_axis=0, tiled=True
        ).reshape(expert_count * capacity, D)
        grad_moe = jnp.einsum(
            "st,sd->td", place_both, grad_back, preferred_element_type=jnp.float32
        )
        weighted = dgate_first * gate_first + dgate_second * gate_second
        grad_pick = ((dgate_first - weighted) / denom)[:, None] * pick_first + (
            (dgate_second - weighted) / denom
        )[:, None] * pick_second
        grad_logits = router_probs * (
            grad_pick - jnp.sum(router_probs * grad_pick, axis=-1, keepdims=True)
        )
        normed_mf = normed_mb.astype(jnp.float32)
        grad_router_w = jnp.dot(normed_mf.T, grad_logits, precision=TOP_PRECISION)
        grad_moe = grad_moe + jnp.dot(
            grad_logits, router_w.astype(jnp.float32).T, precision=TOP_PRECISION
        )
        grad_resid_norm, grad_gain_m = norm_backward(grad_moe, scaled_m, inverse_m, gain_mf)
        grad_resid = grad_top + grad_resid_norm
        grad_branch = grad_resid.astype(jnp.bfloat16)
        grad_output_w = jnp.einsum(
            "td,te->de", attended, grad_branch, preferred_element_type=jnp.float32
        )
        grad_attended = jnp.einsum(
            "te,de->td", grad_branch, output_w, preferred_element_type=jnp.float32
        ).astype(jnp.bfloat16)
        grad_heads = split_heads(grad_attended, heads)
        scores_again = score_block(q_heads, k_heads, bias, allowed, scale)
        probs_again = jnp.exp(scores_again - log_total)
        probs_again_b = probs_again.astype(jnp.bfloat16)
        grad_probs = jnp.einsum(
            "hqd,hkd->hqk", grad_heads, v_heads, preferred_element_type=jnp.float32
        )
        row_delta = jnp.sum(probs_again * grad_probs, axis=-1, keepdims=True)
        grad_scores = probs_again * (grad_probs - row_delta)
        grad_table = jnp.einsum(
            "hqk,qkb->bh", grad_scores, bucket_onehot.astype(jnp.float32), precision=TOP_PRECISION
        )
        grad_scores_b = (grad_scores * scale).astype(jnp.bfloat16)
        grad_q_heads = jnp.einsum(
            "hqk,hkd->hqd", grad_scores_b, k_heads, preferred_element_type=jnp.float32
        )
        grad_v_heads = jnp.einsum(
            "hqk,hqd->hkd", probs_again_b, grad_heads, preferred_element_type=jnp.float32
        )
        grad_k_heads = jnp.einsum(
            "hqk,hqd->hkd", grad_scores_b, q_heads, preferred_element_type=jnp.float32
        )
        grad_keys, grad_values = (
            lax.psum_scatter(merge_heads(grad_k_heads), "expert", scatter_dimension=0, tiled=True),
            lax.psum_scatter(merge_heads(grad_v_heads), "expert", scatter_dimension=0, tiled=True),
        )
        grad_queries_b = merge_heads(grad_q_heads).astype(jnp.bfloat16)
        grad_keys_b = grad_keys.astype(jnp.bfloat16)
        grad_values_b = grad_values.astype(jnp.bfloat16)
        grad_query_w = jnp.einsum(
            "td,te->de", normed_ab, grad_queries_b, preferred_element_type=jnp.float32
        )
        grad_key_w = jnp.einsum(
            "td,te->de", normed_ab, grad_keys_b, preferred_element_type=jnp.float32
        )
        grad_value_w = jnp.einsum(
            "td,te->de", normed_ab, grad_values_b, preferred_element_type=jnp.float32
        )
        grad_normed = (
            jnp.einsum("te,de->td", grad_queries_b, query_w, preferred_element_type=jnp.float32)
            + jnp.einsum("te,de->td", grad_keys_b, key_w, preferred_element_type=jnp.float32)
            + jnp.einsum("te,de->td", grad_values_b, value_w, preferred_element_type=jnp.float32)
        )
        grad_in_norm, grad_gain_a = norm_backward(grad_normed, scaled_a, inverse_a, gain_af)
        grads_list.append(grad_resid + grad_in_norm)
        parts_now = (
            grad_gain_a,
            grad_query_w,
            grad_key_w,
            grad_value_w,
            grad_output_w,
            grad_gain_m,
            grad_router_w,
            grad_table,
        )
        dense_sums = [running + addend for running, addend in zip(dense_sums, parts_now)]
    sum_gain_a, sum_query, sum_key, sum_value, sum_output, sum_gain_m, sum_router, sum_table = (
        dense_sums
    )
    summed = lax.psum(
        (sum_gain_a, sum_query, sum_key, sum_value, sum_output, sum_gain_m, sum_router, sum_table),
        "expert",
    )
    (
        full_gain_a,
        full_query,
        full_key,
        full_value,
        full_output,
        full_gain_m,
        full_router,
        full_table,
    ) = summed
    shares = (
        lax.psum_scatter(full_gain_a, "dp", scatter_dimension=0, tiled=True),
        lax.psum_scatter(full_query, "dp", scatter_dimension=0, tiled=True),
        lax.psum_scatter(full_key, "dp", scatter_dimension=0, tiled=True),
        lax.psum_scatter(full_value, "dp", scatter_dimension=0, tiled=True),
        lax.psum_scatter(full_output, "dp", scatter_dimension=0, tiled=True),
        lax.psum_scatter(full_gain_m, "dp", scatter_dimension=0, tiled=True),
        lax.psum_scatter(full_router, "dp", scatter_dimension=0, tiled=True),
        lax.psum_scatter(full_table, "dp", scatter_dimension=0, tiled=True),
    )
    expert_in_grad, expert_out_grad = (
        lax.psum(in_sum.astype(jnp.bfloat16), "dp").astype(jnp.float32),
        lax.psum(out_sum.astype(jnp.bfloat16), "dp").astype(jnp.float32),
    )
    layer_out = jnp.stack(outputs_list)
    grad_in = jnp.stack(grads_list)
    return (
        layer_out,
        grad_in,
        shares[0],
        shares[1],
        shares[2],
        shares[3],
        shares[4],
        shares[5],
        shares[6],
        shares[7],
        expert_in_grad,
        expert_out_grad,
    )


F32 = jnp.float32
BF16 = jnp.bfloat16
TILE = 256
VMEM_LIMIT = 60 * 2**20


def nn(left, right):
    return lax.dot_general(left, right, (((1,), (0,)), ((), ())), preferred_element_type=F32)


def nt(left, right):
    return lax.dot_general(left, right, (((1,), (1,)), ((), ())), preferred_element_type=F32)


def tn(left, right):
    return lax.dot_general(left, right, (((0,), (0,)), ((), ())), preferred_element_type=F32)


def call(body, name, grid, ins, outs, out_shapes, scratch=(), flops=0, nbytes=0, collective=None):
    extra = {} if collective is None else {"collective_id": collective, "has_side_effects": True}
    return pl.pallas_call(
        body,
        grid=grid,
        in_specs=ins,
        out_specs=outs,
        out_shape=out_shapes,
        scratch_shapes=list(scratch),
        compiler_params=pltpu.CompilerParams(
            dimension_semantics=("arbitrary",) * len(grid), vmem_limit_bytes=VMEM_LIMIT, **extra
        ),
        cost_estimate=pl.CostEstimate(flops=flops, bytes_accessed=nbytes, transcendentals=0),
        name=name,
    )


def whole(shape):
    zeros = (0,) * len(shape)
    return pl.BlockSpec(shape, lambda *_: zeros)


def rows(width, tile=TILE):
    return pl.BlockSpec((tile, width), lambda i: (i, 0))


MESH = pl.DeviceIdType.MESH
ANY = pl.BlockSpec(memory_space=pl.ANY)


def neighbours():
    me = lax.axis_index("dp")
    core = me + 1 - 2 * (me % 2)
    along_x = me + 2 - 4 * ((me // 2) % 2)
    along_y = me + 4 - 8 * (me // 4)
    across = along_x + 4 - 8 * (me // 4)
    return me, core, along_x, along_y, across


def meet(devices):
    barrier = pltpu.get_barrier_semaphore()
    for device in devices:
        pl.semaphore_signal(barrier, inc=1, device_id=device, device_id_type=MESH)
    pl.semaphore_wait(barrier, len(devices))


def plane_devices():
    place = lax.axis_index("expert")
    _, core, along_x, along_y, _ = neighbours()
    return [(core, place), (along_x, place), (along_y, place)]


GATHER_COPIES = 14


def gather_copies(first, second, source_first, source_second, send, recv, local):
    place = lax.axis_index("expert")
    me, core, along_x, along_y, across = neighbours()

    def remote(index, source, target, device):
        return pltpu.make_async_remote_copy(
            src_ref=source,
            dst_ref=target,
            send_sem=send.at[index],
            recv_sem=recv.at[index],
            device_id=(device, place),
            device_id_type=MESH,
        )

    own = [
        pltpu.make_async_copy(source_first, first.at[me], local.at[0]),
        pltpu.make_async_copy(source_second, second.at[me], local.at[1]),
    ]
    stage0 = [
        remote(0, source_first, first.at[me], along_x),
        remote(1, source_second, second.at[me], along_y),
        remote(2, source_first, first.at[me], core),
        remote(3, source_second, second.at[me], core),
    ]
    stage1 = [
        remote(4, first.at[along_x], first.at[along_x], along_y),
        remote(5, second.at[along_y], second.at[along_y], along_x),
        remote(6, source_first, first.at[me], along_y),
        remote(7, source_second, second.at[me], along_x),
        remote(8, first.at[along_x], first.at[along_x], core),
        remote(9, second.at[along_y], second.at[along_y], core),
    ]
    stage2 = [
        remote(10, first.at[along_y], first.at[along_y], core),
        remote(11, second.at[along_x], second.at[along_x], core),
        remote(12, first.at[across], first.at[across], core),
        remote(13, second.at[across], second.at[across], core),
    ]

    def start0():
        for copy in stage0 + own:
            copy.start()

    def start1():
        stage0[0].wait_recv()
        stage0[1].wait_recv()
        for copy in stage1:
            copy.start()

    def start2():
        for copy in stage1[:4]:
            copy.wait_recv()
        for copy in stage2:
            copy.start()

    def finish():
        for copy in own:
            copy.wait()
        for copy in stage0[2:] + stage1[4:] + stage2:
            copy.wait_recv()
        for copy in stage0 + stage1 + stage2:
            copy.wait_send()

    return start0, start1, start2, finish


def gather_sems():
    return [
        pltpu.SemaphoreType.DMA((GATHER_COPIES,)),
        pltpu.SemaphoreType.DMA((GATHER_COPIES,)),
        pltpu.SemaphoreType.DMA((2,)),
    ]


def sds(shape, dtype):
    return jax.ShapeDtypeStruct(shape, dtype)


def place_devices(group):
    me = lax.axis_index("dp")
    place = lax.axis_index("expert")
    return [(me, lax.rem(place + k, group)) for k in range(1, group)]


def along_axis(source, target, send, recv, place):
    return pltpu.make_async_remote_copy(
        src_ref=source,
        dst_ref=target,
        send_sem=send,
        recv_sem=recv,
        device_id=(lax.axis_index("dp"), place),
        device_id_type=MESH,
    )


def swap_copies(source, target, send, recv, group):
    place = lax.axis_index("expert")
    copies = []
    for k in range(1, group):
        other = lax.rem(place + k, group)
        copies.append(along_axis(source.at[other], target.at[place], send.at[k], recv.at[k], other))
    return copies


def slice_copies(w_in, w_out, target, send, recv, base, place):
    me = lax.axis_index("dp")
    chunk = target.shape[2]
    rows_in = w_in.at[0, :, pl.ds(pl.multiple_of(me * chunk, 128), chunk)]
    rows_out = pl.ds(pl.multiple_of(me * chunk, 128), chunk)
    pieces = (
        (rows_in, target.at[0]),
        (w_out.at[0, rows_out, pl.ds(0, chunk)], target.at[1, pl.ds(0, chunk)]),
        (w_out.at[0, rows_out, pl.ds(chunk, chunk)], target.at[1, pl.ds(chunk, chunk)]),
    )
    return [
        along_axis(source, goal, send.at[base + i], recv.at[base + i], place)
        for i, (source, goal) in enumerate(pieces)
    ]


REDUCE_COPIES = 10


def reduce_copies(terms, own, pair, inbox, send, recv, local, emit):
    place = lax.axis_index("expert")
    me, core, along_x, along_y, across = neighbours()
    targets = (across, along_x, along_y, me)

    def remote(index, source, target, device):
        return pltpu.make_async_remote_copy(
            src_ref=source,
            dst_ref=target,
            send_sem=send.at[index],
            recv_sem=recv.at[index],
            device_id=(device, place),
            device_id_type=MESH,
        )

    loads = [pltpu.make_async_copy(terms.at[t], own.at[q], local.at[q]) for q, t in enumerate(targets)]
    pairs = [
        remote(q, terms.at[t + 1 - 2 * lax.rem(t, 2)], pair.at[q], core) for q, t in enumerate(targets)
    ]
    far_first = remote(4, own.at[0, 0], inbox.at[0], along_x)
    far_second = remote(5, own.at[0, 1], inbox.at[1], along_y)
    near_first = remote(6, own.at[1, 0], inbox.at[2], along_x)
    near_second = remote(7, own.at[2, 1], inbox.at[3], along_y)
    late_first = remote(8, own.at[2, 0], inbox.at[4], along_y)
    late_second = remote(9, own.at[1, 1], inbox.at[5], along_x)

    def merge(q):
        loads[q].wait()
        pairs[q].wait_recv()
        own[q] = own[q] + pair[q]

    def start():
        for copy in loads + pairs:
            copy.start()

    def far():
        merge(0)
        far_first.start()
        far_second.start()

    def near():
        merge(1)
        near_first.start()
        merge(2)
        near_second.start()

    def late():
        far_first.wait_recv()
        own[2, 0] = own[2, 0] + inbox[0]
        late_first.start()
        far_second.wait_recv()
        own[1, 1] = own[1, 1] + inbox[1]
        late_second.start()

    def finish():
        merge(3)
        for copy in (near_first, near_second, late_first, late_second):
            copy.wait_recv()
        emit(0, own[3, 0].astype(F32) + inbox[2].astype(F32) + inbox[4].astype(F32))
        emit(1, own[3, 1].astype(F32) + inbox[3].astype(F32) + inbox[5].astype(F32))
        for copy in pairs + [far_first, far_second, near_first, near_second, late_first, late_second]:
            copy.wait_send()

    return start, far, near, late, finish


def reduce_scratch(shape):
    half = shape[1:]
    return [
        pltpu.VMEM((4, *shape), BF16),
        pltpu.VMEM((4, *shape), BF16),
        pltpu.VMEM((6, *half), BF16),
        pltpu.SemaphoreType.DMA((REDUCE_COPIES,)),
        pltpu.SemaphoreType.DMA((REDUCE_COPIES,)),
        pltpu.SemaphoreType.DMA((4,)),
    ]


def weight(slots_ref, index, share):
    return slots_ref[:, index * share : (index + 1) * share, :].reshape(-1, D)


def open_kernel(
    x_ref, routes_ref, w_in_ref, w_out_ref, wq_ref, wk_ref, wv_ref, wo_ref, small_ref, buckets_ref, seg_ref,
    x_out, piece_out, first_out, second_out, a_ref, q_ref, k_ref, v_ref, params_ref, line_ref, across_ref, down_ref,
    land, routes_land, first, second, stage_first, stage_second,
    x_send, x_recv, r_send, r_recv, p_send, p_recv, keep, own_local, send, recv, local,
    *, group, share, heads, experts, scale
):
    me = lax.axis_index("dp")
    place = lax.axis_index("expert")
    pieces = [
        (wq_ref, stage_first.at[pl.ds(0, share)]),
        (wk_ref, stage_first.at[pl.ds(share, share)]),
        (wv_ref, stage_second.at[pl.ds(0, share)]),
        (wo_ref, stage_second.at[pl.ds(share, share)]),
    ]
    staged = [pltpu.make_async_copy(src, dst, own_local.at[i]) for i, (src, dst) in enumerate(pieces)]
    for copy in staged:
        copy.start()
    small = small_ref[...].astype(F32)
    line = lax.broadcasted_iota(jnp.int32, small.shape, 0)
    placed = jnp.where(line < 16, pltpu.roll(small, me * share, 1), pltpu.roll(small, me * 4, 1))
    stage_second[2 * share :, :] = placed.astype(BF16)
    meet(plane_devices() + place_devices(group))
    moves = swap_copies(routes_ref, routes_land, r_send, r_recv, group)
    moves_x = swap_copies(x_ref, land, x_send, x_recv, group)
    slices = slice_copies(w_in_ref, w_out_ref, piece_out, p_send, p_recv, 0, lax.rem(place + group - 1, group))
    kept = [
        pltpu.make_async_copy(routes_ref.at[place], routes_land.at[place], keep.at[0]),
        pltpu.make_async_copy(x_ref.at[place], land.at[place], keep.at[1]),
    ]
    for copy in moves + moves_x + slices + kept:
        copy.start()
    for copy in staged:
        copy.wait()
    start0, start1, start2, finish = gather_copies(first, second, stage_first, stage_second, send, recv, local)
    start0()

    kept[0].wait()
    for copy in moves:
        copy.wait_recv()
    seq = down_ref.shape[0]
    row_id = lax.broadcasted_iota(jnp.int32, (8, routes_land.shape[2]), 0)
    named = []
    for p in range(group):
        picks = []
        for c in range(2):
            pick = routes_land[p, c : c + 1, :] - place
            picks.append(jnp.where(pick < 0, pick + experts, pick))
        named.append(((picks[0] == row_id) | (picks[1] == row_id)).astype(F32))
    named = jnp.concatenate(named, axis=1)
    earlier = lax.broadcasted_iota(jnp.int32, (seq, seq), 0) < lax.broadcasted_iota(jnp.int32, (seq, seq), 1)
    before = nn(named.astype(BF16), earlier.astype(F32).astype(BF16))
    pos = jnp.where(named > 0, before, -1.0)
    which = lax.broadcasted_iota(jnp.int32, seg_ref.shape, 0)
    segs = jnp.where(which == place, seg_ref[...], 0).astype(F32).sum(axis=0, keepdims=True)
    stack = jnp.concatenate([pos, jnp.broadcast_to(segs, (8, seq))], axis=0)
    across_ref[...] = stack.astype(jnp.int32)
    filled = jnp.concatenate([stack, jnp.full((112, seq), -1.0, F32)], axis=0)
    down_ref[...] = filled.T.astype(jnp.int32)

    start1()
    start2()
    finish()
    out_copies = [
        pltpu.make_async_copy(first, first_out, own_local.at[0]),
        pltpu.make_async_copy(second, second_out, own_local.at[1]),
    ]
    for copy in out_copies:
        copy.start()
    params = second[0, 2 * share :, :].astype(F32)
    for slot in range(1, second.shape[0]):
        params = params + second[slot, 2 * share :, :].astype(F32)
    turned = []
    for k in range(experts):
        wanted = lax.rem(place + k, experts)
        picked = jnp.zeros((1, D), F32)
        for e in range(experts):
            picked = picked + params[8 + e : 9 + e, :] * jnp.where(wanted == e, 1.0, 0.0)
        turned.append(picked)
    params_ref[...] = params
    for k in range(experts):
        params_ref[8 + k : 9 + k, :] = turned[k]
    hot = (lax.broadcasted_iota(jnp.int32, (128, seq), 0) == buckets_ref[...]).astype(F32).astype(BF16)
    lines = nn(params[16:32, :128].astype(BF16), hot)
    for h in range(heads):
        line_ref[h] = lines[h : h + 1, :]

    kept[1].wait()
    for copy in moves_x:
        copy.wait_recv()
    out_copies.append(pltpu.make_async_copy(land, x_out, own_local.at[2]))
    out_copies[-1].start()
    part = land.shape[1]
    for p in range(group):
        here = slice(p * part, (p + 1) * part)
        x = land[p].astype(F32)
        inverse = lax.rsqrt(jnp.mean(x * x, axis=-1, keepdims=True) + EPSILON)
        normed = (x * inverse * params[0:1, :]).astype(BF16)
        a_ref[here, :] = normed
        q = nn(normed, weight(first, 0, share)).astype(BF16)
        q_ref[here, :] = (q.astype(F32) * scale).astype(BF16)
        k_ref[here, :] = nn(normed, weight(first, 1, share)).astype(BF16)
        v_ref[here, :] = nn(normed, weight(second, 0, share)).astype(BF16)
    for copy in slices:
        copy.wait_recv()
    for copy in moves + moves_x + slices:
        copy.wait_send()
    for copy in out_copies:
        copy.wait()


def masked_scores(k, q, table_ref, head, i, j, seg_col, seg_row):
    scores = nt(k, q) + table_ref[head, i - j].astype(F32)
    allowed = seg_col == seg_row
    if i == j:
        key_at = lax.broadcasted_iota(jnp.int32, (TILE, TILE), 0)
        query_at = lax.broadcasted_iota(jnp.int32, (TILE, TILE), 1)
        allowed = allowed & (key_at <= query_at)
    return jnp.where(allowed, scores, MASKED)


def attend_kernel(
    q_ref, k_ref, v_ref, line_ref, down_ref, across_ref, source, grad_ref, w_in_ref, w_out_ref,
    o_ref, lse_ref, table_ref, grad_out, piece_out, gather_first, gather_second,
    g_send, g_recv, p_send, p_recv, keep, send, recv, local, *, width, group
):
    step = pl.program_id(0)
    last = pl.num_programs(0) - 1
    place = lax.axis_index("expert")
    start0, start1, start2, finish = gather_copies(
        gather_first, gather_second, source.at[0], source.at[1], send, recv, local
    )
    moves = swap_copies(grad_ref, grad_out, g_send, g_recv, group)
    slices = slice_copies(w_in_ref, w_out_ref, piece_out, p_send, p_recv, 0, lax.rem(place + 1, group))
    kept = pltpu.make_async_copy(grad_ref.at[place], grad_out.at[place], keep.at[0])

    @pl.when(step == 0)
    def _():
        meet(plane_devices() + place_devices(group))
        start0()
        for copy in moves + slices:
            copy.start()
        kept.start()

    @pl.when(step == 3)
    def _():
        start1()

    heads = q_ref.shape[1] // width
    for h in range(heads):
        row = line_ref[h]
        for gap in range(table_ref.shape[1]):
            ahead = row[:, gap * TILE : (gap + 1) * TILE]
            back = row[:, (gap - 1) * TILE : gap * TILE] if gap else jnp.zeros_like(ahead)
            grid = jnp.broadcast_to(jnp.concatenate([ahead, back], axis=1), (TILE, 2 * TILE))
            grid = pltpu.roll(grid, 0, 1, stride=1, stride_axis=0)
            table_ref[h, gap] = grid[:, :TILE].astype(BF16)

    blocks = q_ref.shape[0] // TILE
    turned = [v_ref[:, h * width : (h + 1) * width].T for h in range(heads)]
    for i in range(blocks):
        here = slice(i * TILE, (i + 1) * TILE)
        outs = []
        for h in range(heads):
            lanes = slice(h * width, (h + 1) * width)
            q = q_ref[here, lanes]
            pieces = []
            for j in range(i + 1):
                there = slice(j * TILE, (j + 1) * TILE)
                pieces.append(
                    masked_scores(
                        k_ref[there, lanes], q, table_ref, h, i, j, down_ref[there, 8:9], across_ref[8:9, here]
                    )
                )
            top = pieces[0].max(axis=0, keepdims=True)
            for piece in pieces[1:]:
                top = jnp.maximum(top, piece.max(axis=0, keepdims=True))
            total = jnp.zeros_like(top)
            acc = jnp.zeros((width, TILE), F32)
            for j, piece in enumerate(pieces):
                lifted = jnp.exp(piece - top)
                total = total + lifted.sum(axis=0, keepdims=True)
                acc = acc + nn(turned[h][:, j * TILE : (j + 1) * TILE], lifted.astype(BF16))
            outs.append(acc / total)
            lse_ref[0, h : h + 1, here] = top + jnp.log(total)
        o_ref[here, :] = jnp.concatenate(outs, axis=0).T.astype(BF16)

    @pl.when(step == last)
    def _():
        start2()
        kept.wait()
        for copy in moves + slices:
            copy.wait_recv()
        for copy in moves + slices:
            copy.wait_send()
        finish()


def attend_back_kernel(
    q_ref, k_ref, v_ref, do_ref, table_ref, down_ref, across_ref, lse_ref, result_ref, terms,
    dq_ref, dk_ref, dv_ref, dist_ref, sums_ref, result_out, sum_ref, dk_sum, dv_sum,
    o_send, o_recv, keep, own, pair, inbox, send, recv, local, *, width, scale, group
):
    step = pl.program_id(0)
    last = pl.num_programs(0) - 1
    place = lax.axis_index("expert")

    def emit(half, value):
        sums_ref[half] = value.astype(BF16)

    start, far, near, late, finish = reduce_copies(terms, own, pair, inbox, send, recv, local, emit)
    moves = swap_copies(result_ref, result_out, o_send, o_recv, group)
    kept = pltpu.make_async_copy(result_ref.at[place], result_out.at[place], keep.at[0])

    @pl.when(step == 0)
    def _():
        meet(plane_devices() + place_devices(group))
        start()
        for copy in moves:
            copy.start()
        kept.start()

    @pl.when(step == 1)
    def _():
        far()
        near()

    @pl.when(step == 5)
    def _():
        late()

    blocks = q_ref.shape[0] // TILE
    heads = q_ref.shape[1] // width
    turned = [k_ref[:, h * width : (h + 1) * width].T for h in range(heads)]
    dist_ref[...] = jnp.zeros_like(dist_ref)
    for h in range(heads):
        lanes = slice(h * width, (h + 1) * width)
        for i in range(blocks):
            here = slice(i * TILE, (i + 1) * TILE)
            q = q_ref[here, lanes]
            do = do_ref[here, lanes]
            lse = lse_ref[0, h : h + 1, here]
            probs, dprobs = [], []
            delta = jnp.zeros((1, TILE), F32)
            for j in range(i + 1):
                there = slice(j * TILE, (j + 1) * TILE)
                scores = masked_scores(
                    k_ref[there, lanes], q, table_ref, h, i, j, down_ref[there, 8:9], across_ref[8:9, here]
                )
                p = jnp.exp(scores - lse)
                dp = nt(v_ref[there, lanes], do)
                delta = delta + (p * dp).sum(axis=0, keepdims=True)
                probs.append(p)
                dprobs.append(dp)
            turned_dq = jnp.zeros((width, TILE), F32)
            for j in range(i + 1):
                there = slice(j * TILE, (j + 1) * TILE)
                ds = probs[j] * (dprobs[j] - delta)
                low = ds.astype(BF16)
                dv = nn(probs[j].astype(BF16), do)
                dk = nn(low, q)
                if i == j:
                    dv_sum[there, lanes] = dv
                    dk_sum[there, lanes] = dk
                else:
                    dv_sum[there, lanes] += dv
                    dk_sum[there, lanes] += dk
                turned_dq = turned_dq + nn(turned[h][:, there], low)
                if j == 0:
                    sum_ref[i - j] = ds
                else:
                    sum_ref[i - j] += ds
            dq_ref[here, lanes] = (turned_dq * scale).T.astype(BF16)
        for gap in range(blocks):
            part = sum_ref[gap]
            part = jnp.concatenate([part, jnp.zeros_like(part)], axis=1)
            half = TILE // 2
            while half:
                part = part[:half] + pltpu.roll(part[half : 2 * half], 2 * TILE - half, 1)
                half //= 2
            dist_ref[0, h : h + 1, gap * TILE : (gap + 1) * TILE] += part[:, :TILE]
            if gap:
                dist_ref[0, h : h + 1, (gap - 1) * TILE : gap * TILE] += part[:, TILE:]
    dk_ref[...] = dk_sum[...].astype(BF16)
    dv_ref[...] = dv_sum[...].astype(BF16)

    @pl.when(step == last)
    def _():
        kept.wait()
        for copy in moves:
            copy.wait_recv()
        for copy in moves:
            copy.wait_send()
        finish()


def route_kernel(
    x_ref, o_ref, second_ref, params_ref, down_ref, h_ref, a_ref, gate_ref, pr_ref, *, share, experts
):
    h1 = x_ref[...].astype(F32) + nn(o_ref[...], weight(second_ref, 1, share))
    h_ref[...] = h1
    inverse = lax.rsqrt(jnp.mean(h1 * h1, axis=-1, keepdims=True) + EPSILON)
    normed = (h1 * inverse * params_ref[1:2, :]).astype(BF16)
    a_ref[...] = normed
    router = jnp.concatenate([params_ref[8:16, :], jnp.zeros((120, D), F32)], axis=0).astype(BF16)
    logits = nt(normed, router)
    lane = lax.broadcasted_iota(jnp.int32, logits.shape, 1)
    logits = jnp.where(lane < experts, logits, MASKED)
    lifted = jnp.exp(logits - logits.max(axis=-1, keepdims=True))
    pr = lifted / lifted.sum(axis=-1, keepdims=True)
    named = (down_ref[...] >= 0) & (lane < experts)
    picked = jnp.where(named, pr, 0.0)
    pr_ref[...] = pr
    gate_ref[...] = picked / picked.sum(axis=-1, keepdims=True)


def expert_kernel(a_ref, g_ref, gate_ref, across_ref, wi_ref, wo_ref, *refs, index, capacity, fetch, relay, reduce, pass_on, group):
    refs = list(refs)
    take = lambda count: [refs.pop(0) for _ in range(count)]
    source = take(1) if fetch else None
    relayed = take(2) if relay else None
    terms = take(1) if reduce else None
    passed = take(1) if pass_on else None
    eo_ref, da_ref, dw_ref = take(3)
    buffers = take(2) if fetch else None
    relay_out = take(1) if relay else None
    sums_ref = take(1)[0] if reduce else None
    pass_out = take(1) if pass_on else None
    rows_a, turned_a, rows_d, eo_sum, da_sum = take(5)
    step = pl.program_id(0)
    last = pl.num_programs(0) - 1
    place = lax.axis_index("expert")
    at_start, at_end = [], []
    at_step = {}
    if fetch:
        start0, start1, start2, finish = gather_copies(
            *buffers, source[0].at[0], source[0].at[1], *take(3)
        )
        at_start.append(start0)
        at_step[3] = [start1]
        at_end += [start2, finish]
    if relay:
        send, recv = take(2)
        down = along_axis(relayed[0], relay_out[0], send.at[0], recv.at[0], jnp.maximum(place - 1, 0))
        up = along_axis(relayed[1], relay_out[0], send.at[1], recv.at[0], jnp.minimum(place + 1, group - 1))
        middle = (place == 1) | (place == 2)

        def start_relay():
            @pl.when(middle)
            def _():
                down.start()
                up.start()

        def end_relay():
            down.wait_recv()

            @pl.when(middle)
            def _():
                down.wait_send()
                up.wait_send()

        at_start.append(start_relay)
        at_end.append(end_relay)
    if reduce:
        scratch = take(6)

        def emit(half, value):
            sums_ref[half] = value.astype(BF16)

        start, far, near, late, end_reduce = reduce_copies(terms[0], *scratch, emit)
        at_start.append(start)
        at_step[1] = [far]
        at_step[2] = [near]
        at_step[6 if fetch else 5] = [late]
        at_end.append(end_reduce)
    if pass_on:
        send, recv = take(2)
        hop = along_axis(passed[0], pass_out[0], send.at[0], recv.at[0], lax.rem(place + pass_on, group))
        at_start.append(hop.start)
        at_end.append(hop.wait)

    if at_start:
        @pl.when(step == 0)
        def _():
            far_devices = place_devices(group) if relay or pass_on else []
            near_devices = plane_devices() if fetch or reduce else []
            meet(near_devices + far_devices)
            for action in at_start:
                action()

    for when, actions in at_step.items():
        @pl.when(step == when)
        def _(actions=actions):
            for action in actions:
                action()

    @pl.when(step == 0)
    def _():
        tokens = a_ref.shape[0]
        slot = lax.broadcasted_iota(jnp.int32, (capacity, tokens), 0)
        pick = (across_ref[index : index + 1, :] == slot).astype(BF16)
        rows = nn(pick, a_ref[...]).astype(BF16)
        rows_a[...] = rows
        turned_a[...] = rows.T
        scaled = (gate_ref[:, index : index + 1] * g_ref[...].astype(F32)).astype(BF16)
        rows_d[...] = nn(pick, scaled).astype(BF16)
        eo_sum[...] = jnp.zeros_like(eo_sum)
        da_sum[...] = jnp.zeros_like(da_sum)

    d = rows_d[...]
    w_in = wi_ref[0]
    w_out = wo_ref[0]
    chunk = w_in.shape[1]
    if index:
        w_out = jnp.concatenate([w_out[:chunk], w_out[chunk:]], axis=1)
    u = nn(rows_a[...], w_in)
    square = u * u
    t = jnp.tanh(GELU_A * u * (1.0 + GELU_B * square))
    half = 0.5 * (1.0 + t)
    z = (u * half).astype(BF16)
    eo_sum[...] += nn(z, w_out)
    dw_out = tn(z, d).astype(BF16)
    dw_ref[0, 1, :chunk] = dw_out[:, :chunk]
    dw_ref[0, 1, chunk:] = dw_out[:, chunk:]
    slope = half + (0.5 * GELU_A) * u * (1.0 - t * t) * (1.0 + 3.0 * GELU_B * square)
    du = (nt(d, w_out) * slope).astype(BF16)
    da_sum[...] += nt(du, w_in)
    dw_ref[0, 0] = nn(turned_a[...], du).astype(BF16)

    @pl.when(step == last)
    def _():
        eo_ref[...] = eo_sum[...].astype(BF16)
        da_ref[...] = da_sum[...].astype(BF16)
        for action in at_end:
            action()


def combine_kernel(
    h_ref, a_ref, g_ref, o_ref, gate_ref, pr_ref, pos_ref, eo0, eo1, eo2, eo3,
    da0, da1, da2, da3, second_ref, params_ref,
    out_ref, dh_ref, do_ref, dw_ref, dgain_ref, drouter_ref, *, share, experts, capacity
):
    step = pl.program_id(0)

    @pl.when(step == 0)
    def _():
        dw_ref[...] = jnp.zeros_like(dw_ref)
        dgain_ref[...] = jnp.zeros_like(dgain_ref)
        drouter_ref[...] = jnp.zeros_like(drouter_ref)

    tile = h_ref.shape[0]
    h1 = h_ref[...]
    g = g_ref[...].astype(F32)
    gates = gate_ref[...]
    pr = pr_ref[...]
    lane = lax.broadcasted_iota(jnp.int32, pr.shape, 1)
    slot = lax.broadcasted_iota(jnp.int32, (tile, capacity), 1)
    result = h1
    dgate = jnp.zeros_like(pr)
    da = jnp.zeros_like(h1)
    for k, (eo, back) in enumerate(((eo0, da0), (eo1, da1), (eo2, da2), (eo3, da3))):
        spot = (pos_ref[:, k : k + 1] == slot).astype(BF16)
        got = nn(spot, eo[...])
        result = result + gates[:, k : k + 1] * got
        dgate = jnp.where(lane == k, jnp.sum(g * got, axis=-1, keepdims=True), dgate)
        da = da + nn(spot, back[...])
    out_ref[...] = result.astype(BF16)
    named = (pos_ref[...] >= 0) & (lane < experts)
    denom = jnp.sum(jnp.where(named, pr, 0.0), axis=-1, keepdims=True)
    weighted = jnp.sum(dgate * gates, axis=-1, keepdims=True)
    dpr = jnp.where(named, (dgate - weighted) / denom, 0.0)
    dlog = pr * (dpr - jnp.sum(pr * dpr, axis=-1, keepdims=True))
    high = dlog.astype(BF16)
    lost = (dlog - high.astype(F32)).astype(BF16)
    a = a_ref[...]
    drouter_ref[...] += (tn(high, a) + tn(lost, a))[: drouter_ref.shape[0]]
    for k in range(experts):
        da = da + dlog[:, k : k + 1] * params_ref[8 + k : 9 + k, :]
    inverse = lax.rsqrt(jnp.mean(h1 * h1, axis=-1, keepdims=True) + EPSILON)
    n2 = h1 * inverse
    dgain_ref[...] += jnp.sum(da * n2, axis=0, keepdims=True)
    dn = da * params_ref[1:2, :]
    dh = g + inverse * (dn - n2 * jnp.mean(dn * n2, axis=-1, keepdims=True))
    dh_ref[...] = dh
    dy = dh.astype(BF16)
    do_ref[...] = nt(dy, weight(second_ref, 1, share)).astype(BF16)
    dw_ref[...] += tn(o_ref[...], dy)


def close_kernel(
    x_ref, a_ref, dq_ref, dk_ref, dv_ref, dh_ref, first_ref, second_ref, params_ref, dwo_ref, dgain_m_ref, drouter_ref,
    dist_ref, buckets_ref, sum0, sum1, sum2, sum3,
    din_out, gather_first, gather_second, dense_ref,
    sum_ref, dgain, stage, total, pack, own, pair, inbox, r_send, r_recv, r_local, sends, recvs, keep,
    z_in, z_total, z_final, z_send, z_recv, g_send, g_recv, g_local, *, share, group, experts
):
    step = pl.program_id(0)
    last = pl.num_programs(0) - 1
    me = lax.axis_index("dp")
    place = lax.axis_index("expert")
    start0, start1, start2, finish = gather_copies(
        gather_first, gather_second, total.at[0], total.at[1], g_send, g_recv, g_local
    )
    tile = a_ref.shape[0]

    def din_copy(p):
        return along_axis(stage.at[p], din_out.at[place], sends.at[p], recvs.at[place], p)

    def din_keep(p):
        return pltpu.make_async_copy(stage.at[p], din_out.at[p], keep.at[0])

    @pl.when(step == 0)
    def _():
        for half in range(2):
            value = sum0[half].astype(F32) + sum1[half].astype(F32)
            total[half] = (value + sum2[half].astype(F32) + sum3[half].astype(F32)).astype(BF16)
        meet(plane_devices() + place_devices(group))
        start0()
        sum_ref[...] = jnp.zeros_like(sum_ref)
        dgain[...] = jnp.zeros_like(dgain)

    a = a_ref[...]
    da = jnp.zeros(dh_ref.shape, F32)
    places = ((first_ref, 0), (first_ref, 1), (second_ref, 0))
    for index, grad_ref in enumerate((dq_ref, dk_ref, dv_ref)):
        grad = grad_ref[...]
        sum_ref[index] += tn(a, grad)
        slots_ref, at = places[index]
        da = da + nt(grad, weight(slots_ref, at, share))
    x = x_ref[...].astype(F32)
    inverse = lax.rsqrt(jnp.mean(x * x, axis=-1, keepdims=True) + EPSILON)
    n1 = x * inverse
    dgain[...] += jnp.sum(da * n1, axis=0, keepdims=True)
    dn = da * params_ref[0:1, :]
    din = dh_ref[...] + inverse * (dn - n1 * jnp.mean(dn * n1, axis=-1, keepdims=True))
    for p in range(group):
        @pl.when(step == p)
        def _(p=p):
            stage[p] = din.astype(BF16)

            @pl.when(place == p)
            def _():
                din_keep(p).start()

            @pl.when(place != p)
            def _():
                din_copy(p).start()

    @pl.when(step == last)
    def _():
        start1()
        for index in range(2):
            pack[:, 0, index * share : (index + 1) * share, :] = sum_ref[index].astype(BF16).reshape(-1, share, D)
        pack[:, 1, :share, :] = sum_ref[2].astype(BF16).reshape(-1, share, D)
        pack[:, 1, share : 2 * share, :] = dwo_ref[...].astype(BF16).reshape(-1, share, D)
        seq = dist_ref.shape[1]
        hot = (lax.broadcasted_iota(jnp.int32, (128, seq), 0) == buckets_ref[...]).astype(F32).astype(BF16)
        left = dist_ref[...]
        table = jnp.zeros((left.shape[0], 128), F32)
        for _ in range(3):
            part = left.astype(BF16)
            left = left - part.astype(F32)
            table = table + nt(part, hot)
        rows_out = [dgain[...], dgain_m_ref[...], jnp.zeros((6, D), F32)]
        for e in range(experts):
            picked = jnp.zeros((1, D), F32)
            for k in range(experts):
                picked = picked + drouter_ref[k : k + 1, :] * jnp.where(lax.rem(place + k, experts) == e, 1.0, 0.0)
            rows_out.append(picked)
        rows_out.append(jnp.zeros((8 - experts, D), F32))
        rows_out.append(jnp.concatenate([table, jnp.zeros((table.shape[0], D - 128), F32)], axis=1))
        rows_out.append(jnp.zeros((16 - table.shape[0], D), F32))
        small = jnp.concatenate(rows_out, axis=0).astype(BF16)
        for slot in range(pack.shape[0]):
            pack[slot, 0, 2 * share :, :] = small
            pack[slot, 1, 2 * share :, :] = jnp.zeros_like(small)
        quarter = pack.shape[2] // 2

        def emit(half, value):
            low = value.astype(BF16)
            z_total[2 * half] = low[:quarter]
            z_total[2 * half + 1] = low[quarter:]

        start, far, near, late, end_reduce = reduce_copies(pack, own, pair, inbox, r_send, r_recv, r_local, emit)
        start()
        far()
        near()
        start2()
        late()
        end_reduce()
        spread = [
            along_axis(z_total.at[lax.rem(place + k, group)], z_in.at[k - 1], z_send.at[k], z_recv.at[k],
                       lax.rem(place + k, group))
            for k in range(1, group)
        ]
        for copy in spread:
            copy.start()
        for copy in spread:
            copy.wait_recv()
        value = z_total[place].astype(F32)
        for k in range(group - 1):
            value = value + z_in[k].astype(F32)
        z_final[place] = value.astype(BF16)
        share_out = [
            along_axis(z_final.at[place], z_final.at[place], z_send.at[group + k], z_recv.at[group + k],
                       lax.rem(place + k, group))
            for k in range(1, group)
        ]
        for copy in share_out:
            copy.start()
        for copy in share_out:
            copy.wait_recv()
        for copy in spread + share_out:
            copy.wait_send()
        dense_ref[...] = z_final[...]
        for k in range(1, group):
            other = lax.rem(place + k, group)
            along_axis(stage.at[other], din_out.at[other], sends.at[other], recvs.at[other], other).wait_recv()
        for k in range(1, group):
            other = lax.rem(place + k, group)
            along_axis(stage.at[other], din_out.at[place], sends.at[other], recvs.at[place], other).wait_send()
        pltpu.make_async_copy(stage.at[place], din_out.at[place], keep.at[0]).wait()
        finish()


def unpack_kernel(first_ref, second_ref, in_ref, out_ref):
    chunk = first_ref.shape[2]
    in_ref[0] = first_ref[0].astype(F32)
    out_ref[0, :, :chunk] = second_ref[0, :chunk].astype(F32)
    out_ref[0, :, chunk:] = second_ref[0, chunk:].astype(F32)


def on_device_whole(
    layer_in, out_grad, routes, segments, buckets, gain_attn, w_query, w_key, w_value, w_output,
    gain_moe, router, rel_bias, w_expert_in, w_expert_out,
):
    group = lax.axis_size("expert")
    shards = lax.axis_size("dp")
    shard = lax.axis_index("dp")
    experts = router.shape[1]
    seq = segments.shape[1]
    heads = rel_bias.shape[1]
    width = D // heads
    scale = 1.0 / math.sqrt(width)
    share = D // shards
    ff = w_expert_in.shape[2]
    chunk = ff // shards
    blocks = seq // TILE
    part = seq // group
    capacity = 3 * seq // group
    pairs = 128 // width
    tokens = (seq, D)
    slots = (capacity, D)
    piece = (2, D, chunk)
    buffer = sds((shards, D, chunk), BF16)
    dma = pltpu.SemaphoreType.DMA
    vmem = pl.BlockSpec(memory_space=pltpu.VMEM)

    wide = lambda v, count: jnp.pad(v, ((0, count - v.shape[0]), (0, D - v.shape[1])))
    small = jnp.concatenate([
        wide(jnp.stack([gain_attn, gain_moe]), 8), wide(router.T, 8), wide(rel_bias.T, 16)])
    routes_in = jnp.pad(routes.transpose(0, 2, 1), ((0, 0), (0, 6), (0, 0)))
    bucket_row = buckets.reshape(1, seq)
    second_rows = 2 * share + 32
    x, moved, first, second, normed, q, k, v, params, lines, across, down = call(
        functools.partial(open_kernel, group=group, share=share, heads=heads, experts=experts, scale=scale),
        "open", (1,),
        [ANY] * 8 + [vmem] * 3,
        [ANY] * 4 + [vmem] * 8,
        [sds((group, part, D), BF16), sds(piece, BF16), sds((shards, 2 * share, D), BF16),
         sds((shards, second_rows, D), BF16)] + [sds(tokens, BF16)] * 4
        + [sds((32, D), F32), sds((heads, 1, seq), F32), sds((16, seq), jnp.int32), sds((seq, 128), jnp.int32)],
        [pltpu.VMEM((group, part, D), BF16), pltpu.VMEM((group, 8, part), jnp.int32),
         pltpu.VMEM((shards, 2 * share, D), BF16), pltpu.VMEM((shards, second_rows, D), BF16),
         pltpu.VMEM((2 * share, D), BF16), pltpu.VMEM((second_rows, D), BF16)]
        + [dma((group,))] * 4 + [dma((3,))] * 2 + [dma((2,)), dma((4,))] + gather_sems(), collective=1,
    )(layer_in, routes_in, w_expert_in, w_expert_out, w_query, w_key, w_value, w_output, small, bucket_row, segments)
    x = x.reshape(tokens)

    cols = pl.BlockSpec((seq, 128), lambda i: (0, i))
    table_spec = pl.BlockSpec((pairs, blocks, TILE, TILE), lambda i: (i, 0, 0, 0))
    lse_spec = pl.BlockSpec((1, pairs, seq), lambda i: (i, 0, 0))
    o, lse, table, g, moved3, *buffers = call(
        functools.partial(attend_kernel, width=width, group=group), "attend", (heads // pairs,),
        [cols, cols, cols, pl.BlockSpec((pairs, 1, seq), lambda i: (i, 0, 0)), whole((seq, 128)), whole((16, seq))]
        + [ANY] * 4,
        [cols, lse_spec, table_spec] + [ANY] * 4,
        [sds(tokens, BF16), sds((heads // pairs, pairs, seq), F32), sds((heads, blocks, TILE, TILE), BF16),
         sds((group, part, D), BF16), sds(piece, BF16), buffer, buffer],
        [dma((group,))] * 2 + [dma((3,))] * 2 + [dma((1,))] + gather_sems(),
        flops=8 * seq * seq * D, nbytes=16 * 2**20, collective=2,
    )(q, k, v, lines, down, across, moved, out_grad, w_expert_in, w_expert_out)
    g = g.reshape(tokens)
    h1, normed_m, gates, pr = call(
        functools.partial(route_kernel, share=share, experts=experts), "route", (blocks,),
        [rows(D), rows(D), whole(second.shape), whole((32, D)), rows(128)],
        [rows(D), rows(D), rows(128), rows(128)],
        [sds(tokens, F32), sds(tokens, BF16), sds((seq, 128), F32), sds((seq, 128), F32)],
        flops=2 * seq * D * D, nbytes=12 * 2**20,
    )(x, o, second, params, down)

    def run_expert(index, buffers, collective, fetch=None, relay=None, reduce=None, pass_on=None, hop=0):
        in_block, out_block = (1, D, chunk), (1, D, chunk)
        in_map = out_map = lambda i: (i, 0, 0)
        if index == 0:
            buffers = (w_expert_in, w_expert_out)
            out_block = (1, chunk, D)
            in_map, out_map = (lambda i: (0, 0, i)), (lambda i: (0, i, 0))
        extra_in, extra_out, shapes, scratch = [], [], [], []
        if fetch is not None:
            extra_in.append(fetch)
            extra_out += [ANY] * 2
            shapes += [buffer] * 2
            scratch += gather_sems()
        if relay is not None:
            extra_in += relay
            extra_out.append(ANY)
            shapes.append(sds(piece, BF16))
            scratch += [dma((2,)), dma((1,))]
        if reduce is not None:
            extra_in.append(reduce)
            extra_out.append(whole(piece))
            shapes.append(sds(piece, BF16))
            scratch += reduce_scratch(piece)
        if pass_on is not None:
            extra_in.append(pass_on)
            extra_out.append(ANY)
            shapes.append(sds(piece, BF16))
            scratch += [dma((1,)), dma((1,))]
        return call(
            functools.partial(
                expert_kernel, index=index, capacity=capacity, fetch=fetch is not None, relay=relay is not None,
                reduce=reduce is not None, pass_on=hop, group=group),
            f"expert{index}", (shards,),
            [whole(tokens), whole(tokens), whole((seq, 128)), whole((16, seq)),
             pl.BlockSpec(in_block, in_map), pl.BlockSpec(out_block, out_map)] + [ANY] * len(extra_in),
            [whole(slots), whole(slots), pl.BlockSpec((1, 2, D, chunk), lambda i: (i, 0, 0, 0))] + extra_out,
            [sds(slots, BF16), sds(slots, BF16), sds((shards, *piece), BF16)] + shapes,
            [pltpu.VMEM(slots, BF16), pltpu.VMEM((D, capacity), BF16), pltpu.VMEM(slots, BF16),
             pltpu.VMEM(slots, F32), pltpu.VMEM(slots, F32)] + scratch,
            flops=12 * capacity * D * ff, nbytes=24 * 2**20, collective=collective if extra_in else None,
        )(normed_m, g, gates, across, *buffers, *extra_in)

    eo1, da1, dw1, *rest = run_expert(1, buffers, 3, fetch=moved3, relay=[moved, moved3])
    buffers, moved2 = rest[:2], rest[2]
    eo3, da3, dw3, *rest = run_expert(3, buffers, 4, fetch=moved2, reduce=dw1)
    buffers, sum1 = rest[:2], rest[2]
    eo2, da2, dw2, sum3, sum1 = run_expert(2, buffers, 5, reduce=dw3, pass_on=sum1, hop=1)
    eo0, da0, dw0, sum2, sum3 = run_expert(0, None, 6, reduce=dw2, pass_on=sum3, hop=3)
    sum2 = lax.ppermute(sum2, "expert", [(s, (s + 2) % group) for s in range(group)])
    result, dh, do, grad_output, grad_gain_m, grad_router = call(
        functools.partial(combine_kernel, share=share, experts=experts, capacity=capacity), "combine",
        (blocks,),
        [rows(D)] * 4 + [rows(128)] * 3 + [whole(slots)] * 8 + [whole(second.shape), whole((32, D))],
        [rows(D), rows(D), rows(D), whole((D, D)), whole((1, D)), whole((8, D))],
        [sds(tokens, BF16), sds(tokens, F32), sds(tokens, BF16), sds((D, D), F32), sds((1, D), F32),
         sds((8, D), F32)],
        flops=24 * seq * D * D, nbytes=32 * 2**20,
    )(h1, normed_m, g, o, gates, pr, down, eo0, eo1, eo2, eo3, da0, da1, da2, da3, second, params)
    dq, dk, dv, dist, sum0, layer_out = call(
        functools.partial(attend_back_kernel, width=width, scale=scale, group=group), "attend_back",
        (heads // pairs,),
        [cols, cols, cols, cols, table_spec, whole((seq, 128)), whole((16, seq)), lse_spec, ANY, ANY],
        [cols, cols, cols, lse_spec, whole(piece), ANY],
        [sds(tokens, BF16)] * 3 + [sds((heads // pairs, pairs, seq), F32), sds(piece, BF16),
                                   sds((group, part, D), BF16)],
        [pltpu.VMEM((blocks, TILE, TILE), F32), pltpu.VMEM((seq, 128), F32), pltpu.VMEM((seq, 128), F32)]
        + [dma((group,))] * 2 + [dma((1,))] + reduce_scratch(piece),
        flops=20 * seq * seq * D, nbytes=24 * 2**20, collective=7,
    )(q, k, v, do, table, down, across, lse, result.reshape(group, part, D), dw0)
    dense_slot = (2, 2 * share + 32, D)
    quarter = (dense_slot[1] // 2, D)
    grad_in, *gathered, dense = call(
        functools.partial(close_kernel, share=share, group=group, experts=experts), "close", (blocks,),
        [rows(D)] * 6 + [whole(first.shape), whole(second.shape), whole((32, D)), whole((D, D)), whole((1, D)),
                         whole((8, D)), whole((heads, seq)), whole((1, seq))] + [whole(piece)] * 4,
        [ANY, ANY, ANY, whole((group, *quarter))],
        [sds((group, part, D), BF16), buffer, buffer, sds((group, *quarter), BF16)],
        [pltpu.VMEM((3, D, D), F32), pltpu.VMEM((1, D), F32), pltpu.VMEM((group, part, D), BF16),
         pltpu.VMEM(piece, BF16), pltpu.VMEM((shards, *dense_slot), BF16)] + reduce_scratch(dense_slot)
        + [dma((group,)), dma((group,)), dma((1,)), pltpu.VMEM((group - 1, *quarter), BF16),
           pltpu.VMEM((group, *quarter), BF16), pltpu.VMEM((group, *quarter), BF16), dma((2 * group,)), dma((2 * group,))] + gather_sems(),
        flops=12 * seq * D * D, nbytes=24 * 2**20, collective=8,
    )(x, normed, dq, dk, dv, dh, first, second, params, grad_output, grad_gain_m, grad_router,
      dist.reshape(heads, seq), bucket_row, sum0, sum1, sum2, sum3)
    spec = pl.BlockSpec((1, D, chunk), lambda i: (i, 0, 0))
    expert_in, expert_out = call(
        unpack_kernel, "unpack", (shards,), [spec, spec],
        [pl.BlockSpec((1, D, chunk), lambda i: (0, 0, i)), pl.BlockSpec((1, chunk, D), lambda i: (0, i, 0))],
        [sds(w_expert_in.shape, F32), sds(w_expert_out.shape, F32)], nbytes=28 * 2**20,
    )(*gathered)
    dense = dense.reshape(dense_slot).astype(F32)
    rest = dense[0, 2 * share :]
    line = lax.dynamic_slice_in_dim(rest[:16], shard * share, share, axis=1)
    grad_table = lax.dynamic_slice_in_dim(rest[16 : 16 + heads], shard * rel_bias.shape[0], rel_bias.shape[0], axis=1)
    return (
        layer_out,
        grad_in.astype(F32),
        line[0],
        dense[0, :share],
        dense[0, share : 2 * share],
        dense[1, :share],
        dense[1, share : 2 * share],
        line[1],
        line[8 : 8 + experts].T,
        grad_table.T,
        expert_in,
        expert_out,
    )


def solution(mesh):
    in_specs = (
        P(None, ("dp", "expert"), None),
        P(None, ("dp", "expert"), None),
        P(None, ("dp", "expert"), None),
        P(None, "dp"),
        P(),
        P("dp"),
        P("dp", None),
        P("dp", None),
        P("dp", None),
        P("dp", None),
        P("dp"),
        P("dp", None),
        P("dp", None),
        P("expert", None, None),
        P("expert", None, None),
    )
    out_specs = (
        P(None, ("dp", "expert"), None),
        P(None, ("dp", "expert"), None),
        P("dp"),
        P("dp", None),
        P("dp", None),
        P("dp", None),
        P("dp", None),
        P("dp"),
        P("dp", None),
        P("dp", None),
        P("expert", None, None),
        P("expert", None, None),
    )
    body = on_device_whole if mesh.shape["expert"] == MICRO else on_device
    return jax.shard_map(
        body, mesh=mesh, in_specs=in_specs, out_specs=out_specs, check_vma=False
    )
```

```python
import functools
import math

import jax
import jax.numpy as jnp
from jax import lax
from jax.experimental import pallas as pl
from jax.experimental.pallas import tpu as pltpu
from jax.sharding import PartitionSpec as P

D = 768
NB = 32
MICRO = 4


EPSILON = 1e-06
MASKED = -1e30
TOP_PRECISION = lax.Precision.HIGHEST
GELU_A = math.sqrt(2.0 / math.pi)
GELU_B = 0.044715


def norm_forward(values, gain):
    inverse = lax.rsqrt(jnp.mean(values * values, axis=-1, keepdims=True) + EPSILON)
    scaled = values * inverse
    return (scaled, inverse, scaled * gain)


def norm_backward(grad_top, scaled, inverse, gain):
    grad_scaled = grad_top * gain
    grad_values = inverse * (
        grad_scaled - scaled * jnp.mean(grad_scaled * scaled, axis=-1, keepdims=True)
    )
    return (grad_values, jnp.sum(grad_top * scaled, axis=0))


def split_heads(values, heads):
    return values.reshape(values.shape[0], heads, -1).transpose(1, 0, 2)


def merge_heads(values):
    return values.transpose(1, 0, 2).reshape(values.shape[1], -1)


def score_block(q_heads, k_heads, bias, allowed, scale):
    raw = jnp.einsum("hqd,hkd->hqk", q_heads, k_heads, preferred_element_type=jnp.float32)
    return jnp.where(allowed[None], raw * scale + bias, MASKED)


def bucket_table(distances, bucket_starts):
    lower = bucket_starts[:-1]
    upper = bucket_starts[1:]
    return (
        (distances[:, :, None] >= lower[None, None, :])
        & (distances[:, :, None] < upper[None, None, :])
    ).astype(jnp.bfloat16)


def on_device(
    layer_in,
    out_grad,
    routes,
    segments,
    buckets,
    gain_attn,
    w_query,
    w_key,
    w_value,
    w_output,
    gain_moe,
    router,
    rel_bias,
    w_expert_in,
    w_expert_out,
):
    tok_rows = layer_in.shape[1]
    seq_len = segments.shape[1]
    heads = rel_bias.shape[1]
    group_size = lax.axis_size("expert")
    rank_here = lax.axis_index("expert")
    expert_count = router.shape[1]
    local_experts = w_expert_in.shape[0]
    capacity = 3 * tok_rows // group_size
    scale = 1.0 / math.sqrt(D // heads)
    bucket_starts = jnp.sum(
        (buckets[None, :] < jnp.arange(NB + 1, dtype=jnp.int32)[:, None]).astype(jnp.int32), axis=1
    )
    query_pos = rank_here * tok_rows + jnp.arange(tok_rows, dtype=jnp.int32)
    key_pos = jnp.arange(seq_len, dtype=jnp.int32)
    offsets = jnp.maximum(query_pos[:, None] - key_pos[None, :], 0)
    bucket_onehot = bucket_table(offsets, bucket_starts)
    causal = query_pos[:, None] >= key_pos[None, :]
    slot_ids = jnp.arange(expert_count * capacity, dtype=jnp.int32)
    expert_ids = jnp.arange(expert_count, dtype=jnp.int32)
    pair_ids = jnp.arange(2 * tok_rows, dtype=jnp.int32)
    earlier = (pair_ids[None, :] < pair_ids[:, None]).astype(jnp.bfloat16)
    dense_sums = [
        jnp.zeros((D,), jnp.float32),
        jnp.zeros((D, D), jnp.float32),
        jnp.zeros((D, D), jnp.float32),
        jnp.zeros((D, D), jnp.float32),
        jnp.zeros((D, D), jnp.float32),
        jnp.zeros((D,), jnp.float32),
        jnp.zeros((D, expert_count), jnp.float32),
        jnp.zeros((NB, heads), jnp.float32),
    ]
    in_sum = jnp.zeros(w_expert_in.shape, jnp.float32)
    out_sum = jnp.zeros(w_expert_out.shape, jnp.float32)
    outputs_list = []
    grads_list = []
    for step_index in range(MICRO):
        weights_now = (
            lax.all_gather(gain_attn, "dp", axis=0, tiled=True),
            lax.all_gather(w_query, "dp", axis=0, tiled=True),
            lax.all_gather(w_key, "dp", axis=0, tiled=True),
            lax.all_gather(w_value, "dp", axis=0, tiled=True),
            lax.all_gather(w_output, "dp", axis=0, tiled=True),
            lax.all_gather(gain_moe, "dp", axis=0, tiled=True),
            lax.all_gather(router, "dp", axis=0, tiled=True),
            lax.all_gather(rel_bias, "dp", axis=0, tiled=True),
        )
        gain_a, query_w, key_w, value_w, output_w, gain_m, router_w, bias_table = weights_now
        gain_af = gain_a.astype(jnp.float32)
        gain_mf = gain_m.astype(jnp.float32)
        inputs = layer_in[step_index].astype(jnp.float32)
        scaled_a, inverse_a, normed_a = norm_forward(inputs, gain_af)
        normed_ab = normed_a.astype(jnp.bfloat16)
        queries = jnp.dot(normed_ab, query_w, preferred_element_type=jnp.float32).astype(
            jnp.bfloat16
        )
        keys_loc = jnp.dot(normed_ab, key_w, preferred_element_type=jnp.float32).astype(
            jnp.bfloat16
        )
        values_loc = jnp.dot(normed_ab, value_w, preferred_element_type=jnp.float32).astype(
            jnp.bfloat16
        )
        keys_all, values_all = (
            lax.all_gather(keys_loc, "expert", axis=0, tiled=True),
            lax.all_gather(values_loc, "expert", axis=0, tiled=True),
        )
        q_heads = split_heads(queries, heads)
        k_heads = split_heads(keys_all, heads)
        v_heads = split_heads(values_all, heads)
        bias = jnp.einsum(
            "qkb,bh->hqk", bucket_onehot, bias_table, preferred_element_type=jnp.float32
        )
        seg_all = segments[step_index]
        seg_here = lax.dynamic_slice_in_dim(seg_all, rank_here * tok_rows, tok_rows)
        allowed = causal & (seg_here[:, None] == seg_all[None, :])
        scores = score_block(q_heads, k_heads, bias, allowed, scale)
        top_score = jnp.max(scores, axis=-1, keepdims=True)
        lifted = jnp.exp(scores - top_score)
        total = jnp.sum(lifted, axis=-1, keepdims=True)
        log_total = top_score + jnp.log(total)
        probs_b = (lifted / total).astype(jnp.bfloat16)
        attended = merge_heads(
            jnp.einsum("hqk,hkd->hqd", probs_b, v_heads, preferred_element_type=jnp.float32)
        ).astype(jnp.bfloat16)
        resid = inputs + jnp.dot(attended, output_w, preferred_element_type=jnp.float32)
        scaled_m, inverse_m, normed_m = norm_forward(resid, gain_mf)
        normed_mb = normed_m.astype(jnp.bfloat16)
        logits = jnp.dot(normed_mb, router_w, preferred_element_type=jnp.float32)
        router_probs = jax.nn.softmax(logits, axis=-1)
        routes_now = routes[step_index]
        pick_first = (routes_now[:, 0:1] == expert_ids[None, :]).astype(jnp.float32)
        pick_second = (routes_now[:, 1:2] == expert_ids[None, :]).astype(jnp.float32)
        prob_first = jnp.sum(router_probs * pick_first, axis=-1)
        prob_second = jnp.sum(router_probs * pick_second, axis=-1)
        denom = prob_first + prob_second
        gate_first = prob_first / denom
        gate_second = prob_second / denom
        flat = routes_now.reshape(-1)
        flat_hot = (flat[:, None] == expert_ids[None, :]).astype(jnp.bfloat16)
        before = jnp.dot(earlier, flat_hot, preferred_element_type=jnp.float32)
        places = jnp.sum(before * flat_hot.astype(jnp.float32), axis=1).astype(jnp.int32)
        slot_pairs = (flat * capacity + places).reshape(tok_rows, 2)
        place_first = (slot_ids[:, None] == slot_pairs[None, :, 0]).astype(jnp.bfloat16)
        place_second = (slot_ids[:, None] == slot_pairs[None, :, 1]).astype(jnp.bfloat16)
        place_both = place_first + place_second
        outgoing = jnp.dot(place_both, normed_mb, preferred_element_type=jnp.float32).astype(
            jnp.bfloat16
        )
        outgoing = outgoing.reshape(group_size, local_experts, capacity, D)
        arrived_rows = lax.all_to_all(outgoing, "expert", split_axis=0, concat_axis=0, tiled=True)
        pre_act = jnp.einsum(
            "sjcd,jdf->sjcf", arrived_rows, w_expert_in, preferred_element_type=jnp.float32
        )
        post_act = jax.nn.gelu(pre_act).astype(jnp.bfloat16)
        produced = jnp.einsum(
            "sjcf,jfd->sjcd", post_act, w_expert_out, preferred_element_type=jnp.float32
        ).astype(jnp.bfloat16)
        produced, pre_act, post_act, arrived = (produced, pre_act, post_act, arrived_rows)
        returned = lax.all_to_all(
            produced, "expert", split_axis=0, concat_axis=0, tiled=True
        ).reshape(expert_count * capacity, D)
        got_first = jnp.einsum(
            "st,sd->td", place_first, returned, preferred_element_type=jnp.float32
        )
        got_second = jnp.einsum(
            "st,sd->td", place_second, returned, preferred_element_type=jnp.float32
        )
        result = resid + (gate_first[:, None] * got_first + gate_second[:, None] * got_second)
        outputs_list.append(result.astype(jnp.bfloat16))
        grad_top = out_grad[step_index].astype(jnp.float32)
        dgate_first = jnp.sum(grad_top * got_first, axis=-1)
        dgate_second = jnp.sum(grad_top * got_second, axis=-1)
        sent_first = (gate_first[:, None] * grad_top).astype(jnp.bfloat16)
        sent_second = (gate_second[:, None] * grad_top).astype(jnp.bfloat16)
        grad_slots = (
            jnp.dot(place_first, sent_first, preferred_element_type=jnp.float32)
            + jnp.dot(place_second, sent_second, preferred_element_type=jnp.float32)
        ).astype(jnp.bfloat16)
        grad_slots = grad_slots.reshape(group_size, local_experts, capacity, D)
        grad_arrived = lax.all_to_all(grad_slots, "expert", split_axis=0, concat_axis=0, tiled=True)
        grad_post = jnp.einsum(
            "sjcd,jfd->sjcf", grad_arrived, w_expert_out, preferred_element_type=jnp.float32
        )
        out_sum = out_sum + jnp.einsum(
            "sjcf,sjcd->jfd", post_act, grad_arrived, preferred_element_type=jnp.float32
        )
        grad_pre = jax.vjp(jax.nn.gelu, pre_act)[1](grad_post)[0].astype(jnp.bfloat16)
        in_sum = in_sum + jnp.einsum(
            "sjcd,sjcf->jdf", arrived, grad_pre, preferred_element_type=jnp.float32
        )
        grad_rows = jnp.einsum(
            "sjcf,jdf->sjcd", grad_pre, w_expert_in, preferred_element_type=jnp.float32
        ).astype(jnp.bfloat16)
        grad_back = lax.all_to_all(
            grad_rows, "expert", split_axis=0, concat_axis=0, tiled=True
        ).reshape(expert_count * capacity, D)
        grad_moe = jnp.einsum(
            "st,sd->td", place_both, grad_back, preferred_element_type=jnp.float32
        )
        weighted = dgate_first * gate_first + dgate_second * gate_second
        grad_pick = ((dgate_first - weighted) / denom)[:, None] * pick_first + (
            (dgate_second - weighted) / denom
        )[:, None] * pick_second
        grad_logits = router_probs * (
            grad_pick - jnp.sum(router_probs * grad_pick, axis=-1, keepdims=True)
        )
        normed_mf = normed_mb.astype(jnp.float32)
        grad_router_w = jnp.dot(normed_mf.T, grad_logits, precision=TOP_PRECISION)
        grad_moe = grad_moe + jnp.dot(
            grad_logits, router_w.astype(jnp.float32).T, precision=TOP_PRECISION
        )
        grad_resid_norm, grad_gain_m = norm_backward(grad_moe, scaled_m, inverse_m, gain_mf)
        grad_resid = grad_top + grad_resid_norm
        grad_branch = grad_resid.astype(jnp.bfloat16)
        grad_output_w = jnp.einsum(
            "td,te->de", attended, grad_branch, preferred_element_type=jnp.float32
        )
        grad_attended = jnp.einsum(
            "te,de->td", grad_branch, output_w, preferred_element_type=jnp.float32
        ).astype(jnp.bfloat16)
        grad_heads = split_heads(grad_attended, heads)
        scores_again = score_block(q_heads, k_heads, bias, allowed, scale)
        probs_again = jnp.exp(scores_again - log_total)
        probs_again_b = probs_again.astype(jnp.bfloat16)
        grad_probs = jnp.einsum(
            "hqd,hkd->hqk", grad_heads, v_heads, preferred_element_type=jnp.float32
        )
        row_delta = jnp.sum(probs_again * grad_probs, axis=-1, keepdims=True)
        grad_scores = probs_again * (grad_probs - row_delta)
        grad_table = jnp.einsum(
            "hqk,qkb->bh", grad_scores, bucket_onehot.astype(jnp.float32), precision=TOP_PRECISION
        )
        grad_scores_b = (grad_scores * scale).astype(jnp.bfloat16)
        grad_q_heads = jnp.einsum(
            "hqk,hkd->hqd", grad_scores_b, k_heads, preferred_element_type=jnp.float32
        )
        grad_v_heads = jnp.einsum(
            "hqk,hqd->hkd", probs_again_b, grad_heads, preferred_element_type=jnp.float32
        )
        grad_k_heads = jnp.einsum(
            "hqk,hqd->hkd", grad_scores_b, q_heads, preferred_element_type=jnp.float32
        )
        grad_keys, grad_values = (
            lax.psum_scatter(merge_heads(grad_k_heads), "expert", scatter_dimension=0, tiled=True),
            lax.psum_scatter(merge_heads(grad_v_heads), "expert", scatter_dimension=0, tiled=True),
        )
        grad_queries_b = merge_heads(grad_q_heads).astype(jnp.bfloat16)
        grad_keys_b = grad_keys.astype(jnp.bfloat16)
        grad_values_b = grad_values.astype(jnp.bfloat16)
        grad_query_w = jnp.einsum(
            "td,te->de", normed_ab, grad_queries_b, preferred_element_type=jnp.float32
        )
        grad_key_w = jnp.einsum(
            "td,te->de", normed_ab, grad_keys_b, preferred_element_type=jnp.float32
        )
        grad_value_w = jnp.einsum(
            "td,te->de", normed_ab, grad_values_b, preferred_element_type=jnp.float32
        )
        grad_normed = (
            jnp.einsum("te,de->td", grad_queries_b, query_w, preferred_element_type=jnp.float32)
            + jnp.einsum("te,de->td", grad_keys_b, key_w, preferred_element_type=jnp.float32)
            + jnp.einsum("te,de->td", grad_values_b, value_w, preferred_element_type=jnp.float32)
        )
        grad_in_norm, grad_gain_a = norm_backward(grad_normed, scaled_a, inverse_a, gain_af)
        grads_list.append(grad_resid + grad_in_norm)
        parts_now = (
            grad_gain_a,
            grad_query_w,
            grad_key_w,
            grad_value_w,
            grad_output_w,
            grad_gain_m,
            grad_router_w,
            grad_table,
        )
        dense_sums = [running + addend for running, addend in zip(dense_sums, parts_now)]
    sum_gain_a, sum_query, sum_key, sum_value, sum_output, sum_gain_m, sum_router, sum_table = (
        dense_sums
    )
    summed = lax.psum(
        (sum_gain_a, sum_query, sum_key, sum_value, sum_output, sum_gain_m, sum_router, sum_table),
        "expert",
    )
    (
        full_gain_a,
        full_query,
        full_key,
        full_value,
        full_output,
        full_gain_m,
        full_router,
        full_table,
    ) = summed
    shares = (
        lax.psum_scatter(full_gain_a, "dp", scatter_dimension=0, tiled=True),
        lax.psum_scatter(full_query, "dp", scatter_dimension=0, tiled=True),
        lax.psum_scatter(full_key, "dp", scatter_dimension=0, tiled=True),
        lax.psum_scatter(full_value, "dp", scatter_dimension=0, tiled=True),
        lax.psum_scatter(full_output, "dp", scatter_dimension=0, tiled=True),
        lax.psum_scatter(full_gain_m, "dp", scatter_dimension=0, tiled=True),
        lax.psum_scatter(full_router, "dp", scatter_dimension=0, tiled=True),
        lax.psum_scatter(full_table, "dp", scatter_dimension=0, tiled=True),
    )
    expert_in_grad, expert_out_grad = (
        lax.psum(in_sum.astype(jnp.bfloat16), "dp").astype(jnp.float32),
        lax.psum(out_sum.astype(jnp.bfloat16), "dp").astype(jnp.float32),
    )
    layer_out = jnp.stack(outputs_list)
    grad_in = jnp.stack(grads_list)
    return (
        layer_out,
        grad_in,
        shares[0],
        shares[1],
        shares[2],
        shares[3],
        shares[4],
        shares[5],
        shares[6],
        shares[7],
        expert_in_grad,
        expert_out_grad,
    )


F32 = jnp.float32
BF16 = jnp.bfloat16
TILE = 256
VMEM_LIMIT = 60 * 2**20


def nn(left, right):
    return lax.dot_general(left, right, (((1,), (0,)), ((), ())), preferred_element_type=F32)


def nt(left, right):
    return lax.dot_general(left, right, (((1,), (1,)), ((), ())), preferred_element_type=F32)


def tn(left, right):
    return lax.dot_general(left, right, (((0,), (0,)), ((), ())), preferred_element_type=F32)


def call(body, name, grid, ins, outs, out_shapes, scratch=(), flops=0, nbytes=0, collective=None):
    extra = {} if collective is None else {"collective_id": collective, "has_side_effects": True}
    return pl.pallas_call(
        body,
        grid=grid,
        in_specs=ins,
        out_specs=outs,
        out_shape=out_shapes,
        scratch_shapes=list(scratch),
        compiler_params=pltpu.CompilerParams(
            dimension_semantics=("arbitrary",) * len(grid), vmem_limit_bytes=VMEM_LIMIT, **extra
        ),
        cost_estimate=pl.CostEstimate(flops=flops, bytes_accessed=nbytes, transcendentals=0),
        name=name,
    )


def whole(shape):
    zeros = (0,) * len(shape)
    return pl.BlockSpec(shape, lambda *_: zeros)


def rows(width, tile=TILE):
    return pl.BlockSpec((tile, width), lambda i: (i, 0))


MESH = pl.DeviceIdType.MESH
ANY = pl.BlockSpec(memory_space=pl.ANY)


def neighbours():
    me = lax.axis_index("dp")
    core = me + 1 - 2 * (me % 2)
    along_x = me + 2 - 4 * ((me // 2) % 2)
    along_y = me + 4 - 8 * (me // 4)
    across = along_x + 4 - 8 * (me // 4)
    return me, core, along_x, along_y, across


def meet(devices):
    barrier = pltpu.get_barrier_semaphore()
    for device in devices:
        pl.semaphore_signal(barrier, inc=1, device_id=device, device_id_type=MESH)
    pl.semaphore_wait(barrier, len(devices))


def plane_devices():
    place = lax.axis_index("expert")
    _, core, along_x, along_y, _ = neighbours()
    return [(core, place), (along_x, place), (along_y, place)]


GATHER_COPIES = 14


def gather_copies(first, second, source_first, source_second, send, recv, local):
    place = lax.axis_index("expert")
    me, core, along_x, along_y, across = neighbours()

    def remote(index, source, target, device):
        return pltpu.make_async_remote_copy(
            src_ref=source,
            dst_ref=target,
            send_sem=send.at[index],
            recv_sem=recv.at[index],
            device_id=(device, place),
            device_id_type=MESH,
        )

    own = [
        pltpu.make_async_copy(source_first, first.at[me], local.at[0]),
        pltpu.make_async_copy(source_second, second.at[me], local.at[1]),
    ]
    near = [
        remote(0, source_first, first.at[me], along_x),
        remote(1, source_second, second.at[me], along_y),
        remote(2, source_first, first.at[me], along_y),
        remote(3, source_second, second.at[me], along_x),
    ]
    paired = [
        remote(4, source_first, first.at[me], core),
        remote(5, source_second, second.at[me], core),
    ]
    far = [
        remote(6, first.at[along_x], first.at[along_x], along_y),
        remote(7, second.at[along_y], second.at[along_y], along_x),
    ]
    paired_near = [
        remote(8, first.at[along_x], first.at[along_x], core),
        remote(9, second.at[along_y], second.at[along_y], core),
        remote(10, first.at[along_y], first.at[along_y], core),
        remote(11, second.at[along_x], second.at[along_x], core),
    ]
    paired_far = [
        remote(12, first.at[across], first.at[across], core),
        remote(13, second.at[across], second.at[across], core),
    ]

    def start0():
        for copy in near + paired + own:
            copy.start()

    def start1():
        near[0].wait_recv()
        far[0].start()
        near[1].wait_recv()
        far[1].start()
        near[2].wait_recv()
        near[3].wait_recv()
        for copy in paired_near:
            copy.start()

    def start2():
        for copy, onward in zip(far, paired_far):
            copy.wait_recv()
            onward.start()

    def finish():
        for copy in own:
            copy.wait()
        for copy in paired + paired_near + paired_far:
            copy.wait_recv()
        for copy in near + paired + far + paired_near + paired_far:
            copy.wait_send()

    return start0, start1, start2, finish


def gather_sems():
    return [
        pltpu.SemaphoreType.DMA((GATHER_COPIES,)),
        pltpu.SemaphoreType.DMA((GATHER_COPIES,)),
        pltpu.SemaphoreType.DMA((2,)),
    ]


def sds(shape, dtype):
    return jax.ShapeDtypeStruct(shape, dtype)


def partner(place, k):
    return 2 * lax.rem(place // 2 + k // 2, 2) + lax.rem(lax.rem(place, 2) + k % 2, 2)


ORDER = (1, 0, 3, 2)


def place_devices(group):
    me = lax.axis_index("dp")
    place = lax.axis_index("expert")
    return [(me, lax.rem(place + k, group)) for k in range(1, group)]


def along_axis(source, target, send, recv, place):
    return pltpu.make_async_remote_copy(
        src_ref=source,
        dst_ref=target,
        send_sem=send,
        recv_sem=recv,
        device_id=(lax.axis_index("dp"), place),
        device_id_type=MESH,
    )


def swap_copies(source, target, send, recv, group):
    place = lax.axis_index("expert")
    copies = []
    for k in range(1, group):
        other = lax.rem(place + k, group)
        copies.append(along_axis(source.at[other], target.at[place], send.at[k], recv.at[k], other))
    return copies


def slice_copies(w_in, w_out, first, second, send, recv, base, place):
    me = lax.axis_index("dp")
    chunk = (first if second is None else second).shape[1]
    here = pl.ds(pl.multiple_of(me * chunk, 128), chunk)
    pieces = []
    if first is not None:
        pieces.append((w_in.at[0, :, here], first))
    if second is not None:
        pieces += [
            (w_out.at[0, here, pl.ds(at, chunk)], second.at[pl.ds(at, chunk)]) for at in (0, chunk)
        ]
    return [
        along_axis(source, goal, send.at[base + i], recv.at[base + i], place)
        for i, (source, goal) in enumerate(pieces)
    ]


REDUCE_COPIES = 10


def reduce_copies(terms, own, pair, inbox, send, recv, local, emit):
    place = lax.axis_index("expert")
    me, core, along_x, along_y, across = neighbours()
    targets = (across, along_x, along_y, me)

    def remote(index, source, target, device):
        return pltpu.make_async_remote_copy(
            src_ref=source,
            dst_ref=target,
            send_sem=send.at[index],
            recv_sem=recv.at[index],
            device_id=(device, place),
            device_id_type=MESH,
        )

    loads = [pltpu.make_async_copy(terms.at[t], own.at[q], local.at[q]) for q, t in enumerate(targets)]
    pairs = [
        remote(q, terms.at[t + 1 - 2 * lax.rem(t, 2)], pair.at[q], core) for q, t in enumerate(targets)
    ]
    far_first = remote(4, own.at[0, 0], inbox.at[0], along_x)
    far_second = remote(5, own.at[0, 1], inbox.at[1], along_y)
    near_first = remote(6, own.at[1, 0], inbox.at[2], along_x)
    near_second = remote(7, own.at[2, 1], inbox.at[3], along_y)
    late_first = remote(8, own.at[2, 0], inbox.at[4], along_y)
    late_second = remote(9, own.at[1, 1], inbox.at[5], along_x)

    def merge(q):
        loads[q].wait()
        pairs[q].wait_recv()
        own[q] = own[q] + pair[q]

    def start():
        pairs[0].start()
        for copy in loads:
            copy.start()

    def far():
        merge(0)
        far_first.start()
        far_second.start()
        for copy in pairs[1:]:
            copy.start()

    def near():
        merge(1)
        near_first.start()
        merge(2)
        near_second.start()

    def late():
        far_first.wait_recv()
        own[2, 0] = own[2, 0] + inbox[0]
        late_first.start()
        far_second.wait_recv()
        own[1, 1] = own[1, 1] + inbox[1]
        late_second.start()

    def finish():
        merge(3)
        for copy in (near_first, near_second, late_first, late_second):
            copy.wait_recv()
        emit(0, own[3, 0].astype(F32) + inbox[2].astype(F32) + inbox[4].astype(F32))
        emit(1, own[3, 1].astype(F32) + inbox[3].astype(F32) + inbox[5].astype(F32))
        for copy in pairs + [far_first, far_second, near_first, near_second, late_first, late_second]:
            copy.wait_send()

    return start, far, near, late, finish


def reduce_scratch(shape):
    half = shape[1:]
    return [
        pltpu.VMEM((4, *shape), BF16),
        pltpu.VMEM((4, *shape), BF16),
        pltpu.VMEM((6, *half), BF16),
        pltpu.SemaphoreType.DMA((REDUCE_COPIES,)),
        pltpu.SemaphoreType.DMA((REDUCE_COPIES,)),
        pltpu.SemaphoreType.DMA((4,)),
    ]


def weight(slots_ref, index, share):
    return slots_ref[:, index * share : (index + 1) * share, :].reshape(-1, D)


def front_kernel(
    x_ref, grad_ref, routes_ref, w_in_ref, w_out_ref, wq_ref, wk_ref, wv_ref, wo_ref, small_ref, buckets_ref, seg_ref,
    x_out, grad_out, c0_out, c1_out, first_out, second_out, a_out, q_out, k_out, v_out, o_out, table_out,
    h_out, n_out, gate_out, pr_out, gather_first, gather_second, piece_out, params_ref, across_ref, down_ref, lse_ref,
    land, routes_land, first, second, stage_first, stage_second,
    a_ref, q_ref, k_ref, v_ref, o_ref, table_ref, h_ref, n_ref, gate_ref, pr_ref, line_ref,
    x_send, x_recv, r_send, r_recv, g_send, g_recv, p_send, p_recv, keep, own_local, out_sem,
    send, recv, local, send_w, recv_w, local_w,
    *, group, share, heads, experts, scale, width
):
    me = lax.axis_index("dp")
    place = lax.axis_index("expert")
    pieces = [
        (wq_ref, stage_first.at[pl.ds(0, share)]),
        (wk_ref, stage_first.at[pl.ds(share, share)]),
        (wv_ref, stage_second.at[pl.ds(0, share)]),
        (wo_ref, stage_second.at[pl.ds(share, share)]),
    ]
    staged = [pltpu.make_async_copy(src, dst, own_local.at[i]) for i, (src, dst) in enumerate(pieces)]
    for copy in staged:
        copy.start()
    small = small_ref[...].astype(F32)
    line = lax.broadcasted_iota(jnp.int32, small.shape, 0)
    placed = jnp.where(line < 16, pltpu.roll(small, me * share, 1), pltpu.roll(small, me * 4, 1))
    stage_second[2 * share :, :] = placed.astype(BF16)
    meet(plane_devices() + place_devices(group))
    moves = swap_copies(routes_ref, routes_land, r_send, r_recv, group)
    moves_x = swap_copies(x_ref, land, x_send, x_recv, group)
    moves_g = swap_copies(grad_ref, grad_out, g_send, g_recv, group)
    slices = slice_copies(w_in_ref, w_out_ref, piece_out.at[0], piece_out.at[1], p_send, p_recv, 0, partner(place, 1))
    distant = slice_copies(w_in_ref, w_out_ref, c0_out, c1_out, p_send, p_recv, 3, partner(place, 3))
    kept = [
        pltpu.make_async_copy(routes_ref.at[place], routes_land.at[place], keep.at[0]),
        pltpu.make_async_copy(x_ref.at[place], land.at[place], keep.at[1]),
        pltpu.make_async_copy(grad_ref.at[place], grad_out.at[place], keep.at[2]),
    ]
    for copy in moves + moves_x + kept:
        copy.start()
    for copy in staged:
        copy.wait()
    start0, start1, start2, finish = gather_copies(first, second, stage_first, stage_second, send, recv, local)
    start0()

    kept[0].wait()
    for copy in moves:
        copy.wait_recv()
    seq = down_ref.shape[0]
    row_id = lax.broadcasted_iota(jnp.int32, (8, routes_land.shape[2]), 0)
    holder = jnp.full(row_id.shape, -1, jnp.int32)
    for k in range(experts):
        holder = jnp.where(row_id == k, partner(place, ORDER[k]), holder)
    named = []
    for p in range(group):
        picks = [routes_land[p, c : c + 1, :] == holder for c in range(2)]
        named.append((picks[0] | picks[1]).astype(F32))
    named = jnp.concatenate(named, axis=1)
    earlier = lax.broadcasted_iota(jnp.int32, (seq, seq), 0) < lax.broadcasted_iota(jnp.int32, (seq, seq), 1)
    before = nn(named.astype(BF16), earlier.astype(F32).astype(BF16))
    pos = jnp.where(named > 0, before, -1.0)
    which = lax.broadcasted_iota(jnp.int32, seg_ref.shape, 0)
    segs = jnp.where(which == place, seg_ref[...], 0).astype(F32).sum(axis=0, keepdims=True)
    stack = jnp.concatenate([pos, jnp.broadcast_to(segs, (8, seq))], axis=0)
    across_ref[...] = stack.astype(jnp.int32)
    filled = jnp.concatenate([stack, jnp.full((112, seq), -1.0, F32)], axis=0)
    down_ref[...] = filled.T.astype(jnp.int32)

    start1()
    start2()
    finish()
    out_copies = []

    def put(source, target):
        out_copies.append(pltpu.make_async_copy(source, target, out_sem.at[len(out_copies)]))
        out_copies[-1].start()

    put(first, first_out)
    put(second, second_out)
    params = second[0, 2 * share :, :].astype(F32)
    for slot in range(1, second.shape[0]):
        params = params + second[slot, 2 * share :, :].astype(F32)
    turned = []
    for k in range(experts):
        wanted = partner(place, ORDER[k])
        picked = jnp.zeros((1, D), F32)
        for e in range(experts):
            picked = picked + params[8 + e : 9 + e, :] * jnp.where(wanted == e, 1.0, 0.0)
        turned.append(picked)
    params_ref[...] = params
    for k in range(experts):
        params_ref[8 + k : 9 + k, :] = turned[k]
    hot = (lax.broadcasted_iota(jnp.int32, (128, seq), 0) == buckets_ref[...]).astype(F32).astype(BF16)
    lines = nn(params[16:32, :128].astype(BF16), hot)
    for h in range(heads):
        line_ref[h] = lines[h : h + 1, :]

    kept[1].wait()
    for copy in moves_x:
        copy.wait_recv()
    for copy in slices + distant + moves_g:
        copy.start()
    put(land, x_out)
    part = land.shape[1]
    for p in range(group):
        here = slice(p * part, (p + 1) * part)
        x = land[p].astype(F32)
        inverse = lax.rsqrt(jnp.mean(x * x, axis=-1, keepdims=True) + EPSILON)
        normed = (x * inverse * params[0:1, :]).astype(BF16)
        a_ref[here, :] = normed
        q = nn(normed, weight(first, 0, share)).astype(BF16)
        q_ref[here, :] = (q.astype(F32) * scale).astype(BF16)
        k_ref[here, :] = nn(normed, weight(first, 1, share)).astype(BF16)
        v_ref[here, :] = nn(normed, weight(second, 0, share)).astype(BF16)
    for source, target in ((a_ref, a_out), (q_ref, q_out), (k_ref, k_out), (v_ref, v_out)):
        put(source, target)
    gather = gather_copies(
        gather_first, gather_second, piece_out.at[0], piece_out.at[1], send_w, recv_w, local_w
    )
    pairs = 128 // width
    count = heads // pairs

    def table_copy(n):
        heads_here = pl.ds(n * pairs, pairs)
        return pltpu.make_async_copy(table_ref.at[heads_here], table_out.at[heads_here], keep.at[3 + n])

    def attend(n, carry):
        @pl.when(n == 4)
        def _():
            for copy in slices:
                copy.wait_recv()
            gather[0]()

        attend_pair(n, q_ref, k_ref, v_ref, line_ref, table_ref, down_ref, across_ref, o_ref, lse_ref, width)
        table_copy(n).start()
        return carry

    lax.fori_loop(0, count, attend, 0)
    put(o_ref, o_out)

    def route(i, carry):
        here = pl.ds(pl.multiple_of(i * TILE, TILE), TILE)
        route_rows(
            land[i], o_ref[here, :], second, params_ref, down_ref, h_ref, n_ref, gate_ref, pr_ref, here, share, experts
        )
        return carry

    lax.fori_loop(0, group, route, 0)
    for source, target in ((h_ref, h_out), (n_ref, n_out), (gate_ref, gate_out), (pr_ref, pr_out)):
        put(source, target)
    gather[1]()
    gather[2]()
    kept[2].wait()
    for copy in distant + moves_g:
        copy.wait_recv()
    for copy in moves + moves_x + slices + distant + moves_g:
        copy.wait_send()
    gather[3]()
    for n in range(count):
        table_copy(n).wait()
    for copy in out_copies:
        copy.wait()


def masked_scores(k, q, table_ref, head, i, j, seg_col, seg_row):
    scores = nt(k, q) + table_ref[head, i - j].astype(F32)
    allowed = seg_col == seg_row
    if i == j:
        key_at = lax.broadcasted_iota(jnp.int32, (TILE, TILE), 0)
        query_at = lax.broadcasted_iota(jnp.int32, (TILE, TILE), 1)
        allowed = allowed & (key_at <= query_at)
    return jnp.where(allowed, scores, MASKED)


def route_rows(x, o, second_ref, params_ref, down_ref, h_ref, a_ref, gate_ref, pr_ref, here, share, experts):
    h1 = x.astype(F32) + nn(o, weight(second_ref, 1, share))
    h_ref[here, :] = h1
    inverse = lax.rsqrt(jnp.mean(h1 * h1, axis=-1, keepdims=True) + EPSILON)
    normed = (h1 * inverse * params_ref[1:2, :]).astype(BF16)
    a_ref[here, :] = normed
    router = jnp.concatenate([params_ref[8:16, :], jnp.zeros((120, D), F32)], axis=0).astype(BF16)
    logits = nt(normed, router)
    lane = lax.broadcasted_iota(jnp.int32, logits.shape, 1)
    logits = jnp.where(lane < experts, logits, MASKED)
    lifted = jnp.exp(logits - logits.max(axis=-1, keepdims=True))
    pr = lifted / lifted.sum(axis=-1, keepdims=True)
    named = (down_ref[here, :] >= 0) & (lane < experts)
    picked = jnp.where(named, pr, 0.0)
    pr_ref[here, :] = pr
    gate_ref[here, :] = picked / picked.sum(axis=-1, keepdims=True)


def attend_pair(n, q_ref, k_ref, v_ref, line_ref, table_ref, down_ref, across_ref, o_ref, lse_ref, width):
    columns = pl.ds(pl.multiple_of(n * 128, 128), 128)
    heads = 128 // width
    for h in range(heads):
        row = line_ref[n * heads + h]
        for gap in range(table_ref.shape[1]):
            ahead = row[:, gap * TILE : (gap + 1) * TILE]
            back = row[:, (gap - 1) * TILE : gap * TILE] if gap else jnp.zeros_like(ahead)
            grid = jnp.broadcast_to(jnp.concatenate([ahead, back], axis=1), (TILE, 2 * TILE))
            grid = pltpu.roll(grid, 0, 1, stride=1, stride_axis=0)
            table_ref[n * heads + h, gap] = grid[:, :TILE].astype(BF16)
    q_all, k_all, v_all = q_ref[:, columns], k_ref[:, columns], v_ref[:, columns]
    blocks = q_all.shape[0] // TILE
    turned = [v_all[:, h * width : (h + 1) * width].T for h in range(heads)]
    for i in range(blocks):
        here = slice(i * TILE, (i + 1) * TILE)
        outs = []
        for h in range(heads):
            lanes = slice(h * width, (h + 1) * width)
            q = q_all[here, lanes]
            pieces = []
            for j in range(i + 1):
                there = slice(j * TILE, (j + 1) * TILE)
                pieces.append(
                    masked_scores(
                        k_all[there, lanes], q, table_ref, n * heads + h, i, j, down_ref[there, 8:9],
                        across_ref[8:9, here]
                    )
                )
            top = pieces[0].max(axis=0, keepdims=True)
            for piece in pieces[1:]:
                top = jnp.maximum(top, piece.max(axis=0, keepdims=True))
            total = jnp.zeros_like(top)
            acc = jnp.zeros((width, TILE), F32)
            for j, piece in enumerate(pieces):
                lifted = jnp.exp(piece - top)
                total = total + lifted.sum(axis=0, keepdims=True)
                acc = acc + nn(turned[h][:, j * TILE : (j + 1) * TILE], lifted.astype(BF16))
            outs.append(acc / total)
            lse_ref[n, h : h + 1, here] = top + jnp.log(total)
        o_ref[here, columns] = jnp.concatenate(outs, axis=0).T.astype(BF16)


def attend_back_kernel(
    q_ref, k_ref, v_ref, do_ref, table_ref, down_ref, across_ref, lse_ref, a_ref, passed, terms,
    dq_ref, dk_ref, dv_ref, dist_ref, dwq_ref, dwk_ref, dwv_ref, sums_ref, pass_out,
    sum_ref, dk_sum, dv_sum, turned_a, p_send, p_recv, own, pair, inbox, send, recv, local, *, width, scale, group
):
    step = pl.program_id(0)
    last = pl.num_programs(0) - 1
    place = lax.axis_index("expert")

    def emit(half, value):
        sums_ref[half] = value.astype(BF16)

    start, far, near, late, finish = reduce_copies(terms.at[1], own, pair, inbox, send, recv, local, emit)
    hop = along_axis(passed, pass_out, p_send.at[0], p_recv.at[0], partner(place, 2))

    @pl.when(step == 0)
    def _():
        meet(plane_devices() + [(lax.axis_index("dp"), partner(place, 2))])
        start()
        hop.start()
        far()
        turned_a[...] = a_ref[...].T
        near()

    @pl.when(step == 3)
    def _():
        late()

    blocks = q_ref.shape[0] // TILE
    heads = q_ref.shape[1] // width
    turned = [k_ref[:, h * width : (h + 1) * width].T for h in range(heads)]
    dist_ref[...] = jnp.zeros_like(dist_ref)
    for h in range(heads):
        lanes = slice(h * width, (h + 1) * width)
        for i in range(blocks):
            here = slice(i * TILE, (i + 1) * TILE)
            q = q_ref[here, lanes]
            do = do_ref[here, lanes]
            lse = lse_ref[0, h : h + 1, here]
            probs, dprobs = [], []
            delta = jnp.zeros((1, TILE), F32)
            for j in range(i + 1):
                there = slice(j * TILE, (j + 1) * TILE)
                scores = masked_scores(
                    k_ref[there, lanes], q, table_ref, h, i, j, down_ref[there, 8:9], across_ref[8:9, here]
                )
                p = jnp.exp(scores - lse)
                dp = nt(v_ref[there, lanes], do)
                delta = delta + (p * dp).sum(axis=0, keepdims=True)
                probs.append(p)
                dprobs.append(dp)
            turned_dq = jnp.zeros((width, TILE), F32)
            for j in range(i + 1):
                there = slice(j * TILE, (j + 1) * TILE)
                ds = probs[j] * (dprobs[j] - delta)
                low = ds.astype(BF16)
                dv = nn(probs[j].astype(BF16), do)
                dk = nn(low, q)
                if i == j:
                    dv_sum[there, lanes] = dv
                    dk_sum[there, lanes] = dk
                else:
                    dv_sum[there, lanes] += dv
                    dk_sum[there, lanes] += dk
                turned_dq = turned_dq + nn(turned[h][:, there], low)
                if j == 0:
                    sum_ref[i - j] = ds
                else:
                    sum_ref[i - j] += ds
            dq_ref[here, lanes] = (turned_dq * scale).T.astype(BF16)
        for gap in range(blocks):
            part = sum_ref[gap]
            part = jnp.concatenate([part, jnp.zeros_like(part)], axis=1)
            half = TILE // 2
            while half:
                part = part[:half] + pltpu.roll(part[half : 2 * half], 2 * TILE - half, 1)
                half //= 2
            dist_ref[h, :, gap * TILE : (gap + 1) * TILE] += part[:, :TILE]
            if gap:
                dist_ref[h, :, (gap - 1) * TILE : gap * TILE] += part[:, TILE:]
    dk_ref[...] = dk_sum[...].astype(BF16)
    dv_ref[...] = dv_sum[...].astype(BF16)

    grads = jnp.concatenate([dq_ref[...], dk_ref[...], dv_ref[...]], axis=1)
    sums = nn(turned_a[...], grads).astype(BF16)
    for index, dw_ref in enumerate((dwq_ref, dwk_ref, dwv_ref)):
        dw_ref[...] = sums[:, index * 128 : (index + 1) * 128]

    @pl.when(step == last)
    def _():
        finish()
        hop.wait()


def experts_kernel(
    a_ref, g_ref, gate_ref, across_ref, first_a, second_a, piece_c0, piece_c1, w_in_ref, w_out_ref,
    eo_ref, da_ref, dw_out, sum_a, sum_c, piece_b, first_c, second_c, first_b, second_b,
    rows_a, turned_a, rows_d, eo_sum, da_sum, w_in_two, w_out_two, dw_two, total_a,
    w_sem, dw_sem, hop_send, hop_recv, save, free, own, pair, inbox, send_a, recv_a, local_a,
    send_c, recv_c, local_c, *gather, capacity, group, shards
):
    step = pl.program_id(0)
    last = pl.num_programs(0) - 1
    steps = shards // 2
    turn = step // steps
    slot = lax.rem(step, 2)
    place = lax.axis_index("expert")
    chunk = w_in_two.shape[3]

    def loads(at, which):
        c = lax.rem(at, steps)
        two = lax.rem(at, 2)
        if which != 1:
            first, second = {0: (first_a, second_a), 2: (first_c, second_c), 3: (first_b, second_b)}[which]
            both = pl.ds(2 * c, 2)
            return [
                pltpu.make_async_copy(first.at[both], w_in_two.at[two], w_sem.at[0, two]),
                pltpu.make_async_copy(second.at[both], w_out_two.at[two], w_sem.at[1, two]),
            ]
        copies = []
        for h in range(2):
            cols = pl.ds(pl.multiple_of((2 * c + h) * chunk, 128), chunk)
            copies.append(
                pltpu.make_async_copy(w_in_ref.at[0, :, cols], w_in_two.at[two, h], w_sem.at[3 * h, two])
            )
            for l in range(2):
                lanes = pl.ds(l * chunk, chunk)
                copies.append(
                    pltpu.make_async_copy(
                        w_out_ref.at[0, cols, lanes], w_out_two.at[two, h, lanes], w_sem.at[3 * h + 1 + l, two]
                    )
                )
        return copies

    def each_turn(at, action):
        for which in range(group):
            @pl.when(at // steps == which)
            def _(which=which):
                for copy in loads(at, which):
                    action(copy)

    def saved(at):
        two = lax.rem(at, 2)
        return pltpu.make_async_copy(
            dw_two.at[two], dw_out.at[at // steps, pl.ds(2 * lax.rem(at, steps), 2)], dw_sem.at[two]
        )

    gather_c = gather_copies(first_c, second_c, piece_c0, piece_c1, *gather[:3])
    gather_b = gather_copies(first_b, second_b, piece_b.at[0], piece_b.at[1], *gather[3:])
    relays = [
        along_axis(piece, piece_b.at[i], hop_send.at[2 * i], hop_recv.at[2 * i], partner(place, 1))
        for i, piece in enumerate((piece_c0, piece_c1))
    ]
    hop = along_axis(total_a, sum_a, hop_send.at[1], hop_recv.at[1], partner(place, 1))
    keep = pltpu.make_async_copy(own.at[3], sum_c, save.at[0])

    def emit_a(half, value):
        total_a[half] = value.astype(BF16)

    def emit_c(half, value):
        own[3, half] = value.astype(BF16)

    reduce_a = reduce_copies(dw_out.at[0], own, pair, inbox, send_a, recv_a, local_a, emit_a)
    reduce_c = reduce_copies(dw_out.at[2], own, pair, inbox, send_c, recv_c, local_c, emit_c)

    @pl.when(step == 0)
    def _():
        meet(plane_devices() + [(lax.axis_index("dp"), partner(place, 1))])
        gather_c[0]()
        for copy in relays:
            copy.start()
        each_turn(step, lambda copy: copy.start())

    def release():
        for device in plane_devices():
            pl.semaphore_signal(free, inc=1, device_id=device, device_id_type=MESH)

    def claim():
        pl.semaphore_wait(free, len(plane_devices()))

    schedule = {
        3: [gather_c[1]],
        6: [gather_c[2], gather_c[3], relays[0].wait, relays[1].wait, gather_b[0]],
        9: [gather_b[1], reduce_a[0], reduce_a[1]],
        10: [reduce_a[2]],
        12: [reduce_a[3]],
        14: [reduce_a[4], release, hop.start, claim, reduce_c[0], reduce_c[1]],
        15: [reduce_c[2]],
    }
    for when, actions in schedule.items():
        @pl.when(step == when)
        def _(actions=actions):
            for action in actions:
                action()

    @pl.when(lax.rem(step, steps) == 0)
    def _():
        tokens = a_ref.shape[0]
        places = lax.broadcasted_iota(jnp.int32, (capacity, tokens), 0)
        pick = (across_ref[pl.ds(turn, 1), :] == places).astype(BF16)
        rows = nn(pick, a_ref[...]).astype(BF16)
        rows_a[...] = rows
        turned_a[...] = rows.T
        lane = lax.broadcasted_iota(jnp.int32, gate_ref.shape, 1)
        gate = jnp.sum(jnp.where(lane == turn, gate_ref[...], 0.0), axis=-1, keepdims=True)
        rows_d[...] = nn(pick, (gate * g_ref[...].astype(F32)).astype(BF16)).astype(BF16)
        eo_sum[...] = jnp.zeros_like(eo_sum)
        da_sum[...] = jnp.zeros_like(da_sum)

    each_turn(step, lambda copy: copy.wait())
    ahead = step + 1

    @pl.when((step < last) & (ahead != 3 * steps))
    def _():
        each_turn(ahead, lambda copy: copy.start())

    @pl.when(step > 1)
    def _():
        saved(step - 2).wait()

    d = rows_d[...]
    w_in = jnp.concatenate([w_in_two[slot, h] for h in range(2)], axis=1)
    w_out = jnp.concatenate(
        [
            jnp.concatenate([w_out_two[slot, h, :chunk], w_out_two[slot, h, chunk:]], axis=1)
            for h in range(2)
        ],
        axis=0,
    )
    u = nn(rows_a[...], w_in)
    square = u * u
    t = jnp.tanh(GELU_A * u * (1.0 + GELU_B * square))
    half = 0.5 * (1.0 + t)
    z = (u * half).astype(BF16)
    eo_sum[...] += nn(z, w_out)
    dw_last = tn(z, d).astype(BF16)
    slope = half + (0.5 * GELU_A) * u * (1.0 - t * t) * (1.0 + 3.0 * GELU_B * square)
    du = (nt(d, w_out) * slope).astype(BF16)
    da_sum[...] += nt(du, w_in)
    dw_first = nn(turned_a[...], du).astype(BF16)
    for h in range(2):
        here = slice(h * chunk, (h + 1) * chunk)
        dw_two[slot, h, 0] = dw_first[:, here]
        dw_two[slot, h, 1, :chunk] = dw_last[here, :chunk]
        dw_two[slot, h, 1, chunk:] = dw_last[here, chunk:]
    saved(step).start()

    @pl.when(lax.rem(ahead, steps) == 0)
    def _():
        eo_ref[0] = eo_sum[...].astype(BF16)
        da_ref[0] = da_sum[...].astype(BF16)

    @pl.when(ahead == 3 * steps)
    def _():
        gather_b[2]()
        gather_b[3]()
        each_turn(ahead, lambda copy: copy.start())

    @pl.when(step == last)
    def _():
        saved(step - 1).wait()
        saved(step).wait()
        reduce_c[3]()
        reduce_c[4]()
        keep.start()
        hop.wait()
        keep.wait()


def send_rows(step, value, stage, target, sends, recvs, keep, group):
    place = lax.axis_index("expert")
    for p in range(group):
        @pl.when(step == p)
        def _(p=p):
            stage[p] = value

            @pl.when(place == p)
            def _():
                pltpu.make_async_copy(stage.at[p], target.at[p], keep.at[0]).start()

            @pl.when(place != p)
            def _():
                along_axis(stage.at[p], target.at[place], sends.at[p], recvs.at[place], p).start()


def end_rows(stage, target, sends, recvs, keep, group):
    place = lax.axis_index("expert")
    for k in range(1, group):
        other = lax.rem(place + k, group)
        along_axis(stage.at[other], target.at[other], sends.at[other], recvs.at[other], other).wait_recv()
    for k in range(1, group):
        other = lax.rem(place + k, group)
        along_axis(stage.at[other], target.at[place], sends.at[other], recvs.at[place], other).wait_send()
    pltpu.make_async_copy(stage.at[place], target.at[place], keep.at[0]).wait()


def combine_kernel(
    h_ref, a_ref, g_ref, o_ref, gate_ref, pr_ref, pos_ref, eo_ref, back_ref, second_ref, params_ref, terms, passed,
    out_all, dh_ref, do_ref, dw_ref, dgain_ref, drouter_ref, sums_ref,
    stage, landed, p_send, p_recv, sends, recvs, keep, own, pair, inbox, send, recv, local,
    *, share, experts, capacity, group
):
    step = pl.program_id(0)
    last = pl.num_programs(0) - 1
    place = lax.axis_index("expert")

    def emit(half, value):
        sums_ref[half] = (value + landed[half].astype(F32)).astype(BF16)

    start, far, near, late, finish = reduce_copies(terms.at[3], own, pair, inbox, send, recv, local, emit)
    hop = along_axis(passed, landed, p_send.at[0], p_recv.at[0], partner(place, 1))

    @pl.when(step == 0)
    def _():
        meet(plane_devices() + place_devices(group))
        start()
        hop.start()
        far()

    @pl.when(step == 1)
    def _():
        near()

    @pl.when(step == 3)
    def _():
        late()

    @pl.when(step == 0)
    def _():
        dw_ref[...] = jnp.zeros_like(dw_ref)
        dgain_ref[...] = jnp.zeros_like(dgain_ref)
        drouter_ref[...] = jnp.zeros_like(drouter_ref)

    tile = h_ref.shape[0]
    h1 = h_ref[...]
    g = g_ref[...].astype(F32)
    gates = gate_ref[...]
    pr = pr_ref[...]
    lane = lax.broadcasted_iota(jnp.int32, pr.shape, 1)
    slot = lax.broadcasted_iota(jnp.int32, (tile, capacity), 1)
    result = h1
    dgate = jnp.zeros_like(pr)
    da = jnp.zeros_like(h1)
    for k in range(experts):
        spot = (pos_ref[:, k : k + 1] == slot).astype(BF16)
        got = nn(spot, eo_ref[k])
        result = result + gates[:, k : k + 1] * got
        dgate = jnp.where(lane == k, jnp.sum(g * got, axis=-1, keepdims=True), dgate)
        da = da + nn(spot, back_ref[k])
    send_rows(step, result.astype(BF16), stage, out_all, sends, recvs, keep, group)
    named = (pos_ref[...] >= 0) & (lane < experts)
    denom = jnp.sum(jnp.where(named, pr, 0.0), axis=-1, keepdims=True)
    weighted = jnp.sum(dgate * gates, axis=-1, keepdims=True)
    dpr = jnp.where(named, (dgate - weighted) / denom, 0.0)
    dlog = pr * (dpr - jnp.sum(pr * dpr, axis=-1, keepdims=True))
    high = dlog.astype(BF16)
    lost = (dlog - high.astype(F32)).astype(BF16)
    a = a_ref[...]
    drouter_ref[...] += (tn(high, a) + tn(lost, a))[: drouter_ref.shape[0]]
    for k in range(experts):
        da = da + dlog[:, k : k + 1] * params_ref[8 + k : 9 + k, :]
    inverse = lax.rsqrt(jnp.mean(h1 * h1, axis=-1, keepdims=True) + EPSILON)
    n2 = h1 * inverse
    dgain_ref[...] += jnp.sum(da * n2, axis=0, keepdims=True)
    dn = da * params_ref[1:2, :]
    dh = g + inverse * (dn - n2 * jnp.mean(dn * n2, axis=-1, keepdims=True))
    dh_ref[...] = dh
    dy = dh.astype(BF16)
    do_ref[...] = nt(dy, weight(second_ref, 1, share)).astype(BF16)
    dw_ref[...] += tn(o_ref[...], dy)

    @pl.when(step == last)
    def _():
        hop.wait()
        finish()
        end_rows(stage, out_all, sends, recvs, keep, group)


def close_kernel(
    x_ref, dq_ref, dk_ref, dv_ref, dh_ref, first_ref, second_ref, params_ref, dwq_ref, dwk_ref, dwv_ref, dwo_ref,
    dgain_m_ref, drouter_ref, dist_ref, buckets_ref, sum0, sum1, sum2,
    din_out, gather_first, gather_second, dense_ref,
    stage, total, pack, own, pair, inbox, r_send, r_recv, r_local, sends, recvs, keep,
    z_in, z_total, z_final, z_send, z_recv, g_send, g_recv, g_local, *, share, group, experts
):
    step = pl.program_id(0)
    last = pl.num_programs(0) - 1
    place = lax.axis_index("expert")
    start0, start1, start2, finish = gather_copies(
        gather_first, gather_second, total.at[0], total.at[1], g_send, g_recv, g_local
    )
    quarter = pack.shape[2] // 2

    def emit(half, value):
        low = value.astype(BF16)
        z_total[2 * half] = low[:quarter]
        z_total[2 * half + 1] = low[quarter:]

    start, far, near, late, end_reduce = reduce_copies(pack, own, pair, inbox, r_send, r_recv, r_local, emit)

    @pl.when(step == 0)
    def _():
        places = ((0, 0, dwq_ref), (0, share, dwk_ref), (1, 0, dwv_ref), (1, share, dwo_ref))
        for half, at, grad_ref in places:
            pack[:, half, at : at + share, :] = grad_ref[...].astype(BF16).reshape(-1, share, D)
        seq = dist_ref.shape[2]
        hot = (lax.broadcasted_iota(jnp.int32, (128, seq), 0) == buckets_ref[...]).astype(F32).astype(BF16)
        left = jnp.concatenate([dist_ref[h] for h in range(dist_ref.shape[0])], axis=0)
        table = jnp.zeros((left.shape[0], 128), F32)
        for _ in range(3):
            low = left.astype(BF16)
            left = left - low.astype(F32)
            table = table + nt(low, hot)
        rows_out = [jnp.zeros((1, D), F32), dgain_m_ref[...], jnp.zeros((6, D), F32)]
        for e in range(experts):
            picked = jnp.zeros((1, D), F32)
            for k in range(experts):
                picked = picked + drouter_ref[k : k + 1, :] * jnp.where(partner(place, ORDER[k]) == e, 1.0, 0.0)
            rows_out.append(picked)
        rows_out.append(jnp.zeros((8 - experts, D), F32))
        rows_out.append(jnp.concatenate([table, jnp.zeros((table.shape[0], D - 128), F32)], axis=1))
        rows_out.append(jnp.zeros((16 - table.shape[0], D), F32))
        small = jnp.concatenate(rows_out, axis=0).astype(BF16)
        for slot in range(pack.shape[0]):
            pack[slot, 0, 2 * share :, :] = small
            pack[slot, 1, 2 * share :, :] = jnp.zeros_like(small)
        meet(plane_devices() + place_devices(group))
        start()
        far()
        near()
        for half in range(2):
            value = sum0[half].astype(F32) + sum1[half].astype(F32)
            total[half] = (value + sum2[half].astype(F32)).astype(BF16)

    @pl.when(step == 1)
    def _():
        start0()

    @pl.when(step == 2)
    def _():
        late()

    da = jnp.zeros(dh_ref.shape, F32)
    places = ((first_ref, 0), (first_ref, 1), (second_ref, 0))
    for index, grad_ref in enumerate((dq_ref, dk_ref, dv_ref)):
        slots_ref, at = places[index]
        da = da + nt(grad_ref[...], weight(slots_ref, at, share))
    x = x_ref[...].astype(F32)
    inverse = lax.rsqrt(jnp.mean(x * x, axis=-1, keepdims=True) + EPSILON)
    n1 = x * inverse
    dn = da * params_ref[0:1, :]
    din = dh_ref[...] + inverse * (dn - n1 * jnp.mean(dn * n1, axis=-1, keepdims=True))
    send_rows(step, din.astype(BF16), stage, din_out, sends, recvs, keep, group)

    @pl.when(step == last)
    def _():
        end_reduce()
        spread = [
            along_axis(z_total.at[lax.rem(place + k, group)], z_in.at[k - 1], z_send.at[k], z_recv.at[k],
                       lax.rem(place + k, group))
            for k in range(1, group)
        ]
        for copy in spread:
            copy.start()
        start1()
        for copy in spread:
            copy.wait_recv()
        value = z_total[place].astype(F32)
        for k in range(group - 1):
            value = value + z_in[k].astype(F32)
        z_final[place] = value.astype(BF16)
        share_out = [
            along_axis(z_final.at[place], z_final.at[place], z_send.at[group + k], z_recv.at[group + k],
                       lax.rem(place + k, group))
            for k in range(1, group)
        ]
        for copy in share_out:
            copy.start()
        start2()
        for copy in share_out:
            copy.wait_recv()
        for copy in spread + share_out:
            copy.wait_send()
        dense_ref[...] = z_final[...]
        end_rows(stage, din_out, sends, recvs, keep, group)
        finish()


def unpack_kernel(
    first_ref, second_ref, din_ref, dense_ref, wq_ref, wk_ref, wv_ref, gain_ref,
    in_ref, out_ref, grad_ref, dq_ref, dk_ref, dv_ref, do_ref, gain_out, small_ref, *, share
):
    chunk = first_ref.shape[2]
    in_ref[0] = first_ref[0].astype(F32)
    out_ref[0, :, :chunk] = second_ref[0, :chunk].astype(F32)
    out_ref[0, :, chunk:] = second_ref[0, chunk:].astype(F32)
    grad_ref[...] = din_ref[...].astype(F32)

    @pl.when(pl.program_id(0) == 0)
    def _():
        grads = []
        for grad, half, at in ((dq_ref, 0, 0), (dk_ref, 0, share), (dv_ref, 1, 0), (do_ref, 1, share)):
            value = dense_ref[half, at : at + share, :].astype(F32)
            grad[...] = value
            grads.append(value)
        moved = grads[0] * wq_ref[...].astype(F32) + grads[1] * wk_ref[...].astype(F32)
        moved = moved + grads[2] * wv_ref[...].astype(F32)
        gain_out[...] = jnp.sum(moved, axis=-1, keepdims=True) / gain_ref[...].astype(F32)
        small_ref[...] = dense_ref[0, 2 * share :, :].astype(F32)


def on_device_whole(
    layer_in, out_grad, routes, segments, buckets, gain_attn, w_query, w_key, w_value, w_output,
    gain_moe, router, rel_bias, w_expert_in, w_expert_out,
):
    group = lax.axis_size("expert")
    shards = lax.axis_size("dp")
    shard = lax.axis_index("dp")
    experts = router.shape[1]
    seq = segments.shape[1]
    heads = rel_bias.shape[1]
    width = D // heads
    scale = 1.0 / math.sqrt(width)
    share = D // shards
    ff = w_expert_in.shape[2]
    chunk = ff // shards
    blocks = seq // TILE
    part = seq // group
    capacity = 3 * seq // group
    pairs = 128 // width
    tokens = (seq, D)
    slots = (capacity, D)
    piece = (2, D, chunk)
    buffer = sds((shards, D, chunk), BF16)
    dma = pltpu.SemaphoreType.DMA
    vmem = pl.BlockSpec(memory_space=pltpu.VMEM)

    wide = lambda v, count: jnp.pad(v, ((0, count - v.shape[0]), (0, D - v.shape[1])))
    small = jnp.concatenate([
        wide(jnp.stack([gain_attn, gain_moe]), 8), wide(router.T, 8), wide(rel_bias.T, 16)])
    routes_in = jnp.pad(routes.transpose(0, 2, 1), ((0, 0), (0, 6), (0, 0)))
    bucket_row = buckets.reshape(1, seq)
    second_rows = 2 * share + 32
    tok16, tok32, wide32 = sds(tokens, BF16), sds(tokens, F32), sds((seq, 128), F32)
    block = sds((group, part, D), BF16)
    table_shape = (heads, blocks, TILE, TILE)
    v16, v32 = pltpu.VMEM(tokens, BF16), pltpu.VMEM(tokens, F32)
    (x, g, far_first, far_second, first, second, normed, q, k, v, o, table, h1, normed_m, gates, pr, near_first,
     near_second, _, params, across, down, lse) = call(
        functools.partial(
            front_kernel, group=group, share=share, heads=heads, experts=experts, scale=scale, width=width),
        "front", (1,),
        [ANY] * 9 + [vmem] * 3,
        [ANY] * 19 + [vmem] * 4,
        [block, block, sds((D, chunk), BF16), sds((D, chunk), BF16), sds((shards, 2 * share, D), BF16),
         sds((shards, second_rows, D), BF16)] + [tok16] * 5
        + [sds(table_shape, BF16), tok32, tok16, wide32, wide32, buffer, buffer, sds(piece, BF16),
           sds((32, D), F32), sds((16, seq), jnp.int32), sds((seq, 128), jnp.int32),
           sds((heads // pairs, pairs, seq), F32)],
        [pltpu.VMEM((group, part, D), BF16), pltpu.VMEM((group, 8, part), jnp.int32),
         pltpu.VMEM((shards, 2 * share, D), BF16), pltpu.VMEM((shards, second_rows, D), BF16),
         pltpu.VMEM((2 * share, D), BF16), pltpu.VMEM((second_rows, D), BF16)] + [v16] * 5
        + [pltpu.VMEM(table_shape, BF16), v32, v16, pltpu.VMEM((seq, 128), F32), pltpu.VMEM((seq, 128), F32),
           pltpu.VMEM((heads, 1, seq), F32)]
        + [dma((group,))] * 6 + [dma((6,))] * 2 + [dma((3 + heads // pairs,)), dma((4,)), dma((12,))]
        + gather_sems() * 2, collective=1, flops=6 * seq * D * D,
    )(layer_in, out_grad, routes_in, w_expert_in, w_expert_out, w_query, w_key, w_value, w_output, small, bucket_row,
      segments)
    x = x.reshape(tokens)
    g = g.reshape(tokens)
    buffers = [near_first, near_second]
    cols = pl.BlockSpec((seq, 128), lambda i: (0, i))
    table_spec = pl.BlockSpec((pairs, blocks, TILE, TILE), lambda i: (i, 0, 0, 0))
    lse_spec = pl.BlockSpec((1, pairs, seq), lambda i: (i, 0, 0))

    once = lambda shape: pl.BlockSpec(shape, lambda *_: (0,) * len(shape), pipeline_mode=pl.Buffered(1))
    turned = pl.BlockSpec((1, *slots), lambda i: (i // (shards // 2), 0, 0))
    eo, da, dw, sum1, sum3, _, _, _, _, _ = call(
        functools.partial(experts_kernel, capacity=capacity, group=group, shards=shards), "experts",
        (experts * shards // 2,),
        [once(tokens), once(tokens), once((seq, 128)), once((16, seq))] + [ANY] * 6,
        [turned, turned] + [ANY] * 8,
        [sds((experts, *slots), BF16)] * 2 + [sds((experts, shards, *piece), BF16)] + [sds(piece, BF16)] * 3
        + [buffer] * 4,
        [pltpu.VMEM(slots, BF16), pltpu.VMEM((D, capacity), BF16), pltpu.VMEM(slots, BF16),
         pltpu.VMEM(slots, F32), pltpu.VMEM(slots, F32), pltpu.VMEM((2, 2, D, chunk), BF16),
         pltpu.VMEM((2, 2, D, chunk), BF16), pltpu.VMEM((2, 2, *piece), BF16), pltpu.VMEM(piece, BF16),
         dma((6, 2)), dma((2,)), dma((3,)), dma((3,)), dma((1,)), pltpu.SemaphoreType.REGULAR]
        + reduce_scratch(piece) + reduce_scratch(piece)[3:] + gather_sems() * 2,
        flops=48 * capacity * D * ff, nbytes=96 * 2**20, collective=3,
    )(normed_m, g, gates, across, *buffers, far_first, far_second, w_expert_in, w_expert_out)
    layer_out, dh, do, grad_output, grad_gain_m, grad_router, sum2 = call(
        functools.partial(combine_kernel, share=share, experts=experts, capacity=capacity, group=group), "combine",
        (blocks,),
        [rows(D)] * 4 + [rows(128)] * 3 + [once((experts, *slots))] * 2 + [once(second.shape), whole((32, D)), ANY, ANY],
        [ANY, rows(D), rows(D), whole((D, D)), whole((1, D)), whole((8, D)), whole(piece)],
        [sds((group, part, D), BF16), sds(tokens, F32), sds(tokens, BF16), sds((D, D), F32), sds((1, D), F32),
         sds((8, D), F32), sds(piece, BF16)],
        [pltpu.VMEM((group, part, D), BF16), pltpu.VMEM(piece, BF16), dma((1,)), dma((1,)), dma((group,)),
         dma((group,)), dma((1,))] + reduce_scratch(piece),
        flops=24 * seq * D * D, nbytes=32 * 2**20, collective=7,
    )(h1, normed_m, g, o, gates, pr, down, eo, da, second, params, dw, sum3)
    dist_spec = pl.BlockSpec((pairs, 1, seq), lambda i: (i, 0, 0))
    dq, dk, dv, dist, grad_query, grad_key, grad_value, sum0, sum2 = call(
        functools.partial(attend_back_kernel, width=width, scale=scale, group=group), "attend_back",
        (heads // pairs,),
        [cols, cols, cols, cols, table_spec, whole((seq, 128)), whole((16, seq)), lse_spec, whole(tokens), ANY, ANY],
        [cols, cols, cols, dist_spec] + [pl.BlockSpec((D, 128), lambda i: (0, i))] * 3 + [whole(piece), ANY],
        [sds(tokens, BF16)] * 3 + [sds((heads, 1, seq), F32)] + [sds((D, D), BF16)] * 3
        + [sds(piece, BF16), sds(piece, BF16)],
        [pltpu.VMEM((blocks, TILE, TILE), F32), pltpu.VMEM((seq, 128), F32), pltpu.VMEM((seq, 128), F32),
         pltpu.VMEM((D, seq), BF16)]
        + [dma((1,))] * 2 + reduce_scratch(piece),
        flops=20 * seq * seq * D, nbytes=24 * 2**20, collective=8,
    )(q, k, v, do, table, down, across, lse, normed, sum2, dw)
    dense_slot = (2, 2 * share + 32, D)
    quarter = (dense_slot[1] // 2, D)
    grad_in, *gathered, dense = call(
        functools.partial(close_kernel, share=share, group=group, experts=experts), "close", (blocks,),
        [rows(D)] * 5 + [whole(first.shape), whole(second.shape), whole((32, D))] + [whole((D, D))] * 4
        + [whole((1, D)), whole((8, D)), whole((heads, 1, seq)), whole((1, seq))] + [whole(piece)] * 3,
        [ANY, ANY, ANY, whole((group, *quarter))],
        [sds((group, part, D), BF16), buffer, buffer, sds((group, *quarter), BF16)],
        [pltpu.VMEM((group, part, D), BF16), pltpu.VMEM(piece, BF16), pltpu.VMEM((shards, *dense_slot), BF16)]
        + reduce_scratch(dense_slot)
        + [dma((group,)), dma((group,)), dma((1,)), pltpu.VMEM((group - 1, *quarter), BF16),
           pltpu.VMEM((group, *quarter), BF16), pltpu.VMEM((group, *quarter), BF16), dma((2 * group,)),
           dma((2 * group,))] + gather_sems(),
        flops=12 * seq * D * D, nbytes=24 * 2**20, collective=9,
    )(x, dq, dk, dv, dh, first, second, params, grad_query, grad_key, grad_value, grad_output, grad_gain_m, grad_router,
      dist, bucket_row, sum0, sum1, sum2)
    spec = pl.BlockSpec((1, D, chunk), lambda i: (i, 0, 0))
    line_rows = pl.BlockSpec((seq // shards, D), lambda i: (i, 0))
    expert_in, expert_out, grad_in, *dense_grads, grad_gain, smalls = call(
        functools.partial(unpack_kernel, share=share), "unpack", (shards,),
        [spec, spec, line_rows, whole(dense_slot)] + [whole((share, D))] * 3 + [whole((share, 1))],
        [pl.BlockSpec((1, D, chunk), lambda i: (0, 0, i)), pl.BlockSpec((1, chunk, D), lambda i: (0, i, 0)), line_rows]
        + [whole((share, D))] * 4 + [whole((share, 1)), whole((32, D))],
        [sds(w_expert_in.shape, F32), sds(w_expert_out.shape, F32), sds(tokens, F32)]
        + [sds((share, D), F32)] * 4 + [sds((share, 1), F32), sds((32, D), F32)],
        nbytes=34 * 2**20,
    )(*gathered, grad_in.reshape(tokens), dense.reshape(dense_slot), w_query, w_key, w_value,
      gain_attn.reshape(share, 1))
    line = lax.dynamic_slice_in_dim(smalls[:16], shard * share, share, axis=1)
    grad_table = lax.dynamic_slice_in_dim(smalls[16 : 16 + heads], shard * rel_bias.shape[0], rel_bias.shape[0], axis=1)
    return (
        layer_out,
        grad_in.reshape(group, part, D),
        grad_gain.reshape(share),
        *dense_grads,
        line[1],
        line[8 : 8 + experts].T,
        grad_table.T,
        expert_in,
        expert_out,
    )


def solution(mesh):
    in_specs = (
        P(None, ("dp", "expert"), None),
        P(None, ("dp", "expert"), None),
        P(None, ("dp", "expert"), None),
        P(None, "dp"),
        P(),
        P("dp"),
        P("dp", None),
        P("dp", None),
        P("dp", None),
        P("dp", None),
        P("dp"),
        P("dp", None),
        P("dp", None),
        P("expert", None, None),
        P("expert", None, None),
    )
    out_specs = (
        P(None, ("dp", "expert"), None),
        P(None, ("dp", "expert"), None),
        P("dp"),
        P("dp", None),
        P("dp", None),
        P("dp", None),
        P("dp", None),
        P("dp"),
        P("dp", None),
        P("dp", None),
        P("expert", None, None),
        P("expert", None, None),
    )
    body = on_device_whole if mesh.shape["expert"] == MICRO else on_device
    return jax.shard_map(
        body, mesh=mesh, in_specs=in_specs, out_specs=out_specs, check_vma=False
    )
```

```python
import functools
import math

import jax
import jax.numpy as jnp
from jax import lax
from jax.experimental import pallas as pl
from jax.experimental.pallas import tpu as pltpu
from jax.sharding import PartitionSpec as P

D = 768
NB = 32
MICRO = 4


EPSILON = 1e-06
MASKED = -1e30
TOP_PRECISION = lax.Precision.HIGHEST
GELU_A = math.sqrt(2.0 / math.pi)
GELU_B = 0.044715


def norm_forward(values, gain):
    inverse = lax.rsqrt(jnp.mean(values * values, axis=-1, keepdims=True) + EPSILON)
    scaled = values * inverse
    return (scaled, inverse, scaled * gain)


def norm_backward(grad_top, scaled, inverse, gain):
    grad_scaled = grad_top * gain
    grad_values = inverse * (
        grad_scaled - scaled * jnp.mean(grad_scaled * scaled, axis=-1, keepdims=True)
    )
    return (grad_values, jnp.sum(grad_top * scaled, axis=0))


def split_heads(values, heads):
    return values.reshape(values.shape[0], heads, -1).transpose(1, 0, 2)


def merge_heads(values):
    return values.transpose(1, 0, 2).reshape(values.shape[1], -1)


def score_block(q_heads, k_heads, bias, allowed, scale):
    raw = jnp.einsum("hqd,hkd->hqk", q_heads, k_heads, preferred_element_type=jnp.float32)
    return jnp.where(allowed[None], raw * scale + bias, MASKED)


def bucket_table(distances, bucket_starts):
    lower = bucket_starts[:-1]
    upper = bucket_starts[1:]
    return (
        (distances[:, :, None] >= lower[None, None, :])
        & (distances[:, :, None] < upper[None, None, :])
    ).astype(jnp.bfloat16)


def on_device(
    layer_in,
    out_grad,
    routes,
    segments,
    buckets,
    gain_attn,
    w_query,
    w_key,
    w_value,
    w_output,
    gain_moe,
    router,
    rel_bias,
    w_expert_in,
    w_expert_out,
):
    tok_rows = layer_in.shape[1]
    seq_len = segments.shape[1]
    heads = rel_bias.shape[1]
    group_size = lax.axis_size("expert")
    rank_here = lax.axis_index("expert")
    expert_count = router.shape[1]
    local_experts = w_expert_in.shape[0]
    capacity = 3 * tok_rows // group_size
    scale = 1.0 / math.sqrt(D // heads)
    bucket_starts = jnp.sum(
        (buckets[None, :] < jnp.arange(NB + 1, dtype=jnp.int32)[:, None]).astype(jnp.int32), axis=1
    )
    query_pos = rank_here * tok_rows + jnp.arange(tok_rows, dtype=jnp.int32)
    key_pos = jnp.arange(seq_len, dtype=jnp.int32)
    offsets = jnp.maximum(query_pos[:, None] - key_pos[None, :], 0)
    bucket_onehot = bucket_table(offsets, bucket_starts)
    causal = query_pos[:, None] >= key_pos[None, :]
    slot_ids = jnp.arange(expert_count * capacity, dtype=jnp.int32)
    expert_ids = jnp.arange(expert_count, dtype=jnp.int32)
    pair_ids = jnp.arange(2 * tok_rows, dtype=jnp.int32)
    earlier = (pair_ids[None, :] < pair_ids[:, None]).astype(jnp.bfloat16)
    dense_sums = [
        jnp.zeros((D,), jnp.float32),
        jnp.zeros((D, D), jnp.float32),
        jnp.zeros((D, D), jnp.float32),
        jnp.zeros((D, D), jnp.float32),
        jnp.zeros((D, D), jnp.float32),
        jnp.zeros((D,), jnp.float32),
        jnp.zeros((D, expert_count), jnp.float32),
        jnp.zeros((NB, heads), jnp.float32),
    ]
    in_sum = jnp.zeros(w_expert_in.shape, jnp.float32)
    out_sum = jnp.zeros(w_expert_out.shape, jnp.float32)
    outputs_list = []
    grads_list = []
    for step_index in range(MICRO):
        weights_now = (
            lax.all_gather(gain_attn, "dp", axis=0, tiled=True),
            lax.all_gather(w_query, "dp", axis=0, tiled=True),
            lax.all_gather(w_key, "dp", axis=0, tiled=True),
            lax.all_gather(w_value, "dp", axis=0, tiled=True),
            lax.all_gather(w_output, "dp", axis=0, tiled=True),
            lax.all_gather(gain_moe, "dp", axis=0, tiled=True),
            lax.all_gather(router, "dp", axis=0, tiled=True),
            lax.all_gather(rel_bias, "dp", axis=0, tiled=True),
        )
        gain_a, query_w, key_w, value_w, output_w, gain_m, router_w, bias_table = weights_now
        gain_af = gain_a.astype(jnp.float32)
        gain_mf = gain_m.astype(jnp.float32)
        inputs = layer_in[step_index].astype(jnp.float32)
        scaled_a, inverse_a, normed_a = norm_forward(inputs, gain_af)
        normed_ab = normed_a.astype(jnp.bfloat16)
        queries = jnp.dot(normed_ab, query_w, preferred_element_type=jnp.float32).astype(
            jnp.bfloat16
        )
        keys_loc = jnp.dot(normed_ab, key_w, preferred_element_type=jnp.float32).astype(
            jnp.bfloat16
        )
        values_loc = jnp.dot(normed_ab, value_w, preferred_element_type=jnp.float32).astype(
            jnp.bfloat16
        )
        keys_all, values_all = (
            lax.all_gather(keys_loc, "expert", axis=0, tiled=True),
            lax.all_gather(values_loc, "expert", axis=0, tiled=True),
        )
        q_heads = split_heads(queries, heads)
        k_heads = split_heads(keys_all, heads)
        v_heads = split_heads(values_all, heads)
        bias = jnp.einsum(
            "qkb,bh->hqk", bucket_onehot, bias_table, preferred_element_type=jnp.float32
        )
        seg_all = segments[step_index]
        seg_here = lax.dynamic_slice_in_dim(seg_all, rank_here * tok_rows, tok_rows)
        allowed = causal & (seg_here[:, None] == seg_all[None, :])
        scores = score_block(q_heads, k_heads, bias, allowed, scale)
        top_score = jnp.max(scores, axis=-1, keepdims=True)
        lifted = jnp.exp(scores - top_score)
        total = jnp.sum(lifted, axis=-1, keepdims=True)
        log_total = top_score + jnp.log(total)
        probs_b = (lifted / total).astype(jnp.bfloat16)
        attended = merge_heads(
            jnp.einsum("hqk,hkd->hqd", probs_b, v_heads, preferred_element_type=jnp.float32)
        ).astype(jnp.bfloat16)
        resid = inputs + jnp.dot(attended, output_w, preferred_element_type=jnp.float32)
        scaled_m, inverse_m, normed_m = norm_forward(resid, gain_mf)
        normed_mb = normed_m.astype(jnp.bfloat16)
        logits = jnp.dot(normed_mb, router_w, preferred_element_type=jnp.float32)
        router_probs = jax.nn.softmax(logits, axis=-1)
        routes_now = routes[step_index]
        pick_first = (routes_now[:, 0:1] == expert_ids[None, :]).astype(jnp.float32)
        pick_second = (routes_now[:, 1:2] == expert_ids[None, :]).astype(jnp.float32)
        prob_first = jnp.sum(router_probs * pick_first, axis=-1)
        prob_second = jnp.sum(router_probs * pick_second, axis=-1)
        denom = prob_first + prob_second
        gate_first = prob_first / denom
        gate_second = prob_second / denom
        flat = routes_now.reshape(-1)
        flat_hot = (flat[:, None] == expert_ids[None, :]).astype(jnp.bfloat16)
        before = jnp.dot(earlier, flat_hot, preferred_element_type=jnp.float32)
        places = jnp.sum(before * flat_hot.astype(jnp.float32), axis=1).astype(jnp.int32)
        slot_pairs = (flat * capacity + places).reshape(tok_rows, 2)
        place_first = (slot_ids[:, None] == slot_pairs[None, :, 0]).astype(jnp.bfloat16)
        place_second = (slot_ids[:, None] == slot_pairs[None, :, 1]).astype(jnp.bfloat16)
        place_both = place_first + place_second
        outgoing = jnp.dot(place_both, normed_mb, preferred_element_type=jnp.float32).astype(
            jnp.bfloat16
        )
        outgoing = outgoing.reshape(group_size, local_experts, capacity, D)
        arrived_rows = lax.all_to_all(outgoing, "expert", split_axis=0, concat_axis=0, tiled=True)
        pre_act = jnp.einsum(
            "sjcd,jdf->sjcf", arrived_rows, w_expert_in, preferred_element_type=jnp.float32
        )
        post_act = jax.nn.gelu(pre_act).astype(jnp.bfloat16)
        produced = jnp.einsum(
            "sjcf,jfd->sjcd", post_act, w_expert_out, preferred_element_type=jnp.float32
        ).astype(jnp.bfloat16)
        produced, pre_act, post_act, arrived = (produced, pre_act, post_act, arrived_rows)
        returned = lax.all_to_all(
            produced, "expert", split_axis=0, concat_axis=0, tiled=True
        ).reshape(expert_count * capacity, D)
        got_first = jnp.einsum(
            "st,sd->td", place_first, returned, preferred_element_type=jnp.float32
        )
        got_second = jnp.einsum(
            "st,sd->td", place_second, returned, preferred_element_type=jnp.float32
        )
        result = resid + (gate_first[:, None] * got_first + gate_second[:, None] * got_second)
        outputs_list.append(result.astype(jnp.bfloat16))
        grad_top = out_grad[step_index].astype(jnp.float32)
        dgate_first = jnp.sum(grad_top * got_first, axis=-1)
        dgate_second = jnp.sum(grad_top * got_second, axis=-1)
        sent_first = (gate_first[:, None] * grad_top).astype(jnp.bfloat16)
        sent_second = (gate_second[:, None] * grad_top).astype(jnp.bfloat16)
        grad_slots = (
            jnp.dot(place_first, sent_first, preferred_element_type=jnp.float32)
            + jnp.dot(place_second, sent_second, preferred_element_type=jnp.float32)
        ).astype(jnp.bfloat16)
        grad_slots = grad_slots.reshape(group_size, local_experts, capacity, D)
        grad_arrived = lax.all_to_all(grad_slots, "expert", split_axis=0, concat_axis=0, tiled=True)
        grad_post = jnp.einsum(
            "sjcd,jfd->sjcf", grad_arrived, w_expert_out, preferred_element_type=jnp.float32
        )
        out_sum = out_sum + jnp.einsum(
            "sjcf,sjcd->jfd", post_act, grad_arrived, preferred_element_type=jnp.float32
        )
        grad_pre = jax.vjp(jax.nn.gelu, pre_act)[1](grad_post)[0].astype(jnp.bfloat16)
        in_sum = in_sum + jnp.einsum(
            "sjcd,sjcf->jdf", arrived, grad_pre, preferred_element_type=jnp.float32
        )
        grad_rows = jnp.einsum(
            "sjcf,jdf->sjcd", grad_pre, w_expert_in, preferred_element_type=jnp.float32
        ).astype(jnp.bfloat16)
        grad_back = lax.all_to_all(
            grad_rows, "expert", split_axis=0, concat_axis=0, tiled=True
        ).reshape(expert_count * capacity, D)
        grad_moe = jnp.einsum(
            "st,sd->td", place_both, grad_back, preferred_element_type=jnp.float32
        )
        weighted = dgate_first * gate_first + dgate_second * gate_second
        grad_pick = ((dgate_first - weighted) / denom)[:, None] * pick_first + (
            (dgate_second - weighted) / denom
        )[:, None] * pick_second
        grad_logits = router_probs * (
            grad_pick - jnp.sum(router_probs * grad_pick, axis=-1, keepdims=True)
        )
        normed_mf = normed_mb.astype(jnp.float32)
        grad_router_w = jnp.dot(normed_mf.T, grad_logits, precision=TOP_PRECISION)
        grad_moe = grad_moe + jnp.dot(
            grad_logits, router_w.astype(jnp.float32).T, precision=TOP_PRECISION
        )
        grad_resid_norm, grad_gain_m = norm_backward(grad_moe, scaled_m, inverse_m, gain_mf)
        grad_resid = grad_top + grad_resid_norm
        grad_branch = grad_resid.astype(jnp.bfloat16)
        grad_output_w = jnp.einsum(
            "td,te->de", attended, grad_branch, preferred_element_type=jnp.float32
        )
        grad_attended = jnp.einsum(
            "te,de->td", grad_branch, output_w, preferred_element_type=jnp.float32
        ).astype(jnp.bfloat16)
        grad_heads = split_heads(grad_attended, heads)
        scores_again = score_block(q_heads, k_heads, bias, allowed, scale)
        probs_again = jnp.exp(scores_again - log_total)
        probs_again_b = probs_again.astype(jnp.bfloat16)
        grad_probs = jnp.einsum(
            "hqd,hkd->hqk", grad_heads, v_heads, preferred_element_type=jnp.float32
        )
        row_delta = jnp.sum(probs_again * grad_probs, axis=-1, keepdims=True)
        grad_scores = probs_again * (grad_probs - row_delta)
        grad_table = jnp.einsum(
            "hqk,qkb->bh", grad_scores, bucket_onehot.astype(jnp.float32), precision=TOP_PRECISION
        )
        grad_scores_b = (grad_scores * scale).astype(jnp.bfloat16)
        grad_q_heads = jnp.einsum(
            "hqk,hkd->hqd", grad_scores_b, k_heads, preferred_element_type=jnp.float32
        )
        grad_v_heads = jnp.einsum(
            "hqk,hqd->hkd", probs_again_b, grad_heads, preferred_element_type=jnp.float32
        )
        grad_k_heads = jnp.einsum(
            "hqk,hqd->hkd", grad_scores_b, q_heads, preferred_element_type=jnp.float32
        )
        grad_keys, grad_values = (
            lax.psum_scatter(merge_heads(grad_k_heads), "expert", scatter_dimension=0, tiled=True),
            lax.psum_scatter(merge_heads(grad_v_heads), "expert", scatter_dimension=0, tiled=True),
        )
        grad_queries_b = merge_heads(grad_q_heads).astype(jnp.bfloat16)
        grad_keys_b = grad_keys.astype(jnp.bfloat16)
        grad_values_b = grad_values.astype(jnp.bfloat16)
        grad_query_w = jnp.einsum(
            "td,te->de", normed_ab, grad_queries_b, preferred_element_type=jnp.float32
        )
        grad_key_w = jnp.einsum(
            "td,te->de", normed_ab, grad_keys_b, preferred_element_type=jnp.float32
        )
        grad_value_w = jnp.einsum(
            "td,te->de", normed_ab, grad_values_b, preferred_element_type=jnp.float32
        )
        grad_normed = (
            jnp.einsum("te,de->td", grad_queries_b, query_w, preferred_element_type=jnp.float32)
            + jnp.einsum("te,de->td", grad_keys_b, key_w, preferred_element_type=jnp.float32)
            + jnp.einsum("te,de->td", grad_values_b, value_w, preferred_element_type=jnp.float32)
        )
        grad_in_norm, grad_gain_a = norm_backward(grad_normed, scaled_a, inverse_a, gain_af)
        grads_list.append(grad_resid + grad_in_norm)
        parts_now = (
            grad_gain_a,
            grad_query_w,
            grad_key_w,
            grad_value_w,
            grad_output_w,
            grad_gain_m,
            grad_router_w,
            grad_table,
        )
        dense_sums = [running + addend for running, addend in zip(dense_sums, parts_now)]
    sum_gain_a, sum_query, sum_key, sum_value, sum_output, sum_gain_m, sum_router, sum_table = (
        dense_sums
    )
    summed = lax.psum(
        (sum_gain_a, sum_query, sum_key, sum_value, sum_output, sum_gain_m, sum_router, sum_table),
        "expert",
    )
    (
        full_gain_a,
        full_query,
        full_key,
        full_value,
        full_output,
        full_gain_m,
        full_router,
        full_table,
    ) = summed
    shares = (
        lax.psum_scatter(full_gain_a, "dp", scatter_dimension=0, tiled=True),
        lax.psum_scatter(full_query, "dp", scatter_dimension=0, tiled=True),
        lax.psum_scatter(full_key, "dp", scatter_dimension=0, tiled=True),
        lax.psum_scatter(full_value, "dp", scatter_dimension=0, tiled=True),
        lax.psum_scatter(full_output, "dp", scatter_dimension=0, tiled=True),
        lax.psum_scatter(full_gain_m, "dp", scatter_dimension=0, tiled=True),
        lax.psum_scatter(full_router, "dp", scatter_dimension=0, tiled=True),
        lax.psum_scatter(full_table, "dp", scatter_dimension=0, tiled=True),
    )
    expert_in_grad, expert_out_grad = (
        lax.psum(in_sum.astype(jnp.bfloat16), "dp").astype(jnp.float32),
        lax.psum(out_sum.astype(jnp.bfloat16), "dp").astype(jnp.float32),
    )
    layer_out = jnp.stack(outputs_list)
    grad_in = jnp.stack(grads_list)
    return (
        layer_out,
        grad_in,
        shares[0],
        shares[1],
        shares[2],
        shares[3],
        shares[4],
        shares[5],
        shares[6],
        shares[7],
        expert_in_grad,
        expert_out_grad,
    )


F32 = jnp.float32
BF16 = jnp.bfloat16
TILE = 256
VMEM_LIMIT = 60 * 2**20


def nn(left, right):
    return lax.dot_general(left, right, (((1,), (0,)), ((), ())), preferred_element_type=F32)


def nt(left, right):
    return lax.dot_general(left, right, (((1,), (1,)), ((), ())), preferred_element_type=F32)


def tn(left, right):
    return lax.dot_general(left, right, (((0,), (0,)), ((), ())), preferred_element_type=F32)


def call(body, name, grid, ins, outs, out_shapes, scratch=(), flops=0, nbytes=0, collective=None):
    extra = {} if collective is None else {"collective_id": collective, "has_side_effects": True}
    return pl.pallas_call(
        body,
        grid=grid,
        in_specs=ins,
        out_specs=outs,
        out_shape=out_shapes,
        scratch_shapes=list(scratch),
        compiler_params=pltpu.CompilerParams(
            dimension_semantics=("arbitrary",) * len(grid), vmem_limit_bytes=VMEM_LIMIT, **extra
        ),
        cost_estimate=pl.CostEstimate(flops=flops, bytes_accessed=nbytes, transcendentals=0),
        name=name,
    )


def whole(shape):
    zeros = (0,) * len(shape)
    return pl.BlockSpec(shape, lambda *_: zeros)


def rows(width, tile=TILE):
    return pl.BlockSpec((tile, width), lambda i: (i, 0))


MESH = pl.DeviceIdType.MESH
ANY = pl.BlockSpec(memory_space=pl.ANY)


def neighbours():
    me = lax.axis_index("dp")
    core = me + 1 - 2 * (me % 2)
    along_x = me + 2 - 4 * ((me // 2) % 2)
    along_y = me + 4 - 8 * (me // 4)
    across = along_x + 4 - 8 * (me // 4)
    return me, core, along_x, along_y, across


def meet(devices):
    barrier = pltpu.get_barrier_semaphore()
    for device in devices:
        pl.semaphore_signal(barrier, inc=1, device_id=device, device_id_type=MESH)
    pl.semaphore_wait(barrier, len(devices))


def plane_devices():
    place = lax.axis_index("expert")
    _, core, along_x, along_y, _ = neighbours()
    return [(core, place), (along_x, place), (along_y, place)]


GATHER_COPIES = 14


def gather_copies(first, second, source_first, source_second, send, recv, local):
    place = lax.axis_index("expert")
    me, core, along_x, along_y, across = neighbours()

    def remote(index, source, target, device):
        return pltpu.make_async_remote_copy(
            src_ref=source,
            dst_ref=target,
            send_sem=send.at[index],
            recv_sem=recv.at[index],
            device_id=(device, place),
            device_id_type=MESH,
        )

    own = [
        pltpu.make_async_copy(source_first, first.at[me], local.at[0]),
        pltpu.make_async_copy(source_second, second.at[me], local.at[1]),
    ]
    near = [
        remote(0, source_first, first.at[me], along_x),
        remote(1, source_second, second.at[me], along_y),
        remote(2, source_first, first.at[me], along_y),
        remote(3, source_second, second.at[me], along_x),
    ]
    paired = [
        remote(4, source_first, first.at[me], core),
        remote(5, source_second, second.at[me], core),
    ]
    far = [
        remote(6, first.at[along_x], first.at[along_x], along_y),
        remote(7, second.at[along_y], second.at[along_y], along_x),
    ]
    paired_near = [
        remote(8, first.at[along_x], first.at[along_x], core),
        remote(9, second.at[along_y], second.at[along_y], core),
        remote(10, first.at[along_y], first.at[along_y], core),
        remote(11, second.at[along_x], second.at[along_x], core),
    ]
    paired_far = [
        remote(12, first.at[across], first.at[across], core),
        remote(13, second.at[across], second.at[across], core),
    ]

    def start0():
        for copy in near + paired + own:
            copy.start()

    def start1():
        near[0].wait_recv()
        far[0].start()
        near[1].wait_recv()
        far[1].start()
        near[2].wait_recv()
        near[3].wait_recv()
        for copy in paired_near:
            copy.start()

    def start2():
        for copy, onward in zip(far, paired_far):
            copy.wait_recv()
            onward.start()

    def finish():
        for copy in own:
            copy.wait()
        for copy in paired + paired_near + paired_far:
            copy.wait_recv()
        for copy in near + paired + far + paired_near + paired_far:
            copy.wait_send()

    return start0, start1, start2, finish


def gather_sems():
    return [
        pltpu.SemaphoreType.DMA((GATHER_COPIES,)),
        pltpu.SemaphoreType.DMA((GATHER_COPIES,)),
        pltpu.SemaphoreType.DMA((2,)),
    ]


def sds(shape, dtype):
    return jax.ShapeDtypeStruct(shape, dtype)


def partner(place, k):
    return 2 * lax.rem(place // 2 + k // 2, 2) + lax.rem(lax.rem(place, 2) + k % 2, 2)


ORDER = (1, 0, 2, 3)


def place_devices(group):
    me = lax.axis_index("dp")
    place = lax.axis_index("expert")
    return [(me, lax.rem(place + k, group)) for k in range(1, group)]


def along_axis(source, target, send, recv, place):
    return pltpu.make_async_remote_copy(
        src_ref=source,
        dst_ref=target,
        send_sem=send,
        recv_sem=recv,
        device_id=(lax.axis_index("dp"), place),
        device_id_type=MESH,
    )


def swap_copies(source, target, send, recv, group):
    place = lax.axis_index("expert")
    copies = []
    for k in range(1, group):
        other = lax.rem(place + k, group)
        copies.append(along_axis(source.at[other], target.at[place], send.at[k], recv.at[k], other))
    return copies


def slice_copies(w_in, w_out, first, second, send, recv, base, place):
    me = lax.axis_index("dp")
    chunk = (first if second is None else second).shape[1]
    here = pl.ds(pl.multiple_of(me * chunk, 128), chunk)
    pieces = []
    if first is not None:
        pieces.append((w_in.at[0, :, here], first))
    if second is not None:
        pieces += [
            (w_out.at[0, here, pl.ds(at, chunk)], second.at[pl.ds(at, chunk)]) for at in (0, chunk)
        ]
    return [
        along_axis(source, goal, send.at[base + i], recv.at[base + i], place)
        for i, (source, goal) in enumerate(pieces)
    ]


REDUCE_COPIES = 10


def reduce_copies(terms, own, pair, inbox, send, recv, local, emit):
    place = lax.axis_index("expert")
    me, core, along_x, along_y, across = neighbours()
    targets = (across, along_x, along_y, me)

    def remote(index, source, target, device):
        return pltpu.make_async_remote_copy(
            src_ref=source,
            dst_ref=target,
            send_sem=send.at[index],
            recv_sem=recv.at[index],
            device_id=(device, place),
            device_id_type=MESH,
        )

    loads = [pltpu.make_async_copy(terms.at[t], own.at[q], local.at[q]) for q, t in enumerate(targets)]
    pairs = [
        remote(q, terms.at[t + 1 - 2 * lax.rem(t, 2)], pair.at[q], core) for q, t in enumerate(targets)
    ]
    far_first = remote(4, own.at[0, 0], inbox.at[0], along_x)
    far_second = remote(5, own.at[0, 1], inbox.at[1], along_y)
    near_first = remote(6, own.at[1, 0], inbox.at[2], along_x)
    near_second = remote(7, own.at[2, 1], inbox.at[3], along_y)
    late_first = remote(8, own.at[2, 0], inbox.at[4], along_y)
    late_second = remote(9, own.at[1, 1], inbox.at[5], along_x)

    def merge(q):
        loads[q].wait()
        pairs[q].wait_recv()
        own[q] = own[q] + pair[q]

    def start():
        pairs[0].start()
        for copy in loads:
            copy.start()

    def far():
        merge(0)
        far_first.start()
        far_second.start()
        for copy in pairs[1:]:
            copy.start()

    def near():
        merge(1)
        near_first.start()
        merge(2)
        near_second.start()

    def late():
        far_first.wait_recv()
        own[2, 0] = own[2, 0] + inbox[0]
        late_first.start()
        far_second.wait_recv()
        own[1, 1] = own[1, 1] + inbox[1]
        late_second.start()

    def finish():
        merge(3)
        for copy in (near_first, near_second, late_first, late_second):
            copy.wait_recv()
        emit(0, own[3, 0].astype(F32) + inbox[2].astype(F32) + inbox[4].astype(F32))
        emit(1, own[3, 1].astype(F32) + inbox[3].astype(F32) + inbox[5].astype(F32))
        for copy in pairs + [far_first, far_second, near_first, near_second, late_first, late_second]:
            copy.wait_send()

    return start, far, near, late, finish


def reduce_scratch(shape):
    half = shape[1:]
    return [
        pltpu.VMEM((4, *shape), BF16),
        pltpu.VMEM((4, *shape), BF16),
        pltpu.VMEM((6, *half), BF16),
        pltpu.SemaphoreType.DMA((REDUCE_COPIES,)),
        pltpu.SemaphoreType.DMA((REDUCE_COPIES,)),
        pltpu.SemaphoreType.DMA((4,)),
    ]


def weight(slots_ref, index, share):
    return slots_ref[:, index * share : (index + 1) * share, :].reshape(-1, D)


def front_kernel(
    x_ref, grad_ref, routes_ref, w_in_ref, w_out_ref, wq_ref, wk_ref, wv_ref, wo_ref, small_ref, buckets_ref, seg_ref,
    x_out, grad_out, c0_out, c1_out, first_out, second_out, a_out, q_out, k_out, v_out, o_out, table_out,
    h_out, n_out, gate_out, pr_out, gather_first, gather_second, piece_out, params_ref, across_ref, down_ref, lse_ref,
    land, routes_land, first, second, stage_first, stage_second,
    a_ref, q_ref, k_ref, v_ref, o_ref, table_ref, h_ref, n_ref, gate_ref, pr_ref, line_ref,
    x_send, x_recv, r_send, r_recv, g_send, g_recv, p_send, p_recv, keep, own_local, out_sem,
    send, recv, local, send_w, recv_w, local_w,
    *, group, share, heads, experts, scale, width
):
    me = lax.axis_index("dp")
    place = lax.axis_index("expert")
    pieces = [
        (wq_ref, stage_first.at[pl.ds(0, share)]),
        (wk_ref, stage_first.at[pl.ds(share, share)]),
        (wv_ref, stage_second.at[pl.ds(0, share)]),
        (wo_ref, stage_second.at[pl.ds(share, share)]),
    ]
    staged = [pltpu.make_async_copy(src, dst, own_local.at[i]) for i, (src, dst) in enumerate(pieces)]
    for copy in staged:
        copy.start()
    small = small_ref[...].astype(F32)
    line = lax.broadcasted_iota(jnp.int32, small.shape, 0)
    placed = jnp.where(line < 16, pltpu.roll(small, me * share, 1), pltpu.roll(small, me * 4, 1))
    stage_second[2 * share :, :] = placed.astype(BF16)
    meet(plane_devices() + place_devices(group))
    moves = swap_copies(routes_ref, routes_land, r_send, r_recv, group)
    moves_x = swap_copies(x_ref, land, x_send, x_recv, group)
    moves_g = swap_copies(grad_ref, grad_out, g_send, g_recv, group)
    slices = slice_copies(w_in_ref, w_out_ref, piece_out.at[0], piece_out.at[1], p_send, p_recv, 0, partner(place, 1))
    distant = slice_copies(w_in_ref, w_out_ref, c0_out, c1_out, p_send, p_recv, 3, partner(place, 2))
    kept = [
        pltpu.make_async_copy(routes_ref.at[place], routes_land.at[place], keep.at[0]),
        pltpu.make_async_copy(x_ref.at[place], land.at[place], keep.at[1]),
        pltpu.make_async_copy(grad_ref.at[place], grad_out.at[place], keep.at[2]),
    ]
    for copy in moves + moves_x + kept:
        copy.start()
    for copy in staged:
        copy.wait()
    start0, start1, start2, finish = gather_copies(first, second, stage_first, stage_second, send, recv, local)
    start0()

    kept[0].wait()
    for copy in moves:
        copy.wait_recv()
    seq = down_ref.shape[0]
    row_id = lax.broadcasted_iota(jnp.int32, (8, routes_land.shape[2]), 0)
    holder = jnp.full(row_id.shape, -1, jnp.int32)
    for k in range(experts):
        holder = jnp.where(row_id == k, partner(place, ORDER[k]), holder)
    named = []
    for p in range(group):
        picks = [routes_land[p, c : c + 1, :] == holder for c in range(2)]
        named.append((picks[0] | picks[1]).astype(F32))
    named = jnp.concatenate(named, axis=1)
    earlier = lax.broadcasted_iota(jnp.int32, (seq, seq), 0) < lax.broadcasted_iota(jnp.int32, (seq, seq), 1)
    before = nn(named.astype(BF16), earlier.astype(F32).astype(BF16))
    pos = jnp.where(named > 0, before, -1.0)
    which = lax.broadcasted_iota(jnp.int32, seg_ref.shape, 0)
    segs = jnp.where(which == place, seg_ref[...], 0).astype(F32).sum(axis=0, keepdims=True)
    stack = jnp.concatenate([pos, jnp.broadcast_to(segs, (8, seq))], axis=0)
    across_ref[...] = stack.astype(jnp.int32)
    filled = jnp.concatenate([stack, jnp.full((112, seq), -1.0, F32)], axis=0)
    down_ref[...] = filled.T.astype(jnp.int32)

    start1()
    start2()
    finish()
    out_copies = []

    def put(source, target):
        out_copies.append(pltpu.make_async_copy(source, target, out_sem.at[len(out_copies)]))
        out_copies[-1].start()

    put(first, first_out)
    put(second, second_out)
    params = second[0, 2 * share :, :].astype(F32)
    for slot in range(1, second.shape[0]):
        params = params + second[slot, 2 * share :, :].astype(F32)
    turned = []
    for k in range(experts):
        wanted = partner(place, ORDER[k])
        picked = jnp.zeros((1, D), F32)
        for e in range(experts):
            picked = picked + params[8 + e : 9 + e, :] * jnp.where(wanted == e, 1.0, 0.0)
        turned.append(picked)
    params_ref[...] = params
    for k in range(experts):
        params_ref[8 + k : 9 + k, :] = turned[k]
    hot = (lax.broadcasted_iota(jnp.int32, (128, seq), 0) == buckets_ref[...]).astype(F32).astype(BF16)
    lines = nn(params[16:32, :128].astype(BF16), hot)
    for h in range(heads):
        line_ref[h] = lines[h : h + 1, :]

    kept[1].wait()
    for copy in moves_x:
        copy.wait_recv()
    for copy in slices + distant:
        copy.start()
    put(land, x_out)
    part = land.shape[1]
    for p in range(group):
        here = slice(p * part, (p + 1) * part)
        x = land[p].astype(F32)
        inverse = lax.rsqrt(jnp.mean(x * x, axis=-1, keepdims=True) + EPSILON)
        normed = (x * inverse * params[0:1, :]).astype(BF16)
        a_ref[here, :] = normed
        q = nn(normed, weight(first, 0, share)).astype(BF16)
        q_ref[here, :] = (q.astype(F32) * scale).astype(BF16)
        k_ref[here, :] = nn(normed, weight(first, 1, share)).astype(BF16)
        v_ref[here, :] = nn(normed, weight(second, 0, share)).astype(BF16)
    for source, target in ((a_ref, a_out), (q_ref, q_out), (k_ref, k_out), (v_ref, v_out)):
        put(source, target)
    gather = gather_copies(
        gather_first, gather_second, piece_out.at[0], piece_out.at[1], send_w, recv_w, local_w
    )
    pairs = 128 // width
    count = heads // pairs

    def table_copy(n):
        heads_here = pl.ds(n * pairs, pairs)
        return pltpu.make_async_copy(table_ref.at[heads_here], table_out.at[heads_here], keep.at[3 + n])

    def attend(n, carry):
        @pl.when(n == 4)
        def _():
            for copy in slices:
                copy.wait_recv()
            gather[0]()
            for copy in moves_g:
                copy.start()

        attend_pair(n, q_ref, k_ref, v_ref, line_ref, table_ref, down_ref, across_ref, o_ref, lse_ref, width)
        table_copy(n).start()
        return carry

    lax.fori_loop(0, count, attend, 0)
    put(o_ref, o_out)

    def route(i, carry):
        here = pl.ds(pl.multiple_of(i * TILE, TILE), TILE)
        route_rows(
            land[i], o_ref[here, :], second, params_ref, down_ref, h_ref, n_ref, gate_ref, pr_ref, here, share, experts
        )
        return carry

    lax.fori_loop(0, group, route, 0)
    for source, target in ((h_ref, h_out), (n_ref, n_out), (gate_ref, gate_out), (pr_ref, pr_out)):
        put(source, target)
    gather[1]()
    gather[2]()
    kept[2].wait()
    for copy in distant + moves_g:
        copy.wait_recv()
    for copy in moves + moves_x + slices + distant + moves_g:
        copy.wait_send()
    gather[3]()
    for n in range(count):
        table_copy(n).wait()
    for copy in out_copies:
        copy.wait()


def masked_scores(k, q, table_ref, head, i, j, seg_col, seg_row):
    scores = nt(k, q) + table_ref[head, i - j].astype(F32)
    allowed = seg_col == seg_row
    if i == j:
        key_at = lax.broadcasted_iota(jnp.int32, (TILE, TILE), 0)
        query_at = lax.broadcasted_iota(jnp.int32, (TILE, TILE), 1)
        allowed = allowed & (key_at <= query_at)
    return jnp.where(allowed, scores, MASKED)


def route_rows(x, o, second_ref, params_ref, down_ref, h_ref, a_ref, gate_ref, pr_ref, here, share, experts):
    h1 = x.astype(F32) + nn(o, weight(second_ref, 1, share))
    h_ref[here, :] = h1
    inverse = lax.rsqrt(jnp.mean(h1 * h1, axis=-1, keepdims=True) + EPSILON)
    normed = (h1 * inverse * params_ref[1:2, :]).astype(BF16)
    a_ref[here, :] = normed
    router = jnp.concatenate([params_ref[8:16, :], jnp.zeros((120, D), F32)], axis=0).astype(BF16)
    logits = nt(normed, router)
    lane = lax.broadcasted_iota(jnp.int32, logits.shape, 1)
    logits = jnp.where(lane < experts, logits, MASKED)
    lifted = jnp.exp(logits - logits.max(axis=-1, keepdims=True))
    pr = lifted / lifted.sum(axis=-1, keepdims=True)
    named = (down_ref[here, :] >= 0) & (lane < experts)
    picked = jnp.where(named, pr, 0.0)
    pr_ref[here, :] = pr
    gate_ref[here, :] = picked / picked.sum(axis=-1, keepdims=True)


def attend_pair(n, q_ref, k_ref, v_ref, line_ref, table_ref, down_ref, across_ref, o_ref, lse_ref, width):
    columns = pl.ds(pl.multiple_of(n * 128, 128), 128)
    heads = 128 // width
    for h in range(heads):
        row = line_ref[n * heads + h]
        for gap in range(table_ref.shape[1]):
            ahead = row[:, gap * TILE : (gap + 1) * TILE]
            back = row[:, (gap - 1) * TILE : gap * TILE] if gap else jnp.zeros_like(ahead)
            grid = jnp.broadcast_to(jnp.concatenate([ahead, back], axis=1), (TILE, 2 * TILE))
            grid = pltpu.roll(grid, 0, 1, stride=1, stride_axis=0)
            table_ref[n * heads + h, gap] = grid[:, :TILE].astype(BF16)
    q_all, k_all, v_all = q_ref[:, columns], k_ref[:, columns], v_ref[:, columns]
    blocks = q_all.shape[0] // TILE
    turned = [v_all[:, h * width : (h + 1) * width].T for h in range(heads)]
    for i in range(blocks):
        here = slice(i * TILE, (i + 1) * TILE)
        outs = []
        for h in range(heads):
            lanes = slice(h * width, (h + 1) * width)
            q = q_all[here, lanes]
            pieces = []
            for j in range(i + 1):
                there = slice(j * TILE, (j + 1) * TILE)
                pieces.append(
                    masked_scores(
                        k_all[there, lanes], q, table_ref, n * heads + h, i, j, down_ref[there, 8:9],
                        across_ref[8:9, here]
                    )
                )
            top = pieces[0].max(axis=0, keepdims=True)
            for piece in pieces[1:]:
                top = jnp.maximum(top, piece.max(axis=0, keepdims=True))
            total = jnp.zeros_like(top)
            acc = jnp.zeros((width, TILE), F32)
            for j, piece in enumerate(pieces):
                lifted = jnp.exp(piece - top)
                total = total + lifted.sum(axis=0, keepdims=True)
                acc = acc + nn(turned[h][:, j * TILE : (j + 1) * TILE], lifted.astype(BF16))
            outs.append(acc / total)
            lse_ref[n, h : h + 1, here] = top + jnp.log(total)
        o_ref[here, columns] = jnp.concatenate(outs, axis=0).T.astype(BF16)


def attend_back_kernel(
    q_ref, k_ref, v_ref, do_ref, table_ref, down_ref, across_ref, lse_ref, a_ref, dwo_ref, dgain_m_ref, drouter_ref, buckets_ref,
    passed, terms,
    dq_ref, dk_ref, dv_ref, pack, sums_ref, pass_out,
    dist_ref, grads_ref, sum_ref, dk_sum, dv_sum, turned_a, p_send, p_recv, own, pair, inbox, send, recv, local, *, width, scale, group, share, experts
):
    step = pl.program_id(0)
    last = pl.num_programs(0) - 1
    place = lax.axis_index("expert")

    def emit(half, value):
        sums_ref[half] = value.astype(BF16)

    start, far, near, late, finish = reduce_copies(terms.at[1], own, pair, inbox, send, recv, local, emit)
    hop = along_axis(passed, pass_out, p_send.at[0], p_recv.at[0], partner(place, 3))

    @pl.when(step == 0)
    def _():
        meet(plane_devices() + [(lax.axis_index("dp"), partner(place, 3))])
        start()
        hop.start()
        far()
        turned_a[...] = a_ref[...].T
        near()

    @pl.when(step == 3)
    def _():
        late()

    blocks = q_ref.shape[0] // TILE
    heads = q_ref.shape[1] // width
    turned = [k_ref[:, h * width : (h + 1) * width].T for h in range(heads)]
    for h in range(heads):
        dist_ref[step * heads + h] = jnp.zeros(dist_ref.shape[1:], F32)
    for h in range(heads):
        lanes = slice(h * width, (h + 1) * width)
        for i in range(blocks):
            here = slice(i * TILE, (i + 1) * TILE)
            q = q_ref[here, lanes]
            do = do_ref[here, lanes]
            lse = lse_ref[0, h : h + 1, here]
            probs, dprobs = [], []
            delta = jnp.zeros((1, TILE), F32)
            for j in range(i + 1):
                there = slice(j * TILE, (j + 1) * TILE)
                scores = masked_scores(
                    k_ref[there, lanes], q, table_ref, h, i, j, down_ref[there, 8:9], across_ref[8:9, here]
                )
                p = jnp.exp(scores - lse)
                dp = nt(v_ref[there, lanes], do)
                delta = delta + (p * dp).sum(axis=0, keepdims=True)
                probs.append(p)
                dprobs.append(dp)
            turned_dq = jnp.zeros((width, TILE), F32)
            for j in range(i + 1):
                there = slice(j * TILE, (j + 1) * TILE)
                ds = probs[j] * (dprobs[j] - delta)
                low = ds.astype(BF16)
                dv = nn(probs[j].astype(BF16), do)
                dk = nn(low, q)
                if i == j:
                    dv_sum[there, lanes] = dv
                    dk_sum[there, lanes] = dk
                else:
                    dv_sum[there, lanes] += dv
                    dk_sum[there, lanes] += dk
                turned_dq = turned_dq + nn(turned[h][:, there], low)
                if j == 0:
                    sum_ref[i - j] = ds
                else:
                    sum_ref[i - j] += ds
            dq_ref[here, lanes] = (turned_dq * scale).T.astype(BF16)
        for gap in range(blocks):
            part = sum_ref[gap]
            part = jnp.concatenate([part, jnp.zeros_like(part)], axis=1)
            half = TILE // 2
            while half:
                part = part[:half] + pltpu.roll(part[half : 2 * half], 2 * TILE - half, 1)
                half //= 2
            dist_ref[step * heads + h, :, gap * TILE : (gap + 1) * TILE] += part[:, :TILE]
            if gap:
                dist_ref[step * heads + h, :, (gap - 1) * TILE : gap * TILE] += part[:, TILE:]
    dk_ref[...] = dk_sum[...].astype(BF16)
    dv_ref[...] = dv_sum[...].astype(BF16)

    grads = jnp.concatenate([dq_ref[...], dk_ref[...], dv_ref[...]], axis=1)
    sums = nn(turned_a[...], grads).astype(BF16)
    for index in range(3):
        grads_ref[step, :, index * 128 : (index + 1) * 128] = sums[:, index * 128 : (index + 1) * 128]

    @pl.when(step == last)
    def _():
        for index, (half, at) in enumerate(((0, 0), (0, share), (1, 0))):
            for n in range(grads_ref.shape[0]):
                part = grads_ref[n, :, index * 128 : (index + 1) * 128]
                pack[:, half, at : at + share, n * 128 : (n + 1) * 128] = part.reshape(-1, share, 128)
        pack[:, 1, share : 2 * share, :] = dwo_ref[...].astype(BF16).reshape(-1, share, D)
        seq = dist_ref.shape[2]
        hot = (lax.broadcasted_iota(jnp.int32, (128, seq), 0) == buckets_ref[...]).astype(F32).astype(BF16)
        left = jnp.concatenate([dist_ref[h] for h in range(dist_ref.shape[0])], axis=0)
        table = jnp.zeros((left.shape[0], 128), F32)
        for _ in range(3):
            low = left.astype(BF16)
            left = left - low.astype(F32)
            table = table + nt(low, hot)
        rows_out = [jnp.zeros((1, D), F32), dgain_m_ref[...], jnp.zeros((6, D), F32)]
        for e in range(experts):
            picked = jnp.zeros((1, D), F32)
            for k in range(experts):
                picked = picked + drouter_ref[k : k + 1, :] * jnp.where(partner(place, ORDER[k]) == e, 1.0, 0.0)
            rows_out.append(picked)
        rows_out.append(jnp.zeros((8 - experts, D), F32))
        rows_out.append(jnp.concatenate([table, jnp.zeros((table.shape[0], D - 128), F32)], axis=1))
        rows_out.append(jnp.zeros((16 - table.shape[0], D), F32))
        small = jnp.concatenate(rows_out, axis=0).astype(BF16)
        for slot in range(pack.shape[0]):
            pack[slot, 0, 2 * share :, :] = small
            pack[slot, 1, 2 * share :, :] = jnp.zeros_like(small)
        finish()
        hop.wait()


def experts_kernel(
    a_ref, g_ref, gate_ref, across_ref, first_a, second_a, piece_c0, piece_c1, w_in_ref, w_out_ref,
    eo_ref, da_ref, dw_out, sum_a, sum_c, piece_b, first_c, second_c, first_b, second_b,
    rows_a, turned_a, rows_d, eo_sum, da_sum, w_in_two, w_out_two, dw_two, total_a,
    w_sem, dw_sem, hop_send, hop_recv, save, free, own, pair, inbox, send_a, recv_a, local_a,
    send_c, recv_c, local_c, *gather, capacity, group, shards
):
    step = pl.program_id(0)
    last = pl.num_programs(0) - 1
    steps = shards // 2
    turn = step // steps
    slot = lax.rem(step, 2)
    place = lax.axis_index("expert")
    chunk = w_in_two.shape[3]

    def loads(at, which):
        c = lax.rem(at, steps)
        two = lax.rem(at, 2)
        if which != 1:
            first, second = {0: (first_a, second_a), 2: (first_c, second_c), 3: (first_b, second_b)}[which]
            both = pl.ds(2 * c, 2)
            return [
                pltpu.make_async_copy(first.at[both], w_in_two.at[two], w_sem.at[0, two]),
                pltpu.make_async_copy(second.at[both], w_out_two.at[two], w_sem.at[1, two]),
            ]
        copies = []
        for h in range(2):
            cols = pl.ds(pl.multiple_of((2 * c + h) * chunk, 128), chunk)
            copies.append(
                pltpu.make_async_copy(w_in_ref.at[0, :, cols], w_in_two.at[two, h], w_sem.at[3 * h, two])
            )
            for l in range(2):
                lanes = pl.ds(l * chunk, chunk)
                copies.append(
                    pltpu.make_async_copy(
                        w_out_ref.at[0, cols, lanes], w_out_two.at[two, h, lanes], w_sem.at[3 * h + 1 + l, two]
                    )
                )
        return copies

    def each_turn(at, action):
        for which in range(group):
            @pl.when(at // steps == which)
            def _(which=which):
                for copy in loads(at, which):
                    action(copy)

    def saved(at):
        two = lax.rem(at, 2)
        return pltpu.make_async_copy(
            dw_two.at[two], dw_out.at[at // steps, pl.ds(2 * lax.rem(at, steps), 2)], dw_sem.at[two]
        )

    gather_c = gather_copies(first_c, second_c, piece_c0, piece_c1, *gather[:3])
    gather_b = gather_copies(first_b, second_b, piece_b.at[0], piece_b.at[1], *gather[3:])
    relays = [
        along_axis(piece, piece_b.at[i], hop_send.at[2 * i], hop_recv.at[2 * i], partner(place, 1))
        for i, piece in enumerate((piece_c0, piece_c1))
    ]
    hop = along_axis(total_a, sum_a, hop_send.at[1], hop_recv.at[1], partner(place, 1))
    keep = pltpu.make_async_copy(own.at[3], sum_c, save.at[0])

    def emit_a(half, value):
        total_a[half] = value.astype(BF16)

    def emit_c(half, value):
        own[3, half] = value.astype(BF16)

    reduce_a = reduce_copies(dw_out.at[0], own, pair, inbox, send_a, recv_a, local_a, emit_a)
    reduce_c = reduce_copies(dw_out.at[2], own, pair, inbox, send_c, recv_c, local_c, emit_c)

    @pl.when(step == 0)
    def _():
        meet(plane_devices() + [(lax.axis_index("dp"), partner(place, 1))])
        gather_c[0]()
        for copy in relays:
            copy.start()
        each_turn(step, lambda copy: copy.start())

    def release():
        for device in plane_devices():
            pl.semaphore_signal(free, inc=1, device_id=device, device_id_type=MESH)

    def claim():
        pl.semaphore_wait(free, len(plane_devices()))

    schedule = {
        3: [gather_c[1]],
        5: [relays[0].wait, relays[1].wait, gather_b[0]],
        6: [gather_c[2]],
        7: [gather_c[3], reduce_a[0]],
        8: [gather_b[1], reduce_a[1]],
        9: [reduce_a[2]],
        12: [reduce_a[3]],
        15: [reduce_a[4], release, hop.start, claim, reduce_c[0], reduce_c[1], reduce_c[2]],
    }
    for when, actions in schedule.items():
        @pl.when(step == when)
        def _(actions=actions):
            for action in actions:
                action()

    @pl.when(lax.rem(step, steps) == 0)
    def _():
        tokens = a_ref.shape[0]
        places = lax.broadcasted_iota(jnp.int32, (capacity, tokens), 0)
        pick = (across_ref[pl.ds(turn, 1), :] == places).astype(BF16)
        rows = nn(pick, a_ref[...]).astype(BF16)
        rows_a[...] = rows
        turned_a[...] = rows.T
        lane = lax.broadcasted_iota(jnp.int32, gate_ref.shape, 1)
        gate = jnp.sum(jnp.where(lane == turn, gate_ref[...], 0.0), axis=-1, keepdims=True)
        rows_d[...] = nn(pick, (gate * g_ref[...].astype(F32)).astype(BF16)).astype(BF16)
        eo_sum[...] = jnp.zeros_like(eo_sum)
        da_sum[...] = jnp.zeros_like(da_sum)

    each_turn(step, lambda copy: copy.wait())
    ahead = step + 1

    @pl.when((step < last) & (ahead != 3 * steps))
    def _():
        each_turn(ahead, lambda copy: copy.start())

    @pl.when(step > 1)
    def _():
        saved(step - 2).wait()

    d = rows_d[...]
    w_in = jnp.concatenate([w_in_two[slot, h] for h in range(2)], axis=1)
    w_out = jnp.concatenate(
        [
            jnp.concatenate([w_out_two[slot, h, :chunk], w_out_two[slot, h, chunk:]], axis=1)
            for h in range(2)
        ],
        axis=0,
    )
    u = nn(rows_a[...], w_in)
    square = u * u
    t = jnp.tanh(GELU_A * u * (1.0 + GELU_B * square))
    half = 0.5 * (1.0 + t)
    z = (u * half).astype(BF16)
    eo_sum[...] += nn(z, w_out)
    dw_last = tn(z, d).astype(BF16)
    slope = half + (0.5 * GELU_A) * u * (1.0 - t * t) * (1.0 + 3.0 * GELU_B * square)
    du = (nt(d, w_out) * slope).astype(BF16)
    da_sum[...] += nt(du, w_in)
    dw_first = nn(turned_a[...], du).astype(BF16)
    for h in range(2):
        here = slice(h * chunk, (h + 1) * chunk)
        dw_two[slot, h, 0] = dw_first[:, here]
        dw_two[slot, h, 1, :chunk] = dw_last[here, :chunk]
        dw_two[slot, h, 1, chunk:] = dw_last[here, chunk:]
    saved(step).start()

    @pl.when(lax.rem(ahead, steps) == 0)
    def _():
        eo_ref[0] = eo_sum[...].astype(BF16)
        da_ref[0] = da_sum[...].astype(BF16)

    @pl.when(ahead == 3 * steps)
    def _():
        gather_b[2]()
        gather_b[3]()
        each_turn(ahead, lambda copy: copy.start())

    @pl.when(step == last)
    def _():
        saved(step - 1).wait()
        saved(step).wait()
        reduce_c[3]()
        reduce_c[4]()
        keep.start()
        hop.wait()
        keep.wait()


def own_last(step, group):
    return lax.rem(lax.axis_index("expert") + 1 + step, group)


def send_rows(p, value, stage, target, sends, recvs, keep):
    place = lax.axis_index("expert")
    stage[p] = value

    @pl.when(p == place)
    def _():
        pltpu.make_async_copy(stage.at[place], target.at[place], keep.at[0]).start()

    @pl.when(p != place)
    def _():
        along_axis(stage.at[p], target.at[place], sends.at[p], recvs.at[place], p).start()


def end_rows(stage, target, sends, recvs, keep, group):
    place = lax.axis_index("expert")
    for k in range(1, group):
        other = lax.rem(place + k, group)
        along_axis(stage.at[other], target.at[other], sends.at[other], recvs.at[other], other).wait_recv()
    for k in range(1, group):
        other = lax.rem(place + k, group)
        along_axis(stage.at[other], target.at[place], sends.at[other], recvs.at[place], other).wait_send()
    pltpu.make_async_copy(stage.at[place], target.at[place], keep.at[0]).wait()


def combine_kernel(
    h_ref, a_ref, g_ref, o_ref, gate_ref, pr_ref, pos_ref, eo_ref, back_ref, second_ref, params_ref, terms, passed,
    out_all, dh_ref, do_ref, dw_ref, dgain_ref, drouter_ref, sums_ref,
    stage, landed, p_send, p_recv, sends, recvs, keep, own, pair, inbox, send, recv, local,
    *, share, experts, capacity, group
):
    step = pl.program_id(0)
    last = pl.num_programs(0) - 1
    place = lax.axis_index("expert")

    def emit(half, value):
        sums_ref[half] = (value + landed[half].astype(F32)).astype(BF16)

    start, far, near, late, finish = reduce_copies(terms.at[3], own, pair, inbox, send, recv, local, emit)
    hop = along_axis(passed, landed, p_send.at[0], p_recv.at[0], partner(place, 1))

    @pl.when(step == 0)
    def _():
        meet(plane_devices() + place_devices(group))
        start()
        hop.start()
        far()

    @pl.when(step == 1)
    def _():
        near()

    @pl.when(step == 3)
    def _():
        late()

    @pl.when(step == 0)
    def _():
        dw_ref[...] = jnp.zeros_like(dw_ref)
        dgain_ref[...] = jnp.zeros_like(dgain_ref)
        drouter_ref[...] = jnp.zeros_like(drouter_ref)

    tile = h_ref.shape[0]
    h1 = h_ref[...]
    g = g_ref[...].astype(F32)
    gates = gate_ref[...]
    pr = pr_ref[...]
    lane = lax.broadcasted_iota(jnp.int32, pr.shape, 1)
    slot = lax.broadcasted_iota(jnp.int32, (tile, capacity), 1)
    result = h1
    dgate = jnp.zeros_like(pr)
    da = jnp.zeros_like(h1)
    for k in range(experts):
        spot = (pos_ref[:, k : k + 1] == slot).astype(BF16)
        got = nn(spot, eo_ref[k])
        result = result + gates[:, k : k + 1] * got
        dgate = jnp.where(lane == k, jnp.sum(g * got, axis=-1, keepdims=True), dgate)
        da = da + nn(spot, back_ref[k])
    send_rows(step, result.astype(BF16), stage, out_all, sends, recvs, keep)
    named = (pos_ref[...] >= 0) & (lane < experts)
    denom = jnp.sum(jnp.where(named, pr, 0.0), axis=-1, keepdims=True)
    weighted = jnp.sum(dgate * gates, axis=-1, keepdims=True)
    dpr = jnp.where(named, (dgate - weighted) / denom, 0.0)
    dlog = pr * (dpr - jnp.sum(pr * dpr, axis=-1, keepdims=True))
    high = dlog.astype(BF16)
    lost = (dlog - high.astype(F32)).astype(BF16)
    a = a_ref[...]
    drouter_ref[...] += (tn(high, a) + tn(lost, a))[: drouter_ref.shape[0]]
    for k in range(experts):
        da = da + dlog[:, k : k + 1] * params_ref[8 + k : 9 + k, :]
    inverse = lax.rsqrt(jnp.mean(h1 * h1, axis=-1, keepdims=True) + EPSILON)
    n2 = h1 * inverse
    dgain_ref[...] += jnp.sum(da * n2, axis=0, keepdims=True)
    dn = da * params_ref[1:2, :]
    dh = g + inverse * (dn - n2 * jnp.mean(dn * n2, axis=-1, keepdims=True))
    dh_ref[...] = dh
    dy = dh.astype(BF16)
    do_ref[...] = nt(dy, weight(second_ref, 1, share)).astype(BF16)
    dw_ref[...] += tn(o_ref[...], dy)

    @pl.when(step == last)
    def _():
        hop.wait()
        finish()
        end_rows(stage, out_all, sends, recvs, keep, group)


def close_kernel(
    x_ref, dq_ref, dk_ref, dv_ref, dh_ref, first_ref, second_ref, params_ref, pack, sum0, sum1, sum2,
    din_out, gather_first, gather_second, dense_ref,
    stage, total, own, pair, inbox, r_send, r_recv, r_local, sends, recvs, keep,
    z_in, z_total, z_final, z_send, z_recv, g_send, g_recv, g_local, *, share, group, experts
):
    step = pl.program_id(0)
    last = pl.num_programs(0) - 1
    place = lax.axis_index("expert")
    start0, start1, start2, finish = gather_copies(
        gather_first, gather_second, total.at[0], total.at[1], g_send, g_recv, g_local
    )
    quarter = pack.shape[2] // 2

    def emit(half, value):
        low = value.astype(BF16)
        z_total[2 * half] = low[:quarter]
        z_total[2 * half + 1] = low[quarter:]

    start, far, near, late, end_reduce = reduce_copies(pack, own, pair, inbox, r_send, r_recv, r_local, emit)

    @pl.when(step == 0)
    def _():
        meet(plane_devices() + place_devices(group))
        start()
        far()
        near()
        for half in range(2):
            value = sum0[half].astype(F32) + sum1[half].astype(F32)
            total[half] = (value + sum2[half].astype(F32)).astype(BF16)

    @pl.when(step == 1)
    def _():
        late()
        start0()

    da = jnp.zeros(dh_ref.shape, F32)
    places = ((first_ref, 0), (first_ref, 1), (second_ref, 0))
    for index, grad_ref in enumerate((dq_ref, dk_ref, dv_ref)):
        slots_ref, at = places[index]
        da = da + nt(grad_ref[...], weight(slots_ref, at, share))
    x = x_ref[...].astype(F32)
    inverse = lax.rsqrt(jnp.mean(x * x, axis=-1, keepdims=True) + EPSILON)
    n1 = x * inverse
    dn = da * params_ref[0:1, :]
    din = dh_ref[...] + inverse * (dn - n1 * jnp.mean(dn * n1, axis=-1, keepdims=True))
    send_rows(own_last(step, group), din.astype(BF16), stage, din_out, sends, recvs, keep)

    @pl.when(step == last)
    def _():
        end_reduce()
        spread = [
            along_axis(z_total.at[lax.rem(place + k, group)], z_in.at[k - 1], z_send.at[k], z_recv.at[k],
                       lax.rem(place + k, group))
            for k in range(1, group)
        ]
        for copy in spread:
            copy.start()
        for copy in spread:
            copy.wait_recv()
        value = z_total[place].astype(F32)
        for k in range(group - 1):
            value = value + z_in[k].astype(F32)
        z_final[place] = value.astype(BF16)
        share_out = [
            along_axis(z_final.at[place], z_final.at[place], z_send.at[group + k], z_recv.at[group + k],
                       lax.rem(place + k, group))
            for k in range(1, group)
        ]
        for copy in share_out:
            copy.start()
        start1()
        start2()
        for copy in share_out:
            copy.wait_recv()
        for copy in spread + share_out:
            copy.wait_send()
        dense_ref[...] = z_final[...]
        end_rows(stage, din_out, sends, recvs, keep, group)
        finish()


def unpack_kernel(
    first_ref, second_ref, din_ref, dense_ref, wq_ref, wk_ref, wv_ref, gain_ref,
    in_ref, out_ref, grad_ref, dq_ref, dk_ref, dv_ref, do_ref, gain_out, small_ref, *, share
):
    chunk = first_ref.shape[2]
    in_ref[0] = first_ref[0].astype(F32)
    out_ref[0, :, :chunk] = second_ref[0, :chunk].astype(F32)
    out_ref[0, :, chunk:] = second_ref[0, chunk:].astype(F32)
    grad_ref[...] = din_ref[...].astype(F32)

    @pl.when(pl.program_id(0) == 0)
    def _():
        grads = []
        for grad, half, at in ((dq_ref, 0, 0), (dk_ref, 0, share), (dv_ref, 1, 0), (do_ref, 1, share)):
            value = dense_ref[half, at : at + share, :].astype(F32)
            grad[...] = value
            grads.append(value)
        moved = grads[0] * wq_ref[...].astype(F32) + grads[1] * wk_ref[...].astype(F32)
        moved = moved + grads[2] * wv_ref[...].astype(F32)
        gain_out[...] = jnp.sum(moved, axis=-1, keepdims=True) / gain_ref[...].astype(F32)
        small_ref[...] = dense_ref[0, 2 * share :, :].astype(F32)


def on_device_whole(
    layer_in, out_grad, routes, segments, buckets, gain_attn, w_query, w_key, w_value, w_output,
    gain_moe, router, rel_bias, w_expert_in, w_expert_out,
):
    group = lax.axis_size("expert")
    shards = lax.axis_size("dp")
    shard = lax.axis_index("dp")
    experts = router.shape[1]
    seq = segments.shape[1]
    heads = rel_bias.shape[1]
    width = D // heads
    scale = 1.0 / math.sqrt(width)
    share = D // shards
    ff = w_expert_in.shape[2]
    chunk = ff // shards
    blocks = seq // TILE
    part = seq // group
    capacity = 3 * seq // group
    pairs = 128 // width
    tokens = (seq, D)
    slots = (capacity, D)
    piece = (2, D, chunk)
    buffer = sds((shards, D, chunk), BF16)
    dma = pltpu.SemaphoreType.DMA
    vmem = pl.BlockSpec(memory_space=pltpu.VMEM)

    wide = lambda v, count: jnp.pad(v, ((0, count - v.shape[0]), (0, D - v.shape[1])))
    small = jnp.concatenate([
        wide(jnp.stack([gain_attn, gain_moe]), 8), wide(router.T, 8), wide(rel_bias.T, 16)])
    routes_in = jnp.pad(routes.transpose(0, 2, 1), ((0, 0), (0, 6), (0, 0)))
    bucket_row = buckets.reshape(1, seq)
    second_rows = 2 * share + 32
    tok16, tok32, wide32 = sds(tokens, BF16), sds(tokens, F32), sds((seq, 128), F32)
    block = sds((group, part, D), BF16)
    table_shape = (heads, blocks, TILE, TILE)
    v16, v32 = pltpu.VMEM(tokens, BF16), pltpu.VMEM(tokens, F32)
    (x, g, far_first, far_second, first, second, normed, q, k, v, o, table, h1, normed_m, gates, pr, near_first,
     near_second, _, params, across, down, lse) = call(
        functools.partial(
            front_kernel, group=group, share=share, heads=heads, experts=experts, scale=scale, width=width),
        "front", (1,),
        [ANY] * 9 + [vmem] * 3,
        [ANY] * 19 + [vmem] * 4,
        [block, block, sds((D, chunk), BF16), sds((D, chunk), BF16), sds((shards, 2 * share, D), BF16),
         sds((shards, second_rows, D), BF16)] + [tok16] * 5
        + [sds(table_shape, BF16), tok32, tok16, wide32, wide32, buffer, buffer, sds(piece, BF16),
           sds((32, D), F32), sds((16, seq), jnp.int32), sds((seq, 128), jnp.int32),
           sds((heads // pairs, pairs, seq), F32)],
        [pltpu.VMEM((group, part, D), BF16), pltpu.VMEM((group, 8, part), jnp.int32),
         pltpu.VMEM((shards, 2 * share, D), BF16), pltpu.VMEM((shards, second_rows, D), BF16),
         pltpu.VMEM((2 * share, D), BF16), pltpu.VMEM((second_rows, D), BF16)] + [v16] * 5
        + [pltpu.VMEM(table_shape, BF16), v32, v16, pltpu.VMEM((seq, 128), F32), pltpu.VMEM((seq, 128), F32),
           pltpu.VMEM((heads, 1, seq), F32)]
        + [dma((group,))] * 6 + [dma((6,))] * 2 + [dma((3 + heads // pairs,)), dma((4,)), dma((12,))]
        + gather_sems() * 2, collective=1, flops=6 * seq * D * D,
    )(layer_in, out_grad, routes_in, w_expert_in, w_expert_out, w_query, w_key, w_value, w_output, small, bucket_row,
      segments)
    x = x.reshape(tokens)
    g = g.reshape(tokens)
    buffers = [near_first, near_second]
    cols = pl.BlockSpec((seq, 128), lambda i: (0, i))
    table_spec = pl.BlockSpec((pairs, blocks, TILE, TILE), lambda i: (i, 0, 0, 0))
    lse_spec = pl.BlockSpec((1, pairs, seq), lambda i: (i, 0, 0))

    turned_rows = lambda width: pl.BlockSpec((TILE, width), lambda i: (own_last(i, group), 0))
    once = lambda shape: pl.BlockSpec(shape, lambda *_: (0,) * len(shape), pipeline_mode=pl.Buffered(1))
    turned = pl.BlockSpec((1, *slots), lambda i: (i // (shards // 2), 0, 0))
    eo, da, dw, sum1, sum3, _, _, _, _, _ = call(
        functools.partial(experts_kernel, capacity=capacity, group=group, shards=shards), "experts",
        (experts * shards // 2,),
        [once(tokens), once(tokens), once((seq, 128)), once((16, seq))] + [ANY] * 6,
        [turned, turned] + [ANY] * 8,
        [sds((experts, *slots), BF16)] * 2 + [sds((experts, shards, *piece), BF16)] + [sds(piece, BF16)] * 3
        + [buffer] * 4,
        [pltpu.VMEM(slots, BF16), pltpu.VMEM((D, capacity), BF16), pltpu.VMEM(slots, BF16),
         pltpu.VMEM(slots, F32), pltpu.VMEM(slots, F32), pltpu.VMEM((2, 2, D, chunk), BF16),
         pltpu.VMEM((2, 2, D, chunk), BF16), pltpu.VMEM((2, 2, *piece), BF16), pltpu.VMEM(piece, BF16),
         dma((6, 2)), dma((2,)), dma((3,)), dma((3,)), dma((1,)), pltpu.SemaphoreType.REGULAR]
        + reduce_scratch(piece) + reduce_scratch(piece)[3:] + gather_sems() * 2,
        flops=48 * capacity * D * ff, nbytes=96 * 2**20, collective=3,
    )(normed_m, g, gates, across, *buffers, far_first, far_second, w_expert_in, w_expert_out)
    layer_out, dh, do, grad_output, grad_gain_m, grad_router, sum2 = call(
        functools.partial(combine_kernel, share=share, experts=experts, capacity=capacity, group=group), "combine",
        (blocks,),
        [rows(D)] * 4 + [rows(128)] * 3 + [once((experts, *slots))] * 2 + [once(second.shape), whole((32, D)), ANY, ANY],
        [ANY, rows(D), rows(D), whole((D, D)), whole((1, D)), whole((8, D)), whole(piece)],
        [sds((group, part, D), BF16), sds(tokens, F32), sds(tokens, BF16), sds((D, D), F32), sds((1, D), F32),
         sds((8, D), F32), sds(piece, BF16)],
        [pltpu.VMEM((group, part, D), BF16), pltpu.VMEM(piece, BF16), dma((1,)), dma((1,)), dma((group,)),
         dma((group,)), dma((1,))] + reduce_scratch(piece),
        flops=24 * seq * D * D, nbytes=32 * 2**20, collective=7,
    )(h1, normed_m, g, o, gates, pr, down, eo, da, second, params, dw, sum3)
    dense_slot = (2, 2 * share + 32, D)
    dq, dk, dv, pack, sum0, sum2 = call(
        functools.partial(
            attend_back_kernel, width=width, scale=scale, group=group, share=share, experts=experts),
        "attend_back", (heads // pairs,),
        [cols, cols, cols, cols, table_spec, whole((seq, 128)), whole((16, seq)), lse_spec, once(tokens), once((D, D)),
         whole((1, D)), whole((8, D)), whole((1, seq)), ANY, ANY],
        [cols, cols, cols, once((shards, *dense_slot)), whole(piece), ANY],
        [sds(tokens, BF16)] * 3 + [sds((shards, *dense_slot), BF16), sds(piece, BF16), sds(piece, BF16)],
        [pltpu.VMEM((heads, 1, seq), F32), pltpu.VMEM((heads // pairs, D, 3 * 128), BF16),
         pltpu.VMEM((blocks, TILE, TILE), F32), pltpu.VMEM((seq, 128), F32), pltpu.VMEM((seq, 128), F32),
         pltpu.VMEM((D, seq), BF16)]
        + [dma((1,))] * 2 + reduce_scratch(piece),
        flops=20 * seq * seq * D, nbytes=24 * 2**20, collective=8,
    )(q, k, v, do, table, down, across, lse, normed, grad_output, grad_gain_m, grad_router, bucket_row, sum2, dw)
    quarter = (dense_slot[1] // 2, D)
    grad_in, *gathered, dense = call(
        functools.partial(close_kernel, share=share, group=group, experts=experts), "close", (blocks,),
        [turned_rows(D)] * 5 + [once(first.shape), once(second.shape), whole((32, D)), ANY] + [once(piece)] * 3,
        [ANY, ANY, ANY, whole((group, *quarter))],
        [sds((group, part, D), BF16), buffer, buffer, sds((group, *quarter), BF16)],
        [pltpu.VMEM((group, part, D), BF16), pltpu.VMEM(piece, BF16)]
        + reduce_scratch(dense_slot)
        + [dma((group,)), dma((group,)), dma((1,)), pltpu.VMEM((group - 1, *quarter), BF16),
           pltpu.VMEM((group, *quarter), BF16), pltpu.VMEM((group, *quarter), BF16), dma((2 * group,)),
           dma((2 * group,))] + gather_sems(),
        flops=12 * seq * D * D, nbytes=24 * 2**20, collective=9,
    )(x, dq, dk, dv, dh, first, second, params, pack, sum0, sum1, sum2)
    spec = pl.BlockSpec((1, D, chunk), lambda i: (i, 0, 0))
    line_rows = pl.BlockSpec((seq // shards, D), lambda i: (i, 0))
    expert_in, expert_out, grad_in, *dense_grads, grad_gain, smalls = call(
        functools.partial(unpack_kernel, share=share), "unpack", (shards,),
        [spec, spec, line_rows, whole(dense_slot)] + [whole((share, D))] * 3 + [whole((share, 1))],
        [pl.BlockSpec((1, D, chunk), lambda i: (0, 0, i)), pl.BlockSpec((1, chunk, D), lambda i: (0, i, 0)), line_rows]
        + [whole((share, D))] * 4 + [whole((share, 1)), whole((32, D))],
        [sds(w_expert_in.shape, F32), sds(w_expert_out.shape, F32), sds(tokens, F32)]
        + [sds((share, D), F32)] * 4 + [sds((share, 1), F32), sds((32, D), F32)],
        nbytes=34 * 2**20,
    )(*gathered, grad_in.reshape(tokens), dense.reshape(dense_slot), w_query, w_key, w_value,
      gain_attn.reshape(share, 1))
    line = lax.dynamic_slice_in_dim(smalls[:16], shard * share, share, axis=1)
    grad_table = lax.dynamic_slice_in_dim(smalls[16 : 16 + heads], shard * rel_bias.shape[0], rel_bias.shape[0], axis=1)
    return (
        layer_out,
        grad_in.reshape(group, part, D),
        grad_gain.reshape(share),
        *dense_grads,
        line[1],
        line[8 : 8 + experts].T,
        grad_table.T,
        expert_in,
        expert_out,
    )


def solution(mesh):
    in_specs = (
        P(None, ("dp", "expert"), None),
        P(None, ("dp", "expert"), None),
        P(None, ("dp", "expert"), None),
        P(None, "dp"),
        P(),
        P("dp"),
        P("dp", None),
        P("dp", None),
        P("dp", None),
        P("dp", None),
        P("dp"),
        P("dp", None),
        P("dp", None),
        P("expert", None, None),
        P("expert", None, None),
    )
    out_specs = (
        P(None, ("dp", "expert"), None),
        P(None, ("dp", "expert"), None),
        P("dp"),
        P("dp", None),
        P("dp", None),
        P("dp", None),
        P("dp", None),
        P("dp"),
        P("dp", None),
        P("dp", None),
        P("expert", None, None),
        P("expert", None, None),
    )
    body = on_device_whole if mesh.shape["expert"] == MICRO else on_device
    return jax.shard_map(
        body, mesh=mesh, in_specs=in_specs, out_specs=out_specs, check_vma=False
    )
```

```python
import functools
import math

import jax
import jax.numpy as jnp
from jax import lax
from jax.experimental import pallas as pl
from jax.experimental.pallas import tpu as pltpu
from jax.sharding import PartitionSpec as P

D = 768
NB = 32
MICRO = 4


EPSILON = 1e-06
MASKED = -1e30
TOP_PRECISION = lax.Precision.HIGHEST
GELU_A = math.sqrt(2.0 / math.pi)
GELU_B = 0.044715


def norm_forward(values, gain):
    inverse = lax.rsqrt(jnp.mean(values * values, axis=-1, keepdims=True) + EPSILON)
    scaled = values * inverse
    return (scaled, inverse, scaled * gain)


def norm_backward(grad_top, scaled, inverse, gain):
    grad_scaled = grad_top * gain
    grad_values = inverse * (
        grad_scaled - scaled * jnp.mean(grad_scaled * scaled, axis=-1, keepdims=True)
    )
    return (grad_values, jnp.sum(grad_top * scaled, axis=0))


def split_heads(values, heads):
    return values.reshape(values.shape[0], heads, -1).transpose(1, 0, 2)


def merge_heads(values):
    return values.transpose(1, 0, 2).reshape(values.shape[1], -1)


def score_block(q_heads, k_heads, bias, allowed, scale):
    raw = jnp.einsum("hqd,hkd->hqk", q_heads, k_heads, preferred_element_type=jnp.float32)
    return jnp.where(allowed[None], raw * scale + bias, MASKED)


def bucket_table(distances, bucket_starts):
    lower = bucket_starts[:-1]
    upper = bucket_starts[1:]
    return (
        (distances[:, :, None] >= lower[None, None, :])
        & (distances[:, :, None] < upper[None, None, :])
    ).astype(jnp.bfloat16)


def on_device(
    layer_in,
    out_grad,
    routes,
    segments,
    buckets,
    gain_attn,
    w_query,
    w_key,
    w_value,
    w_output,
    gain_moe,
    router,
    rel_bias,
    w_expert_in,
    w_expert_out,
):
    tok_rows = layer_in.shape[1]
    seq_len = segments.shape[1]
    heads = rel_bias.shape[1]
    group_size = lax.axis_size("expert")
    rank_here = lax.axis_index("expert")
    expert_count = router.shape[1]
    local_experts = w_expert_in.shape[0]
    capacity = 3 * tok_rows // group_size
    scale = 1.0 / math.sqrt(D // heads)
    bucket_starts = jnp.sum(
        (buckets[None, :] < jnp.arange(NB + 1, dtype=jnp.int32)[:, None]).astype(jnp.int32), axis=1
    )
    query_pos = rank_here * tok_rows + jnp.arange(tok_rows, dtype=jnp.int32)
    key_pos = jnp.arange(seq_len, dtype=jnp.int32)
    offsets = jnp.maximum(query_pos[:, None] - key_pos[None, :], 0)
    bucket_onehot = bucket_table(offsets, bucket_starts)
    causal = query_pos[:, None] >= key_pos[None, :]
    slot_ids = jnp.arange(expert_count * capacity, dtype=jnp.int32)
    expert_ids = jnp.arange(expert_count, dtype=jnp.int32)
    pair_ids = jnp.arange(2 * tok_rows, dtype=jnp.int32)
    earlier = (pair_ids[None, :] < pair_ids[:, None]).astype(jnp.bfloat16)
    dense_sums = [
        jnp.zeros((D,), jnp.float32),
        jnp.zeros((D, D), jnp.float32),
        jnp.zeros((D, D), jnp.float32),
        jnp.zeros((D, D), jnp.float32),
        jnp.zeros((D, D), jnp.float32),
        jnp.zeros((D,), jnp.float32),
        jnp.zeros((D, expert_count), jnp.float32),
        jnp.zeros((NB, heads), jnp.float32),
    ]
    in_sum = jnp.zeros(w_expert_in.shape, jnp.float32)
    out_sum = jnp.zeros(w_expert_out.shape, jnp.float32)
    outputs_list = []
    grads_list = []
    for step_index in range(MICRO):
        weights_now = (
            lax.all_gather(gain_attn, "dp", axis=0, tiled=True),
            lax.all_gather(w_query, "dp", axis=0, tiled=True),
            lax.all_gather(w_key, "dp", axis=0, tiled=True),
            lax.all_gather(w_value, "dp", axis=0, tiled=True),
            lax.all_gather(w_output, "dp", axis=0, tiled=True),
            lax.all_gather(gain_moe, "dp", axis=0, tiled=True),
            lax.all_gather(router, "dp", axis=0, tiled=True),
            lax.all_gather(rel_bias, "dp", axis=0, tiled=True),
        )
        gain_a, query_w, key_w, value_w, output_w, gain_m, router_w, bias_table = weights_now
        gain_af = gain_a.astype(jnp.float32)
        gain_mf = gain_m.astype(jnp.float32)
        inputs = layer_in[step_index].astype(jnp.float32)
        scaled_a, inverse_a, normed_a = norm_forward(inputs, gain_af)
        normed_ab = normed_a.astype(jnp.bfloat16)
        queries = jnp.dot(normed_ab, query_w, preferred_element_type=jnp.float32).astype(
            jnp.bfloat16
        )
        keys_loc = jnp.dot(normed_ab, key_w, preferred_element_type=jnp.float32).astype(
            jnp.bfloat16
        )
        values_loc = jnp.dot(normed_ab, value_w, preferred_element_type=jnp.float32).astype(
            jnp.bfloat16
        )
        keys_all, values_all = (
            lax.all_gather(keys_loc, "expert", axis=0, tiled=True),
            lax.all_gather(values_loc, "expert", axis=0, tiled=True),
        )
        q_heads = split_heads(queries, heads)
        k_heads = split_heads(keys_all, heads)
        v_heads = split_heads(values_all, heads)
        bias = jnp.einsum(
            "qkb,bh->hqk", bucket_onehot, bias_table, preferred_element_type=jnp.float32
        )
        seg_all = segments[step_index]
        seg_here = lax.dynamic_slice_in_dim(seg_all, rank_here * tok_rows, tok_rows)
        allowed = causal & (seg_here[:, None] == seg_all[None, :])
        scores = score_block(q_heads, k_heads, bias, allowed, scale)
        top_score = jnp.max(scores, axis=-1, keepdims=True)
        lifted = jnp.exp(scores - top_score)
        total = jnp.sum(lifted, axis=-1, keepdims=True)
        log_total = top_score + jnp.log(total)
        probs_b = (lifted / total).astype(jnp.bfloat16)
        attended = merge_heads(
            jnp.einsum("hqk,hkd->hqd", probs_b, v_heads, preferred_element_type=jnp.float32)
        ).astype(jnp.bfloat16)
        resid = inputs + jnp.dot(attended, output_w, preferred_element_type=jnp.float32)
        scaled_m, inverse_m, normed_m = norm_forward(resid, gain_mf)
        normed_mb = normed_m.astype(jnp.bfloat16)
        logits = jnp.dot(normed_mb, router_w, preferred_element_type=jnp.float32)
        router_probs = jax.nn.softmax(logits, axis=-1)
        routes_now = routes[step_index]
        pick_first = (routes_now[:, 0:1] == expert_ids[None, :]).astype(jnp.float32)
        pick_second = (routes_now[:, 1:2] == expert_ids[None, :]).astype(jnp.float32)
        prob_first = jnp.sum(router_probs * pick_first, axis=-1)
        prob_second = jnp.sum(router_probs * pick_second, axis=-1)
        denom = prob_first + prob_second
        gate_first = prob_first / denom
        gate_second = prob_second / denom
        flat = routes_now.reshape(-1)
        flat_hot = (flat[:, None] == expert_ids[None, :]).astype(jnp.bfloat16)
        before = jnp.dot(earlier, flat_hot, preferred_element_type=jnp.float32)
        places = jnp.sum(before * flat_hot.astype(jnp.float32), axis=1).astype(jnp.int32)
        slot_pairs = (flat * capacity + places).reshape(tok_rows, 2)
        place_first = (slot_ids[:, None] == slot_pairs[None, :, 0]).astype(jnp.bfloat16)
        place_second = (slot_ids[:, None] == slot_pairs[None, :, 1]).astype(jnp.bfloat16)
        place_both = place_first + place_second
        outgoing = jnp.dot(place_both, normed_mb, preferred_element_type=jnp.float32).astype(
            jnp.bfloat16
        )
        outgoing = outgoing.reshape(group_size, local_experts, capacity, D)
        arrived_rows = lax.all_to_all(outgoing, "expert", split_axis=0, concat_axis=0, tiled=True)
        pre_act = jnp.einsum(
            "sjcd,jdf->sjcf", arrived_rows, w_expert_in, preferred_element_type=jnp.float32
        )
        post_act = jax.nn.gelu(pre_act).astype(jnp.bfloat16)
        produced = jnp.einsum(
            "sjcf,jfd->sjcd", post_act, w_expert_out, preferred_element_type=jnp.float32
        ).astype(jnp.bfloat16)
        produced, pre_act, post_act, arrived = (produced, pre_act, post_act, arrived_rows)
        returned = lax.all_to_all(
            produced, "expert", split_axis=0, concat_axis=0, tiled=True
        ).reshape(expert_count * capacity, D)
        got_first = jnp.einsum(
            "st,sd->td", place_first, returned, preferred_element_type=jnp.float32
        )
        got_second = jnp.einsum(
            "st,sd->td", place_second, returned, preferred_element_type=jnp.float32
        )
        result = resid + (gate_first[:, None] * got_first + gate_second[:, None] * got_second)
        outputs_list.append(result.astype(jnp.bfloat16))
        grad_top = out_grad[step_index].astype(jnp.float32)
        dgate_first = jnp.sum(grad_top * got_first, axis=-1)
        dgate_second = jnp.sum(grad_top * got_second, axis=-1)
        sent_first = (gate_first[:, None] * grad_top).astype(jnp.bfloat16)
        sent_second = (gate_second[:, None] * grad_top).astype(jnp.bfloat16)
        grad_slots = (
            jnp.dot(place_first, sent_first, preferred_element_type=jnp.float32)
            + jnp.dot(place_second, sent_second, preferred_element_type=jnp.float32)
        ).astype(jnp.bfloat16)
        grad_slots = grad_slots.reshape(group_size, local_experts, capacity, D)
        grad_arrived = lax.all_to_all(grad_slots, "expert", split_axis=0, concat_axis=0, tiled=True)
        grad_post = jnp.einsum(
            "sjcd,jfd->sjcf", grad_arrived, w_expert_out, preferred_element_type=jnp.float32
        )
        out_sum = out_sum + jnp.einsum(
            "sjcf,sjcd->jfd", post_act, grad_arrived, preferred_element_type=jnp.float32
        )
        grad_pre = jax.vjp(jax.nn.gelu, pre_act)[1](grad_post)[0].astype(jnp.bfloat16)
        in_sum = in_sum + jnp.einsum(
            "sjcd,sjcf->jdf", arrived, grad_pre, preferred_element_type=jnp.float32
        )
        grad_rows = jnp.einsum(
            "sjcf,jdf->sjcd", grad_pre, w_expert_in, preferred_element_type=jnp.float32
        ).astype(jnp.bfloat16)
        grad_back = lax.all_to_all(
            grad_rows, "expert", split_axis=0, concat_axis=0, tiled=True
        ).reshape(expert_count * capacity, D)
        grad_moe = jnp.einsum(
            "st,sd->td", place_both, grad_back, preferred_element_type=jnp.float32
        )
        weighted = dgate_first * gate_first + dgate_second * gate_second
        grad_pick = ((dgate_first - weighted) / denom)[:, None] * pick_first + (
            (dgate_second - weighted) / denom
        )[:, None] * pick_second
        grad_logits = router_probs * (
            grad_pick - jnp.sum(router_probs * grad_pick, axis=-1, keepdims=True)
        )
        normed_mf = normed_mb.astype(jnp.float32)
        grad_router_w = jnp.dot(normed_mf.T, grad_logits, precision=TOP_PRECISION)
        grad_moe = grad_moe + jnp.dot(
            grad_logits, router_w.astype(jnp.float32).T, precision=TOP_PRECISION
        )
        grad_resid_norm, grad_gain_m = norm_backward(grad_moe, scaled_m, inverse_m, gain_mf)
        grad_resid = grad_top + grad_resid_norm
        grad_branch = grad_resid.astype(jnp.bfloat16)
        grad_output_w = jnp.einsum(
            "td,te->de", attended, grad_branch, preferred_element_type=jnp.float32
        )
        grad_attended = jnp.einsum(
            "te,de->td", grad_branch, output_w, preferred_element_type=jnp.float32
        ).astype(jnp.bfloat16)
        grad_heads = split_heads(grad_attended, heads)
        scores_again = score_block(q_heads, k_heads, bias, allowed, scale)
        probs_again = jnp.exp(scores_again - log_total)
        probs_again_b = probs_again.astype(jnp.bfloat16)
        grad_probs = jnp.einsum(
            "hqd,hkd->hqk", grad_heads, v_heads, preferred_element_type=jnp.float32
        )
        row_delta = jnp.sum(probs_again * grad_probs, axis=-1, keepdims=True)
        grad_scores = probs_again * (grad_probs - row_delta)
        grad_table = jnp.einsum(
            "hqk,qkb->bh", grad_scores, bucket_onehot.astype(jnp.float32), precision=TOP_PRECISION
        )
        grad_scores_b = (grad_scores * scale).astype(jnp.bfloat16)
        grad_q_heads = jnp.einsum(
            "hqk,hkd->hqd", grad_scores_b, k_heads, preferred_element_type=jnp.float32
        )
        grad_v_heads = jnp.einsum(
            "hqk,hqd->hkd", probs_again_b, grad_heads, preferred_element_type=jnp.float32
        )
        grad_k_heads = jnp.einsum(
            "hqk,hqd->hkd", grad_scores_b, q_heads, preferred_element_type=jnp.float32
        )
        grad_keys, grad_values = (
            lax.psum_scatter(merge_heads(grad_k_heads), "expert", scatter_dimension=0, tiled=True),
            lax.psum_scatter(merge_heads(grad_v_heads), "expert", scatter_dimension=0, tiled=True),
        )
        grad_queries_b = merge_heads(grad_q_heads).astype(jnp.bfloat16)
        grad_keys_b = grad_keys.astype(jnp.bfloat16)
        grad_values_b = grad_values.astype(jnp.bfloat16)
        grad_query_w = jnp.einsum(
            "td,te->de", normed_ab, grad_queries_b, preferred_element_type=jnp.float32
        )
        grad_key_w = jnp.einsum(
            "td,te->de", normed_ab, grad_keys_b, preferred_element_type=jnp.float32
        )
        grad_value_w = jnp.einsum(
            "td,te->de", normed_ab, grad_values_b, preferred_element_type=jnp.float32
        )
        grad_normed = (
            jnp.einsum("te,de->td", grad_queries_b, query_w, preferred_element_type=jnp.float32)
            + jnp.einsum("te,de->td", grad_keys_b, key_w, preferred_element_type=jnp.float32)
            + jnp.einsum("te,de->td", grad_values_b, value_w, preferred_element_type=jnp.float32)
        )
        grad_in_norm, grad_gain_a = norm_backward(grad_normed, scaled_a, inverse_a, gain_af)
        grads_list.append(grad_resid + grad_in_norm)
        parts_now = (
            grad_gain_a,
            grad_query_w,
            grad_key_w,
            grad_value_w,
            grad_output_w,
            grad_gain_m,
            grad_router_w,
            grad_table,
        )
        dense_sums = [running + addend for running, addend in zip(dense_sums, parts_now)]
    sum_gain_a, sum_query, sum_key, sum_value, sum_output, sum_gain_m, sum_router, sum_table = (
        dense_sums
    )
    summed = lax.psum(
        (sum_gain_a, sum_query, sum_key, sum_value, sum_output, sum_gain_m, sum_router, sum_table),
        "expert",
    )
    (
        full_gain_a,
        full_query,
        full_key,
        full_value,
        full_output,
        full_gain_m,
        full_router,
        full_table,
    ) = summed
    shares = (
        lax.psum_scatter(full_gain_a, "dp", scatter_dimension=0, tiled=True),
        lax.psum_scatter(full_query, "dp", scatter_dimension=0, tiled=True),
        lax.psum_scatter(full_key, "dp", scatter_dimension=0, tiled=True),
        lax.psum_scatter(full_value, "dp", scatter_dimension=0, tiled=True),
        lax.psum_scatter(full_output, "dp", scatter_dimension=0, tiled=True),
        lax.psum_scatter(full_gain_m, "dp", scatter_dimension=0, tiled=True),
        lax.psum_scatter(full_router, "dp", scatter_dimension=0, tiled=True),
        lax.psum_scatter(full_table, "dp", scatter_dimension=0, tiled=True),
    )
    expert_in_grad, expert_out_grad = (
        lax.psum(in_sum.astype(jnp.bfloat16), "dp").astype(jnp.float32),
        lax.psum(out_sum.astype(jnp.bfloat16), "dp").astype(jnp.float32),
    )
    layer_out = jnp.stack(outputs_list)
    grad_in = jnp.stack(grads_list)
    return (
        layer_out,
        grad_in,
        shares[0],
        shares[1],
        shares[2],
        shares[3],
        shares[4],
        shares[5],
        shares[6],
        shares[7],
        expert_in_grad,
        expert_out_grad,
    )


F32 = jnp.float32
BF16 = jnp.bfloat16
TILE = 256
VMEM_LIMIT = 60 * 2**20


def nn(left, right):
    return lax.dot_general(left, right, (((1,), (0,)), ((), ())), preferred_element_type=F32)


def nt(left, right):
    return lax.dot_general(left, right, (((1,), (1,)), ((), ())), preferred_element_type=F32)


def tn(left, right):
    return lax.dot_general(left, right, (((0,), (0,)), ((), ())), preferred_element_type=F32)


def call(body, name, grid, ins, outs, out_shapes, scratch=(), flops=0, nbytes=0, collective=None):
    extra = {} if collective is None else {"collective_id": collective, "has_side_effects": True}
    return pl.pallas_call(
        body,
        grid=grid,
        in_specs=ins,
        out_specs=outs,
        out_shape=out_shapes,
        scratch_shapes=list(scratch),
        compiler_params=pltpu.CompilerParams(
            dimension_semantics=("arbitrary",) * len(grid), vmem_limit_bytes=VMEM_LIMIT, **extra
        ),
        cost_estimate=pl.CostEstimate(flops=flops, bytes_accessed=nbytes, transcendentals=0),
        name=name,
    )


def whole(shape):
    zeros = (0,) * len(shape)
    return pl.BlockSpec(shape, lambda *_: zeros)


def rows(width, tile=TILE):
    return pl.BlockSpec((tile, width), lambda i: (i, 0))


MESH = pl.DeviceIdType.MESH
ANY = pl.BlockSpec(memory_space=pl.ANY)


def neighbours():
    me = lax.axis_index("dp")
    core = me + 1 - 2 * (me % 2)
    along_x = me + 2 - 4 * ((me // 2) % 2)
    along_y = me + 4 - 8 * (me // 4)
    across = along_x + 4 - 8 * (me // 4)
    return me, core, along_x, along_y, across


def meet(devices):
    barrier = pltpu.get_barrier_semaphore()
    for device in devices:
        pl.semaphore_signal(barrier, inc=1, device_id=device, device_id_type=MESH)
    pl.semaphore_wait(barrier, len(devices))


def plane_devices():
    place = lax.axis_index("expert")
    _, core, along_x, along_y, _ = neighbours()
    return [(core, place), (along_x, place), (along_y, place)]


GATHER_COPIES = 14


def gather_copies(first, second, source_first, source_second, send, recv, local):
    place = lax.axis_index("expert")
    me, core, along_x, along_y, across = neighbours()

    def remote(index, source, target, device):
        return pltpu.make_async_remote_copy(
            src_ref=source,
            dst_ref=target,
            send_sem=send.at[index],
            recv_sem=recv.at[index],
            device_id=(device, place),
            device_id_type=MESH,
        )

    own = [
        pltpu.make_async_copy(source_first, first.at[me], local.at[0]),
        pltpu.make_async_copy(source_second, second.at[me], local.at[1]),
    ]
    near = [
        remote(0, source_first, first.at[me], along_x),
        remote(1, source_second, second.at[me], along_y),
        remote(2, source_first, first.at[me], along_y),
        remote(3, source_second, second.at[me], along_x),
    ]
    paired = [
        remote(4, source_first, first.at[me], core),
        remote(5, source_second, second.at[me], core),
    ]
    far = [
        remote(6, first.at[along_x], first.at[along_x], along_y),
        remote(7, second.at[along_y], second.at[along_y], along_x),
    ]
    paired_near = [
        remote(8, first.at[along_x], first.at[along_x], core),
        remote(9, second.at[along_y], second.at[along_y], core),
        remote(10, first.at[along_y], first.at[along_y], core),
        remote(11, second.at[along_x], second.at[along_x], core),
    ]
    paired_far = [
        remote(12, first.at[across], first.at[across], core),
        remote(13, second.at[across], second.at[across], core),
    ]

    def start0():
        for copy in near + paired + own:
            copy.start()

    def start1():
        near[0].wait_recv()
        far[0].start()
        near[1].wait_recv()
        far[1].start()
        near[2].wait_recv()
        near[3].wait_recv()
        for copy in paired_near:
            copy.start()

    def start2():
        for copy, onward in zip(far, paired_far):
            copy.wait_recv()
            onward.start()

    def finish():
        for copy in own:
            copy.wait()
        for copy in paired + paired_near + paired_far:
            copy.wait_recv()
        for copy in near + paired + far + paired_near + paired_far:
            copy.wait_send()

    return start0, start1, start2, finish


def gather_sems():
    return [
        pltpu.SemaphoreType.DMA((GATHER_COPIES,)),
        pltpu.SemaphoreType.DMA((GATHER_COPIES,)),
        pltpu.SemaphoreType.DMA((2,)),
    ]


def sds(shape, dtype):
    return jax.ShapeDtypeStruct(shape, dtype)


def partner(place, k):
    return 2 * lax.rem(place // 2 + k // 2, 2) + lax.rem(lax.rem(place, 2) + k % 2, 2)


ORDER = (1, 2, 0, 3)


def place_devices(group):
    me = lax.axis_index("dp")
    place = lax.axis_index("expert")
    return [(me, lax.rem(place + k, group)) for k in range(1, group)]


def along_axis(source, target, send, recv, place):
    return pltpu.make_async_remote_copy(
        src_ref=source,
        dst_ref=target,
        send_sem=send,
        recv_sem=recv,
        device_id=(lax.axis_index("dp"), place),
        device_id_type=MESH,
    )


def swap_copies(source, target, send, recv, group):
    place = lax.axis_index("expert")
    copies = []
    for k in range(1, group):
        other = lax.rem(place + k, group)
        copies.append(along_axis(source.at[other], target.at[place], send.at[k], recv.at[k], other))
    return copies


def slice_copies(w_in, w_out, first, second, send, recv, base, place):
    me = lax.axis_index("dp")
    chunk = (first if second is None else second).shape[1]
    here = pl.ds(pl.multiple_of(me * chunk, 128), chunk)
    pieces = []
    if first is not None:
        pieces.append((w_in.at[0, :, here], first))
    if second is not None:
        pieces += [
            (w_out.at[0, here, pl.ds(at, chunk)], second.at[pl.ds(at, chunk)]) for at in (0, chunk)
        ]
    return [
        along_axis(source, goal, send.at[base + i], recv.at[base + i], place)
        for i, (source, goal) in enumerate(pieces)
    ]


REDUCE_COPIES = 10


def reduce_copies(terms, own, pair, inbox, send, recv, local, emit):
    place = lax.axis_index("expert")
    me, core, along_x, along_y, across = neighbours()
    targets = (across, along_x, along_y, me)

    def remote(index, source, target, device):
        return pltpu.make_async_remote_copy(
            src_ref=source,
            dst_ref=target,
            send_sem=send.at[index],
            recv_sem=recv.at[index],
            device_id=(device, place),
            device_id_type=MESH,
        )

    loads = [pltpu.make_async_copy(terms.at[t], own.at[q], local.at[q]) for q, t in enumerate(targets)]
    pairs = [
        remote(q, terms.at[t + 1 - 2 * lax.rem(t, 2)], pair.at[q], core) for q, t in enumerate(targets)
    ]
    far_first = remote(4, own.at[0, 0], inbox.at[0], along_x)
    far_second = remote(5, own.at[0, 1], inbox.at[1], along_y)
    near_first = remote(6, own.at[1, 0], inbox.at[2], along_x)
    near_second = remote(7, own.at[2, 1], inbox.at[3], along_y)
    late_first = remote(8, own.at[2, 0], inbox.at[4], along_y)
    late_second = remote(9, own.at[1, 1], inbox.at[5], along_x)

    def merge(q):
        loads[q].wait()
        pairs[q].wait_recv()
        own[q] = own[q] + pair[q]

    def start():
        pairs[0].start()
        for copy in loads:
            copy.start()

    def far():
        merge(0)
        far_first.start()
        far_second.start()
        for copy in pairs[1:]:
            copy.start()

    def near():
        merge(1)
        near_first.start()
        merge(2)
        near_second.start()

    def late():
        far_first.wait_recv()
        own[2, 0] = own[2, 0] + inbox[0]
        late_first.start()
        far_second.wait_recv()
        own[1, 1] = own[1, 1] + inbox[1]
        late_second.start()

    def finish():
        merge(3)
        for copy in (near_first, near_second, late_first, late_second):
            copy.wait_recv()
        emit(0, own[3, 0].astype(F32) + inbox[2].astype(F32) + inbox[4].astype(F32))
        emit(1, own[3, 1].astype(F32) + inbox[3].astype(F32) + inbox[5].astype(F32))
        for copy in pairs + [far_first, far_second, near_first, near_second, late_first, late_second]:
            copy.wait_send()

    return start, far, near, late, finish


def reduce_scratch(shape):
    half = shape[1:]
    return [
        pltpu.VMEM((4, *shape), BF16),
        pltpu.VMEM((4, *shape), BF16),
        pltpu.VMEM((6, *half), BF16),
        pltpu.SemaphoreType.DMA((REDUCE_COPIES,)),
        pltpu.SemaphoreType.DMA((REDUCE_COPIES,)),
        pltpu.SemaphoreType.DMA((4,)),
    ]


def weight(slots_ref, index, share):
    return slots_ref[:, index * share : (index + 1) * share, :].reshape(-1, D)


def front_kernel(
    x_ref, grad_ref, routes_ref, w_in_ref, w_out_ref, wq_ref, wk_ref, wv_ref, wo_ref, small_ref, buckets_ref, seg_ref,
    x_out, grad_out, c0_out, c1_out, first_out, second_out, a_out, q_out, k_out, v_out, o_out, table_out,
    h_out, n_out, gate_out, pr_out, gather_first, gather_second, piece_out, params_ref, across_ref, down_ref, lse_ref,
    land, routes_land, first, second, stage_first, stage_second,
    a_ref, q_ref, k_ref, v_ref, o_ref, table_ref, h_ref, n_ref, gate_ref, pr_ref, line_ref,
    x_send, x_recv, r_send, r_recv, g_send, g_recv, p_send, p_recv, keep, own_local, out_sem,
    send, recv, local, send_w, recv_w, local_w,
    *, group, share, heads, experts, scale, width
):
    me = lax.axis_index("dp")
    place = lax.axis_index("expert")
    pieces = [
        (wq_ref, stage_first.at[pl.ds(0, share)]),
        (wk_ref, stage_first.at[pl.ds(share, share)]),
        (wv_ref, stage_second.at[pl.ds(0, share)]),
        (wo_ref, stage_second.at[pl.ds(share, share)]),
    ]
    staged = [pltpu.make_async_copy(src, dst, own_local.at[i]) for i, (src, dst) in enumerate(pieces)]
    for copy in staged:
        copy.start()
    small = small_ref[...].astype(F32)
    line = lax.broadcasted_iota(jnp.int32, small.shape, 0)
    placed = jnp.where(line < 16, pltpu.roll(small, me * share, 1), pltpu.roll(small, me * 4, 1))
    stage_second[2 * share :, :] = placed.astype(BF16)
    meet(plane_devices() + place_devices(group))
    moves = swap_copies(routes_ref, routes_land, r_send, r_recv, group)
    moves_x = swap_copies(x_ref, land, x_send, x_recv, group)
    moves_g = swap_copies(grad_ref, grad_out, g_send, g_recv, group)
    slices = slice_copies(w_in_ref, w_out_ref, piece_out.at[0], piece_out.at[1], p_send, p_recv, 0, partner(place, 1))
    distant = slice_copies(w_in_ref, w_out_ref, c0_out, c1_out, p_send, p_recv, 3, partner(place, 2))
    kept = [
        pltpu.make_async_copy(routes_ref.at[place], routes_land.at[place], keep.at[0]),
        pltpu.make_async_copy(x_ref.at[place], land.at[place], keep.at[1]),
        pltpu.make_async_copy(grad_ref.at[place], grad_out.at[place], keep.at[2]),
    ]
    for copy in moves + moves_x + kept:
        copy.start()
    for copy in staged:
        copy.wait()
    start0, start1, start2, finish = gather_copies(first, second, stage_first, stage_second, send, recv, local)
    start0()

    kept[0].wait()
    for copy in moves:
        copy.wait_recv()
    seq = down_ref.shape[0]
    row_id = lax.broadcasted_iota(jnp.int32, (8, routes_land.shape[2]), 0)
    holder = jnp.full(row_id.shape, -1, jnp.int32)
    for k in range(experts):
        holder = jnp.where(row_id == k, partner(place, ORDER[k]), holder)
    named = []
    for p in range(group):
        picks = [routes_land[p, c : c + 1, :] == holder for c in range(2)]
        named.append((picks[0] | picks[1]).astype(F32))
    named = jnp.concatenate(named, axis=1)
    earlier = lax.broadcasted_iota(jnp.int32, (seq, seq), 0) < lax.broadcasted_iota(jnp.int32, (seq, seq), 1)
    before = nn(named.astype(BF16), earlier.astype(F32).astype(BF16))
    pos = jnp.where(named > 0, before, -1.0)
    which = lax.broadcasted_iota(jnp.int32, seg_ref.shape, 0)
    segs = jnp.where(which == place, seg_ref[...], 0).astype(F32).sum(axis=0, keepdims=True)
    stack = jnp.concatenate([pos, jnp.broadcast_to(segs, (8, seq))], axis=0)
    across_ref[...] = stack.astype(jnp.int32)
    filled = jnp.concatenate([stack, jnp.full((112, seq), -1.0, F32)], axis=0)
    down_ref[...] = filled.T.astype(jnp.int32)

    start1()
    start2()
    finish()
    out_copies = []

    def put(source, target):
        out_copies.append(pltpu.make_async_copy(source, target, out_sem.at[len(out_copies)]))
        out_copies[-1].start()

    put(first, first_out)
    put(second, second_out)
    params = second[0, 2 * share :, :].astype(F32)
    for slot in range(1, second.shape[0]):
        params = params + second[slot, 2 * share :, :].astype(F32)
    turned = []
    for k in range(experts):
        wanted = partner(place, ORDER[k])
        picked = jnp.zeros((1, D), F32)
        for e in range(experts):
            picked = picked + params[8 + e : 9 + e, :] * jnp.where(wanted == e, 1.0, 0.0)
        turned.append(picked)
    params_ref[...] = params
    for k in range(experts):
        params_ref[8 + k : 9 + k, :] = turned[k]
    hot = (lax.broadcasted_iota(jnp.int32, (128, seq), 0) == buckets_ref[...]).astype(F32).astype(BF16)
    lines = nn(params[16:32, :128].astype(BF16), hot)
    for h in range(heads):
        line_ref[h] = lines[h : h + 1, :]

    kept[1].wait()
    for copy in moves_x:
        copy.wait_recv()
    for copy in slices + distant:
        copy.start()
    put(land, x_out)
    part = land.shape[1]
    for p in range(group):
        here = slice(p * part, (p + 1) * part)
        x = land[p].astype(F32)
        inverse = lax.rsqrt(jnp.mean(x * x, axis=-1, keepdims=True) + EPSILON)
        normed = (x * inverse * params[0:1, :]).astype(BF16)
        a_ref[here, :] = normed
        q = nn(normed, weight(first, 0, share)).astype(BF16)
        q_ref[here, :] = (q.astype(F32) * scale).astype(BF16)
        k_ref[here, :] = nn(normed, weight(first, 1, share)).astype(BF16)
        v_ref[here, :] = nn(normed, weight(second, 0, share)).astype(BF16)
    for source, target in ((a_ref, a_out), (q_ref, q_out), (k_ref, k_out), (v_ref, v_out)):
        put(source, target)
    gather = gather_copies(
        gather_first, gather_second, piece_out.at[0], piece_out.at[1], send_w, recv_w, local_w
    )
    pairs = 128 // width
    count = heads // pairs

    def table_copy(n):
        heads_here = pl.ds(n * pairs, pairs)
        return pltpu.make_async_copy(table_ref.at[heads_here], table_out.at[heads_here], keep.at[3 + n])

    def attend(n, carry):
        @pl.when(n == 4)
        def _():
            for copy in slices:
                copy.wait_recv()
            gather[0]()
            for copy in moves_g:
                copy.start()

        attend_pair(n, q_ref, k_ref, v_ref, line_ref, table_ref, down_ref, across_ref, o_ref, lse_ref, width)
        table_copy(n).start()
        return carry

    lax.fori_loop(0, count, attend, 0)
    put(o_ref, o_out)

    def route(i, carry):
        here = pl.ds(pl.multiple_of(i * TILE, TILE), TILE)
        route_rows(
            land[i], o_ref[here, :], second, params_ref, down_ref, h_ref, n_ref, gate_ref, pr_ref, here, share, experts
        )
        return carry

    lax.fori_loop(0, group, route, 0)
    for source, target in ((h_ref, h_out), (n_ref, n_out), (gate_ref, gate_out), (pr_ref, pr_out)):
        put(source, target)
    gather[1]()
    gather[2]()
    kept[2].wait()
    for copy in distant + moves_g:
        copy.wait_recv()
    for copy in moves + moves_x + slices + distant + moves_g:
        copy.wait_send()
    gather[3]()
    for n in range(count):
        table_copy(n).wait()
    for copy in out_copies:
        copy.wait()


def masked_scores(k, q, table_ref, head, i, j, seg_col, seg_row):
    scores = nt(k, q) + table_ref[head, i - j].astype(F32)
    allowed = seg_col == seg_row
    if i == j:
        key_at = lax.broadcasted_iota(jnp.int32, (TILE, TILE), 0)
        query_at = lax.broadcasted_iota(jnp.int32, (TILE, TILE), 1)
        allowed = allowed & (key_at <= query_at)
    return jnp.where(allowed, scores, MASKED)


def route_rows(x, o, second_ref, params_ref, down_ref, h_ref, a_ref, gate_ref, pr_ref, here, share, experts):
    h1 = x.astype(F32) + nn(o, weight(second_ref, 1, share))
    h_ref[here, :] = h1
    inverse = lax.rsqrt(jnp.mean(h1 * h1, axis=-1, keepdims=True) + EPSILON)
    normed = (h1 * inverse * params_ref[1:2, :]).astype(BF16)
    a_ref[here, :] = normed
    router = jnp.concatenate([params_ref[8:16, :], jnp.zeros((120, D), F32)], axis=0).astype(BF16)
    logits = nt(normed, router)
    lane = lax.broadcasted_iota(jnp.int32, logits.shape, 1)
    logits = jnp.where(lane < experts, logits, MASKED)
    lifted = jnp.exp(logits - logits.max(axis=-1, keepdims=True))
    pr = lifted / lifted.sum(axis=-1, keepdims=True)
    named = (down_ref[here, :] >= 0) & (lane < experts)
    picked = jnp.where(named, pr, 0.0)
    pr_ref[here, :] = pr
    gate_ref[here, :] = picked / picked.sum(axis=-1, keepdims=True)


def attend_pair(n, q_ref, k_ref, v_ref, line_ref, table_ref, down_ref, across_ref, o_ref, lse_ref, width):
    columns = pl.ds(pl.multiple_of(n * 128, 128), 128)
    heads = 128 // width
    for h in range(heads):
        row = line_ref[n * heads + h]
        for gap in range(table_ref.shape[1]):
            ahead = row[:, gap * TILE : (gap + 1) * TILE]
            back = row[:, (gap - 1) * TILE : gap * TILE] if gap else jnp.zeros_like(ahead)
            grid = jnp.broadcast_to(jnp.concatenate([ahead, back], axis=1), (TILE, 2 * TILE))
            grid = pltpu.roll(grid, 0, 1, stride=1, stride_axis=0)
            table_ref[n * heads + h, gap] = grid[:, :TILE].astype(BF16)
    q_all, k_all, v_all = q_ref[:, columns], k_ref[:, columns], v_ref[:, columns]
    blocks = q_all.shape[0] // TILE
    turned = [v_all[:, h * width : (h + 1) * width].T for h in range(heads)]
    for i in range(blocks):
        here = slice(i * TILE, (i + 1) * TILE)
        outs = []
        for h in range(heads):
            lanes = slice(h * width, (h + 1) * width)
            q = q_all[here, lanes]
            pieces = []
            for j in range(i + 1):
                there = slice(j * TILE, (j + 1) * TILE)
                pieces.append(
                    masked_scores(
                        k_all[there, lanes], q, table_ref, n * heads + h, i, j, down_ref[there, 8:9],
                        across_ref[8:9, here]
                    )
                )
            top = pieces[0].max(axis=0, keepdims=True)
            for piece in pieces[1:]:
                top = jnp.maximum(top, piece.max(axis=0, keepdims=True))
            total = jnp.zeros_like(top)
            acc = jnp.zeros((width, TILE), F32)
            for j, piece in enumerate(pieces):
                lifted = jnp.exp(piece - top)
                total = total + lifted.sum(axis=0, keepdims=True)
                acc = acc + nn(turned[h][:, j * TILE : (j + 1) * TILE], lifted.astype(BF16))
            outs.append(acc / total)
            lse_ref[n, h : h + 1, here] = top + jnp.log(total)
        o_ref[here, columns] = jnp.concatenate(outs, axis=0).T.astype(BF16)


def attend_back_kernel(
    q_ref, k_ref, v_ref, do_ref, table_ref, down_ref, across_ref, lse_ref, a_ref, dwo_ref, dgain_m_ref, drouter_ref, buckets_ref,
    passed, terms,
    dq_ref, dk_ref, dv_ref, pack, sums_ref, pass_out,
    dist_ref, grads_ref, sum_ref, dk_sum, dv_sum, turned_a, p_send, p_recv, own, pair, inbox, send, recv, local, *, width, scale, group, share, experts
):
    step = pl.program_id(0)
    last = pl.num_programs(0) - 1
    place = lax.axis_index("expert")

    def emit(half, value):
        sums_ref[half] = value.astype(BF16)

    start, far, near, late, finish = reduce_copies(terms.at[2], own, pair, inbox, send, recv, local, emit)
    hop = along_axis(passed, pass_out, p_send.at[0], p_recv.at[0], partner(place, 3))

    @pl.when(step == 0)
    def _():
        meet(plane_devices() + [(lax.axis_index("dp"), partner(place, 3))])
        start()
        hop.start()
        far()
        turned_a[...] = a_ref[...].T
        near()

    @pl.when(step == 3)
    def _():
        late()

    blocks = q_ref.shape[0] // TILE
    heads = q_ref.shape[1] // width
    turned = [k_ref[:, h * width : (h + 1) * width].T for h in range(heads)]
    for h in range(heads):
        dist_ref[step * heads + h] = jnp.zeros(dist_ref.shape[1:], F32)
    for h in range(heads):
        lanes = slice(h * width, (h + 1) * width)
        for i in range(blocks):
            here = slice(i * TILE, (i + 1) * TILE)
            q = q_ref[here, lanes]
            do = do_ref[here, lanes]
            lse = lse_ref[0, h : h + 1, here]
            probs, dprobs = [], []
            delta = jnp.zeros((1, TILE), F32)
            for j in range(i + 1):
                there = slice(j * TILE, (j + 1) * TILE)
                scores = masked_scores(
                    k_ref[there, lanes], q, table_ref, h, i, j, down_ref[there, 8:9], across_ref[8:9, here]
                )
                p = jnp.exp(scores - lse)
                dp = nt(v_ref[there, lanes], do)
                delta = delta + (p * dp).sum(axis=0, keepdims=True)
                probs.append(p)
                dprobs.append(dp)
            turned_dq = jnp.zeros((width, TILE), F32)
            for j in range(i + 1):
                there = slice(j * TILE, (j + 1) * TILE)
                ds = probs[j] * (dprobs[j] - delta)
                low = ds.astype(BF16)
                dv = nn(probs[j].astype(BF16), do)
                dk = nn(low, q)
                if i == j:
                    dv_sum[there, lanes] = dv
                    dk_sum[there, lanes] = dk
                else:
                    dv_sum[there, lanes] += dv
                    dk_sum[there, lanes] += dk
                turned_dq = turned_dq + nn(turned[h][:, there], low)
                if j == 0:
                    sum_ref[i - j] = ds
                else:
                    sum_ref[i - j] += ds
            dq_ref[here, lanes] = (turned_dq * scale).T.astype(BF16)
        for gap in range(blocks):
            part = sum_ref[gap]
            part = jnp.concatenate([part, jnp.zeros_like(part)], axis=1)
            half = TILE // 2
            while half:
                part = part[:half] + pltpu.roll(part[half : 2 * half], 2 * TILE - half, 1)
                half //= 2
            dist_ref[step * heads + h, :, gap * TILE : (gap + 1) * TILE] += part[:, :TILE]
            if gap:
                dist_ref[step * heads + h, :, (gap - 1) * TILE : gap * TILE] += part[:, TILE:]
    dk_ref[...] = dk_sum[...].astype(BF16)
    dv_ref[...] = dv_sum[...].astype(BF16)

    grads = jnp.concatenate([dq_ref[...], dk_ref[...], dv_ref[...]], axis=1)
    sums = nn(turned_a[...], grads).astype(BF16)
    for index in range(3):
        grads_ref[step, :, index * 128 : (index + 1) * 128] = sums[:, index * 128 : (index + 1) * 128]

    @pl.when(step == last)
    def _():
        for index, (half, at) in enumerate(((0, 0), (0, share), (1, 0))):
            for n in range(grads_ref.shape[0]):
                part = grads_ref[n, :, index * 128 : (index + 1) * 128]
                pack[:, half, at : at + share, n * 128 : (n + 1) * 128] = part.reshape(-1, share, 128)
        pack[:, 1, share : 2 * share, :] = dwo_ref[...].astype(BF16).reshape(-1, share, D)
        seq = dist_ref.shape[2]
        hot = (lax.broadcasted_iota(jnp.int32, (128, seq), 0) == buckets_ref[...]).astype(F32).astype(BF16)
        left = jnp.concatenate([dist_ref[h] for h in range(dist_ref.shape[0])], axis=0)
        table = jnp.zeros((left.shape[0], 128), F32)
        for _ in range(3):
            low = left.astype(BF16)
            left = left - low.astype(F32)
            table = table + nt(low, hot)
        rows_out = [jnp.zeros((1, D), F32), dgain_m_ref[...], jnp.zeros((6, D), F32)]
        for e in range(experts):
            picked = jnp.zeros((1, D), F32)
            for k in range(experts):
                picked = picked + drouter_ref[k : k + 1, :] * jnp.where(partner(place, ORDER[k]) == e, 1.0, 0.0)
            rows_out.append(picked)
        rows_out.append(jnp.zeros((8 - experts, D), F32))
        rows_out.append(jnp.concatenate([table, jnp.zeros((table.shape[0], D - 128), F32)], axis=1))
        rows_out.append(jnp.zeros((16 - table.shape[0], D), F32))
        small = jnp.concatenate(rows_out, axis=0).astype(BF16)
        for slot in range(pack.shape[0]):
            pack[slot, 0, 2 * share :, :] = small
            pack[slot, 1, 2 * share :, :] = jnp.zeros_like(small)
        finish()
        hop.wait()


def experts_kernel(
    a_ref, g_ref, gate_ref, across_ref, first_a, second_a, piece_c0, piece_c1, w_in_ref, w_out_ref,
    eo_ref, da_ref, dw_out, sum_a, sum_c, piece_b, first_c, second_c, first_b, second_b,
    rows_a, turned_a, rows_d, eo_sum, da_sum, w_in_two, w_out_two, dw_two, total_a,
    w_sem, dw_sem, hop_send, hop_recv, save, free, own, pair, inbox, send_a, recv_a, local_a,
    send_c, recv_c, local_c, *gather, capacity, group, shards
):
    step = pl.program_id(0)
    last = pl.num_programs(0) - 1
    steps = shards // 2
    turn = step // steps
    slot = lax.rem(step, 2)
    place = lax.axis_index("expert")
    chunk = w_in_two.shape[3]

    def loads(at, which):
        c = lax.rem(at, steps)
        two = lax.rem(at, 2)
        if which != 2:
            first, second = {0: (first_a, second_a), 1: (first_c, second_c), 3: (first_b, second_b)}[which]
            both = pl.ds(2 * c, 2)
            return [
                pltpu.make_async_copy(first.at[both], w_in_two.at[two], w_sem.at[0, two]),
                pltpu.make_async_copy(second.at[both], w_out_two.at[two], w_sem.at[1, two]),
            ]
        copies = []
        for h in range(2):
            cols = pl.ds(pl.multiple_of((2 * c + h) * chunk, 128), chunk)
            copies.append(
                pltpu.make_async_copy(w_in_ref.at[0, :, cols], w_in_two.at[two, h], w_sem.at[3 * h, two])
            )
            for l in range(2):
                lanes = pl.ds(l * chunk, chunk)
                copies.append(
                    pltpu.make_async_copy(
                        w_out_ref.at[0, cols, lanes], w_out_two.at[two, h, lanes], w_sem.at[3 * h + 1 + l, two]
                    )
                )
        return copies

    def each_turn(at, action):
        for which in range(group):
            @pl.when(at // steps == which)
            def _(which=which):
                for copy in loads(at, which):
                    action(copy)

    def saved(at):
        two = lax.rem(at, 2)
        return pltpu.make_async_copy(
            dw_two.at[two], dw_out.at[at // steps, pl.ds(2 * lax.rem(at, steps), 2)], dw_sem.at[two]
        )

    gather_c = gather_copies(first_c, second_c, piece_c0, piece_c1, *gather[:3])
    gather_b = gather_copies(first_b, second_b, piece_b.at[0], piece_b.at[1], *gather[3:])
    relays = [
        along_axis(piece, piece_b.at[i], hop_send.at[2 * i], hop_recv.at[2 * i], partner(place, 1))
        for i, piece in enumerate((piece_c0, piece_c1))
    ]
    hop = along_axis(total_a, sum_a, hop_send.at[1], hop_recv.at[1], partner(place, 1))
    keep = pltpu.make_async_copy(own.at[3], sum_c, save.at[0])

    def emit_a(half, value):
        total_a[half] = value.astype(BF16)

    def emit_c(half, value):
        own[3, half] = value.astype(BF16)

    reduce_a = reduce_copies(dw_out.at[0], own, pair, inbox, send_a, recv_a, local_a, emit_a)
    reduce_c = reduce_copies(dw_out.at[1], own, pair, inbox, send_c, recv_c, local_c, emit_c)

    @pl.when(step == 0)
    def _():
        meet(plane_devices() + [(lax.axis_index("dp"), partner(place, 1))])
        gather_c[0]()
        for copy in relays:
            copy.start()
        each_turn(step, lambda copy: copy.start())

    def release():
        for device in plane_devices():
            pl.semaphore_signal(free, inc=1, device_id=device, device_id_type=MESH)

    def claim():
        pl.semaphore_wait(free, len(plane_devices()))

    schedule = {
        3: [gather_c[1]],
        4: [relays[0].wait, relays[1].wait, gather_b[0]],
        6: [reduce_a[0]],
        7: [gather_b[1], reduce_a[1]],
        8: [reduce_a[2]],
        11: [reduce_a[3]],
        13: [reduce_a[4], release, hop.start, claim, reduce_c[0], reduce_c[1], reduce_c[2]],
    }
    for when, actions in schedule.items():
        @pl.when(step == when)
        def _(actions=actions):
            for action in actions:
                action()

    @pl.when(lax.rem(step, steps) == 0)
    def _():
        tokens = a_ref.shape[0]
        places = lax.broadcasted_iota(jnp.int32, (capacity, tokens), 0)
        pick = (across_ref[pl.ds(turn, 1), :] == places).astype(BF16)
        rows = nn(pick, a_ref[...]).astype(BF16)
        rows_a[...] = rows
        turned_a[...] = rows.T
        lane = lax.broadcasted_iota(jnp.int32, gate_ref.shape, 1)
        gate = jnp.sum(jnp.where(lane == turn, gate_ref[...], 0.0), axis=-1, keepdims=True)
        rows_d[...] = nn(pick, (gate * g_ref[...].astype(F32)).astype(BF16)).astype(BF16)
        eo_sum[...] = jnp.zeros_like(eo_sum)
        da_sum[...] = jnp.zeros_like(da_sum)

    each_turn(step, lambda copy: copy.wait())
    ahead = step + 1

    @pl.when((step < last) & (ahead != steps) & (ahead != 3 * steps))
    def _():
        each_turn(ahead, lambda copy: copy.start())

    @pl.when(step > 1)
    def _():
        saved(step - 2).wait()

    d = rows_d[...]
    w_in = jnp.concatenate([w_in_two[slot, h] for h in range(2)], axis=1)
    w_out = jnp.concatenate(
        [
            jnp.concatenate([w_out_two[slot, h, :chunk], w_out_two[slot, h, chunk:]], axis=1)
            for h in range(2)
        ],
        axis=0,
    )
    u = nn(rows_a[...], w_in)
    square = u * u
    t = jnp.tanh(GELU_A * u * (1.0 + GELU_B * square))
    half = 0.5 * (1.0 + t)
    z = (u * half).astype(BF16)
    eo_sum[...] += nn(z, w_out)
    dw_last = tn(z, d).astype(BF16)
    slope = half + (0.5 * GELU_A) * u * (1.0 - t * t) * (1.0 + 3.0 * GELU_B * square)
    du = (nt(d, w_out) * slope).astype(BF16)
    da_sum[...] += nt(du, w_in)
    dw_first = nn(turned_a[...], du).astype(BF16)
    for h in range(2):
        here = slice(h * chunk, (h + 1) * chunk)
        dw_two[slot, h, 0] = dw_first[:, here]
        dw_two[slot, h, 1, :chunk] = dw_last[here, :chunk]
        dw_two[slot, h, 1, chunk:] = dw_last[here, chunk:]
    saved(step).start()

    @pl.when(lax.rem(ahead, steps) == 0)
    def _():
        eo_ref[0] = eo_sum[...].astype(BF16)
        da_ref[0] = da_sum[...].astype(BF16)

    @pl.when(ahead == steps)
    def _():
        gather_c[2]()
        gather_c[3]()
        each_turn(ahead, lambda copy: copy.start())

    @pl.when(ahead == 3 * steps)
    def _():
        gather_b[2]()
        gather_b[3]()
        each_turn(ahead, lambda copy: copy.start())

    @pl.when(step == last)
    def _():
        saved(step - 1).wait()
        saved(step).wait()
        reduce_c[3]()
        reduce_c[4]()
        keep.start()
        hop.wait()
        keep.wait()


def own_last(step, group):
    return lax.rem(lax.axis_index("expert") + 1 + step, group)


def send_rows(p, value, stage, target, sends, recvs, keep):
    place = lax.axis_index("expert")
    stage[p] = value

    @pl.when(p == place)
    def _():
        pltpu.make_async_copy(stage.at[place], target.at[place], keep.at[0]).start()

    @pl.when(p != place)
    def _():
        along_axis(stage.at[p], target.at[place], sends.at[p], recvs.at[place], p).start()


def end_rows(stage, target, sends, recvs, keep, group):
    place = lax.axis_index("expert")
    for k in range(1, group):
        other = lax.rem(place + k, group)
        along_axis(stage.at[other], target.at[other], sends.at[other], recvs.at[other], other).wait_recv()
    for k in range(1, group):
        other = lax.rem(place + k, group)
        along_axis(stage.at[other], target.at[place], sends.at[other], recvs.at[place], other).wait_send()
    pltpu.make_async_copy(stage.at[place], target.at[place], keep.at[0]).wait()


def combine_kernel(
    h_ref, a_ref, g_ref, o_ref, gate_ref, pr_ref, pos_ref, eo_ref, back_ref, second_ref, params_ref, terms, passed,
    out_all, dh_ref, do_ref, dw_ref, dgain_ref, drouter_ref, sums_ref,
    stage, landed, p_send, p_recv, sends, recvs, keep, own, pair, inbox, send, recv, local,
    *, share, experts, capacity, group
):
    step = pl.program_id(0)
    last = pl.num_programs(0) - 1
    place = lax.axis_index("expert")

    def emit(half, value):
        sums_ref[half] = (value + landed[half].astype(F32)).astype(BF16)

    start, far, near, late, finish = reduce_copies(terms.at[3], own, pair, inbox, send, recv, local, emit)
    hop = along_axis(passed, landed, p_send.at[0], p_recv.at[0], partner(place, 1))

    @pl.when(step == 0)
    def _():
        meet(plane_devices() + place_devices(group))
        start()
        hop.start()
        far()

    @pl.when(step == 1)
    def _():
        near()

    @pl.when(step == 3)
    def _():
        late()

    @pl.when(step == 0)
    def _():
        dw_ref[...] = jnp.zeros_like(dw_ref)
        dgain_ref[...] = jnp.zeros_like(dgain_ref)
        drouter_ref[...] = jnp.zeros_like(drouter_ref)

    tile = h_ref.shape[0]
    h1 = h_ref[...]
    g = g_ref[...].astype(F32)
    gates = gate_ref[...]
    pr = pr_ref[...]
    lane = lax.broadcasted_iota(jnp.int32, pr.shape, 1)
    slot = lax.broadcasted_iota(jnp.int32, (tile, capacity), 1)
    result = h1
    dgate = jnp.zeros_like(pr)
    da = jnp.zeros_like(h1)
    for k in range(experts):
        spot = (pos_ref[:, k : k + 1] == slot).astype(BF16)
        got = nn(spot, eo_ref[k])
        result = result + gates[:, k : k + 1] * got
        dgate = jnp.where(lane == k, jnp.sum(g * got, axis=-1, keepdims=True), dgate)
        da = da + nn(spot, back_ref[k])
    send_rows(step, result.astype(BF16), stage, out_all, sends, recvs, keep)
    named = (pos_ref[...] >= 0) & (lane < experts)
    denom = jnp.sum(jnp.where(named, pr, 0.0), axis=-1, keepdims=True)
    weighted = jnp.sum(dgate * gates, axis=-1, keepdims=True)
    dpr = jnp.where(named, (dgate - weighted) / denom, 0.0)
    dlog = pr * (dpr - jnp.sum(pr * dpr, axis=-1, keepdims=True))
    high = dlog.astype(BF16)
    lost = (dlog - high.astype(F32)).astype(BF16)
    a = a_ref[...]
    drouter_ref[...] += (tn(high, a) + tn(lost, a))[: drouter_ref.shape[0]]
    for k in range(experts):
        da = da + dlog[:, k : k + 1] * params_ref[8 + k : 9 + k, :]
    inverse = lax.rsqrt(jnp.mean(h1 * h1, axis=-1, keepdims=True) + EPSILON)
    n2 = h1 * inverse
    dgain_ref[...] += jnp.sum(da * n2, axis=0, keepdims=True)
    dn = da * params_ref[1:2, :]
    dh = g + inverse * (dn - n2 * jnp.mean(dn * n2, axis=-1, keepdims=True))
    dh_ref[...] = dh
    dy = dh.astype(BF16)
    do_ref[...] = nt(dy, weight(second_ref, 1, share)).astype(BF16)
    dw_ref[...] += tn(o_ref[...], dy)

    @pl.when(step == last)
    def _():
        hop.wait()
        finish()
        end_rows(stage, out_all, sends, recvs, keep, group)


def close_kernel(
    x_ref, dq_ref, dk_ref, dv_ref, dh_ref, first_ref, second_ref, params_ref, pack, sum0, sum1, sum2,
    din_out, gather_first, gather_second, dense_ref,
    stage, total, own, pair, inbox, r_send, r_recv, r_local, sends, recvs, keep,
    z_in, z_total, z_final, z_send, z_recv, g_send, g_recv, g_local, *, share, group, experts
):
    step = pl.program_id(0)
    last = pl.num_programs(0) - 1
    place = lax.axis_index("expert")
    start0, start1, start2, finish = gather_copies(
        gather_first, gather_second, total.at[0], total.at[1], g_send, g_recv, g_local
    )
    quarter = pack.shape[2] // 2

    def emit(half, value):
        low = value.astype(BF16)
        z_total[2 * half] = low[:quarter]
        z_total[2 * half + 1] = low[quarter:]

    start, far, near, late, end_reduce = reduce_copies(pack, own, pair, inbox, r_send, r_recv, r_local, emit)

    @pl.when(step == 0)
    def _():
        meet(plane_devices() + place_devices(group))
        start()
        far()
        near()
        for half in range(2):
            value = sum0[half].astype(F32) + sum1[half].astype(F32)
            total[half] = (value + sum2[half].astype(F32)).astype(BF16)

    @pl.when(step == 1)
    def _():
        late()
        start0()

    da = jnp.zeros(dh_ref.shape, F32)
    places = ((first_ref, 0), (first_ref, 1), (second_ref, 0))
    for index, grad_ref in enumerate((dq_ref, dk_ref, dv_ref)):
        slots_ref, at = places[index]
        da = da + nt(grad_ref[...], weight(slots_ref, at, share))
    x = x_ref[...].astype(F32)
    inverse = lax.rsqrt(jnp.mean(x * x, axis=-1, keepdims=True) + EPSILON)
    n1 = x * inverse
    dn = da * params_ref[0:1, :]
    din = dh_ref[...] + inverse * (dn - n1 * jnp.mean(dn * n1, axis=-1, keepdims=True))
    send_rows(own_last(step, group), din.astype(BF16), stage, din_out, sends, recvs, keep)

    @pl.when(step == last)
    def _():
        end_reduce()
        spread = [
            along_axis(z_total.at[lax.rem(place + k, group)], z_in.at[k - 1], z_send.at[k], z_recv.at[k],
                       lax.rem(place + k, group))
            for k in range(1, group)
        ]
        for copy in spread:
            copy.start()
        for copy in spread:
            copy.wait_recv()
        value = z_total[place].astype(F32)
        for k in range(group - 1):
            value = value + z_in[k].astype(F32)
        z_final[place] = value.astype(BF16)
        share_out = [
            along_axis(z_final.at[place], z_final.at[place], z_send.at[group + k], z_recv.at[group + k],
                       lax.rem(place + k, group))
            for k in range(1, group)
        ]
        for copy in share_out:
            copy.start()
        start1()
        start2()
        for copy in share_out:
            copy.wait_recv()
        for copy in spread + share_out:
            copy.wait_send()
        dense_ref[...] = z_final[...]
        end_rows(stage, din_out, sends, recvs, keep, group)
        finish()


def unpack_kernel(
    first_ref, second_ref, din_ref, dense_ref, wq_ref, wk_ref, wv_ref, gain_ref,
    in_ref, out_ref, grad_ref, dq_ref, dk_ref, dv_ref, do_ref, gain_out, small_ref, *, share
):
    chunk = first_ref.shape[2]
    in_ref[0] = first_ref[0].astype(F32)
    out_ref[0, :, :chunk] = second_ref[0, :chunk].astype(F32)
    out_ref[0, :, chunk:] = second_ref[0, chunk:].astype(F32)
    grad_ref[...] = din_ref[...].astype(F32)

    @pl.when(pl.program_id(0) == 0)
    def _():
        grads = []
        for grad, half, at in ((dq_ref, 0, 0), (dk_ref, 0, share), (dv_ref, 1, 0), (do_ref, 1, share)):
            value = dense_ref[half, at : at + share, :].astype(F32)
            grad[...] = value
            grads.append(value)
        moved = grads[0] * wq_ref[...].astype(F32) + grads[1] * wk_ref[...].astype(F32)
        moved = moved + grads[2] * wv_ref[...].astype(F32)
        gain_out[...] = jnp.sum(moved, axis=-1, keepdims=True) / gain_ref[...].astype(F32)
        small_ref[...] = dense_ref[0, 2 * share :, :].astype(F32)


def on_device_whole(
    layer_in, out_grad, routes, segments, buckets, gain_attn, w_query, w_key, w_value, w_output,
    gain_moe, router, rel_bias, w_expert_in, w_expert_out,
):
    group = lax.axis_size("expert")
    shards = lax.axis_size("dp")
    shard = lax.axis_index("dp")
    experts = router.shape[1]
    seq = segments.shape[1]
    heads = rel_bias.shape[1]
    width = D // heads
    scale = 1.0 / math.sqrt(width)
    share = D // shards
    ff = w_expert_in.shape[2]
    chunk = ff // shards
    blocks = seq // TILE
    part = seq // group
    capacity = 3 * seq // group
    pairs = 128 // width
    tokens = (seq, D)
    slots = (capacity, D)
    piece = (2, D, chunk)
    buffer = sds((shards, D, chunk), BF16)
    dma = pltpu.SemaphoreType.DMA
    vmem = pl.BlockSpec(memory_space=pltpu.VMEM)

    wide = lambda v, count: jnp.pad(v, ((0, count - v.shape[0]), (0, D - v.shape[1])))
    small = jnp.concatenate([
        wide(jnp.stack([gain_attn, gain_moe]), 8), wide(router.T, 8), wide(rel_bias.T, 16)])
    routes_in = jnp.pad(routes.transpose(0, 2, 1), ((0, 0), (0, 6), (0, 0)))
    bucket_row = buckets.reshape(1, seq)
    second_rows = 2 * share + 32
    tok16, tok32, wide32 = sds(tokens, BF16), sds(tokens, F32), sds((seq, 128), F32)
    block = sds((group, part, D), BF16)
    table_shape = (heads, blocks, TILE, TILE)
    v16, v32 = pltpu.VMEM(tokens, BF16), pltpu.VMEM(tokens, F32)
    (x, g, far_first, far_second, first, second, normed, q, k, v, o, table, h1, normed_m, gates, pr, near_first,
     near_second, _, params, across, down, lse) = call(
        functools.partial(
            front_kernel, group=group, share=share, heads=heads, experts=experts, scale=scale, width=width),
        "front", (1,),
        [ANY] * 9 + [vmem] * 3,
        [ANY] * 19 + [vmem] * 4,
        [block, block, sds((D, chunk), BF16), sds((D, chunk), BF16), sds((shards, 2 * share, D), BF16),
         sds((shards, second_rows, D), BF16)] + [tok16] * 5
        + [sds(table_shape, BF16), tok32, tok16, wide32, wide32, buffer, buffer, sds(piece, BF16),
           sds((32, D), F32), sds((16, seq), jnp.int32), sds((seq, 128), jnp.int32),
           sds((heads // pairs, pairs, seq), F32)],
        [pltpu.VMEM((group, part, D), BF16), pltpu.VMEM((group, 8, part), jnp.int32),
         pltpu.VMEM((shards, 2 * share, D), BF16), pltpu.VMEM((shards, second_rows, D), BF16),
         pltpu.VMEM((2 * share, D), BF16), pltpu.VMEM((second_rows, D), BF16)] + [v16] * 5
        + [pltpu.VMEM(table_shape, BF16), v32, v16, pltpu.VMEM((seq, 128), F32), pltpu.VMEM((seq, 128), F32),
           pltpu.VMEM((heads, 1, seq), F32)]
        + [dma((group,))] * 6 + [dma((6,))] * 2 + [dma((3 + heads // pairs,)), dma((4,)), dma((12,))]
        + gather_sems() * 2, collective=1, flops=6 * seq * D * D,
    )(layer_in, out_grad, routes_in, w_expert_in, w_expert_out, w_query, w_key, w_value, w_output, small, bucket_row,
      segments)
    x = x.reshape(tokens)
    g = g.reshape(tokens)
    buffers = [near_first, near_second]
    cols = pl.BlockSpec((seq, 128), lambda i: (0, i))
    table_spec = pl.BlockSpec((pairs, blocks, TILE, TILE), lambda i: (i, 0, 0, 0))
    lse_spec = pl.BlockSpec((1, pairs, seq), lambda i: (i, 0, 0))

    turned_rows = lambda width: pl.BlockSpec((TILE, width), lambda i: (own_last(i, group), 0))
    once = lambda shape: pl.BlockSpec(shape, lambda *_: (0,) * len(shape), pipeline_mode=pl.Buffered(1))
    turned = pl.BlockSpec((1, *slots), lambda i: (i // (shards // 2), 0, 0))
    eo, da, dw, sum1, sum3, _, _, _, _, _ = call(
        functools.partial(experts_kernel, capacity=capacity, group=group, shards=shards), "experts",
        (experts * shards // 2,),
        [once(tokens), once(tokens), once((seq, 128)), once((16, seq))] + [ANY] * 6,
        [turned, turned] + [ANY] * 8,
        [sds((experts, *slots), BF16)] * 2 + [sds((experts, shards, *piece), BF16)] + [sds(piece, BF16)] * 3
        + [buffer] * 4,
        [pltpu.VMEM(slots, BF16), pltpu.VMEM((D, capacity), BF16), pltpu.VMEM(slots, BF16),
         pltpu.VMEM(slots, F32), pltpu.VMEM(slots, F32), pltpu.VMEM((2, 2, D, chunk), BF16),
         pltpu.VMEM((2, 2, D, chunk), BF16), pltpu.VMEM((2, 2, *piece), BF16), pltpu.VMEM(piece, BF16),
         dma((6, 2)), dma((2,)), dma((3,)), dma((3,)), dma((1,)), pltpu.SemaphoreType.REGULAR]
        + reduce_scratch(piece) + reduce_scratch(piece)[3:] + gather_sems() * 2,
        flops=48 * capacity * D * ff, nbytes=96 * 2**20, collective=3,
    )(normed_m, g, gates, across, *buffers, far_first, far_second, w_expert_in, w_expert_out)
    layer_out, dh, do, grad_output, grad_gain_m, grad_router, sum2 = call(
        functools.partial(combine_kernel, share=share, experts=experts, capacity=capacity, group=group), "combine",
        (blocks,),
        [rows(D)] * 4 + [rows(128)] * 3 + [once((experts, *slots))] * 2 + [once(second.shape), whole((32, D)), ANY, ANY],
        [ANY, rows(D), rows(D), whole((D, D)), whole((1, D)), whole((8, D)), whole(piece)],
        [sds((group, part, D), BF16), sds(tokens, F32), sds(tokens, BF16), sds((D, D), F32), sds((1, D), F32),
         sds((8, D), F32), sds(piece, BF16)],
        [pltpu.VMEM((group, part, D), BF16), pltpu.VMEM(piece, BF16), dma((1,)), dma((1,)), dma((group,)),
         dma((group,)), dma((1,))] + reduce_scratch(piece),
        flops=24 * seq * D * D, nbytes=32 * 2**20, collective=7,
    )(h1, normed_m, g, o, gates, pr, down, eo, da, second, params, dw, sum3)
    dense_slot = (2, 2 * share + 32, D)
    dq, dk, dv, pack, sum0, sum2 = call(
        functools.partial(
            attend_back_kernel, width=width, scale=scale, group=group, share=share, experts=experts),
        "attend_back", (heads // pairs,),
        [cols, cols, cols, cols, table_spec, whole((seq, 128)), whole((16, seq)), lse_spec, once(tokens), once((D, D)),
         whole((1, D)), whole((8, D)), whole((1, seq)), ANY, ANY],
        [cols, cols, cols, once((shards, *dense_slot)), whole(piece), ANY],
        [sds(tokens, BF16)] * 3 + [sds((shards, *dense_slot), BF16), sds(piece, BF16), sds(piece, BF16)],
        [pltpu.VMEM((heads, 1, seq), F32), pltpu.VMEM((heads // pairs, D, 3 * 128), BF16),
         pltpu.VMEM((blocks, TILE, TILE), F32), pltpu.VMEM((seq, 128), F32), pltpu.VMEM((seq, 128), F32),
         pltpu.VMEM((D, seq), BF16)]
        + [dma((1,))] * 2 + reduce_scratch(piece),
        flops=20 * seq * seq * D, nbytes=24 * 2**20, collective=8,
    )(q, k, v, do, table, down, across, lse, normed, grad_output, grad_gain_m, grad_router, bucket_row, sum2, dw)
    quarter = (dense_slot[1] // 2, D)
    grad_in, *gathered, dense = call(
        functools.partial(close_kernel, share=share, group=group, experts=experts), "close", (blocks,),
        [turned_rows(D)] * 5 + [once(first.shape), once(second.shape), whole((32, D)), ANY] + [once(piece)] * 3,
        [ANY, ANY, ANY, whole((group, *quarter))],
        [sds((group, part, D), BF16), buffer, buffer, sds((group, *quarter), BF16)],
        [pltpu.VMEM((group, part, D), BF16), pltpu.VMEM(piece, BF16)]
        + reduce_scratch(dense_slot)
        + [dma((group,)), dma((group,)), dma((1,)), pltpu.VMEM((group - 1, *quarter), BF16),
           pltpu.VMEM((group, *quarter), BF16), pltpu.VMEM((group, *quarter), BF16), dma((2 * group,)),
           dma((2 * group,))] + gather_sems(),
        flops=12 * seq * D * D, nbytes=24 * 2**20, collective=9,
    )(x, dq, dk, dv, dh, first, second, params, pack, sum0, sum1, sum2)
    spec = pl.BlockSpec((1, D, chunk), lambda i: (i, 0, 0))
    line_rows = pl.BlockSpec((seq // shards, D), lambda i: (i, 0))
    expert_in, expert_out, grad_in, *dense_grads, grad_gain, smalls = call(
        functools.partial(unpack_kernel, share=share), "unpack", (shards,),
        [spec, spec, line_rows, whole(dense_slot)] + [whole((share, D))] * 3 + [whole((share, 1))],
        [pl.BlockSpec((1, D, chunk), lambda i: (0, 0, i)), pl.BlockSpec((1, chunk, D), lambda i: (0, i, 0)), line_rows]
        + [whole((share, D))] * 4 + [whole((share, 1)), whole((32, D))],
        [sds(w_expert_in.shape, F32), sds(w_expert_out.shape, F32), sds(tokens, F32)]
        + [sds((share, D), F32)] * 4 + [sds((share, 1), F32), sds((32, D), F32)],
        nbytes=34 * 2**20,
    )(*gathered, grad_in.reshape(tokens), dense.reshape(dense_slot), w_query, w_key, w_value,
      gain_attn.reshape(share, 1))
    line = lax.dynamic_slice_in_dim(smalls[:16], shard * share, share, axis=1)
    grad_table = lax.dynamic_slice_in_dim(smalls[16 : 16 + heads], shard * rel_bias.shape[0], rel_bias.shape[0], axis=1)
    return (
        layer_out,
        grad_in.reshape(group, part, D),
        grad_gain.reshape(share),
        *dense_grads,
        line[1],
        line[8 : 8 + experts].T,
        grad_table.T,
        expert_in,
        expert_out,
    )


def solution(mesh):
    in_specs = (
        P(None, ("dp", "expert"), None),
        P(None, ("dp", "expert"), None),
        P(None, ("dp", "expert"), None),
        P(None, "dp"),
        P(),
        P("dp"),
        P("dp", None),
        P("dp", None),
        P("dp", None),
        P("dp", None),
        P("dp"),
        P("dp", None),
        P("dp", None),
        P("expert", None, None),
        P("expert", None, None),
    )
    out_specs = (
        P(None, ("dp", "expert"), None),
        P(None, ("dp", "expert"), None),
        P("dp"),
        P("dp", None),
        P("dp", None),
        P("dp", None),
        P("dp", None),
        P("dp"),
        P("dp", None),
        P("dp", None),
        P("expert", None, None),
        P("expert", None, None),
    )
    body = on_device_whole if mesh.shape["expert"] == MICRO else on_device
    return jax.shard_map(
        body, mesh=mesh, in_specs=in_specs, out_specs=out_specs, check_vma=False
    )
```
